32 devices in a mesh: section: 2 (over x), dp: 4 (over y, core), tensor: 4 (over z).
Axes of the slice: x: 2, y: 2, z: 4, core: 2. Of those that a mesh axis runs over, the one named last changes fastest.
Arguments:
- block_input: bfloat16 [3, 4, 1376, 1024], P(None, 'dp', 'tensor'), may hold values from -6 to 6
- out_cotangent: bfloat16 [3, 4, 1376, 1024], P(None, 'dp', 'tensor'), may hold values from -6 to 6
- lengths: int32 [4], replicated, may hold values from 1 to 344, 1370 in all
- qkv_weight: bfloat16 [2, 1024, 3, 1024], P('section', 'dp', None, 'tensor'), may hold values from -0.1875 to 0.1875
- qv_bias: bfloat16 [2, 2, 1024], P('section', None, 'tensor'), may hold values from -0.59765625 to 0.59765625
- proj_weight: bfloat16 [2, 1024, 1024], P('section', 'tensor', 'dp'), may hold values from -1.5 to 1.5
- fc1_weight: bfloat16 [2, 1024, 4096], P('section', 'dp', 'tensor'), may hold values from -0.1875 to 0.1875
- fc1_bias: bfloat16 [2, 4096], P('section', 'tensor'), may hold values from -1.796875 to 1.796875
- fc2_weight: bfloat16 [2, 4096, 1024], P('section', 'tensor', 'dp'), may hold values from -0.09375 to 0.09375
- gains: bfloat16 [2, 4, 1024], P('section', None, ('dp', 'tensor')), may hold values from 0.5 to 1.5
- biases: bfloat16 [2, 4, 1024], P('section', None, ('dp', 'tensor')), may hold values from -1.796875 to 1.796875
Outputs:
- section_out: bfloat16 [2, 3, 4, 1376, 1024], P('section', None, 'dp', 'tensor')
- input_grad: bfloat16 [2, 3, 4, 1376, 1024], P('section', None, 'dp', 'tensor')
- qkv_grad: float32 [2, 1024, 3, 1024], P('section', 'dp', None, 'tensor')
- qv_bias_grad: float32 [2, 2, 1024], P('section', None, 'tensor')
- proj_grad: float32 [2, 1024, 1024], P('section', 'tensor', 'dp')
- fc1_grad: float32 [2, 1024, 4096], P('section', 'dp', 'tensor')
- fc1_bias_grad: float32 [2, 4096], P('section', 'tensor')
- fc2_grad: float32 [2, 4096, 1024], P('section', 'tensor', 'dp')
- gain_grad: float32 [2, 4, 1024], P('section', None, ('dp', 'tensor'))
- bias_grad: float32 [2, 4, 1024], P('section', None, ('dp', 'tensor'))
The draws below stay inside these ranges and needn't reach their ends.
Inputs may be any that keep to these rules, and one draw needn't show every extreme that they name: lengths[r] is the number of live slots, always the first ones, of token shard r of 344 slots; the entries sum to 1370 and one of them equals 344.
All inputs are finite; a program needn't handle non-finite values.
Results may differ from the reference program's by a relative error of at most 0.018.
Values may be sent and summed in bfloat16 or wider, within the bound.
A program may use at most 384 MiB of HBM per device.

```python
import math
import jax
import jax.numpy as jnp
import numpy as np
from jax import lax

D = 1024
HEADS = 16
HD = 64
FF = 4096
SEQ = 1370
MB = 3
SECTIONS = 2
SHARDS = 4
CAP = 344
TOKPAD = 1376
IMAGES = 4


def block_scale(own_key, shape, pieces, low, high):
    level, own = 1.0, jax.random.fold_in(own_key, 6)
    for axis_at, blocks in pieces:
        steps = jnp.exp(jax.random.uniform(jax.random.fold_in(own, axis_at), (blocks,), jnp.float32, low / len(pieces), high / len(pieces)))
        level = level * jnp.repeat(steps, shape[axis_at] // blocks).reshape([-1 if axis == axis_at else 1 for axis in range(len(shape))])
    return level


def length_profile(amount, total, most, lean):
    portions = [(1 << 20) // math.isqrt(grade ** lean) + 1 for grade in range(2, amount + 1)]
    surplus, given = total - most - (amount - 1), [1] * (amount - 1)
    while surplus > 0:
        movable = [i for i in range(amount - 1) if given[i] < most]
        mass, left = sum([portions[i] for i in movable]), surplus
        for i in movable:
            more = min(most - given[i], max(1, left * portions[i] // mass), surplus)
            given[i] = given[i] + more
            surplus = surplus - more
    return np.array([most] + given)


def uneven_parts(own_key, amount, total, limit, skew):
    if amount == 2:
        one = jax.random.randint(own_key, (), max(1, total - limit), min(limit, total - 1) + 1)
        return jnp.stack([one, total - one])
    sizes = jnp.asarray(length_profile(amount, total, limit, skew), jnp.int32)
    couples = (amount - 1) // 2
    giver, receiver = sizes[1:1 + 2 * couples:2], sizes[2:2 + 2 * couples:2]
    margin = jnp.minimum(giver - 1, limit - receiver)
    moved = jax.random.randint(jax.random.fold_in(own_key, 1), (couples,), 0, 1 << 20) % (margin + 1)
    sizes = sizes.at[1:1 + 2 * couples:2].set(giver - moved).at[2:2 + 2 * couples:2].set(receiver + moved)
    return sizes[jax.random.permutation(jax.random.fold_in(own_key, 2), amount)]


def scatter_about(key, shape, scale, limit, split=(), kind=jnp.bfloat16):
    gain = block_scale(key, shape, split, -0.22, 0.18) if split else 1.0
    entries = jax.random.normal(key, shape, jnp.float32) * scale * gain
    return jnp.minimum(jnp.maximum(entries, -limit), limit).astype(kind)


def setup_inputs(seed: int = 0) -> dict:
    streams_of = jax.random.split(jax.random.key(seed), 12)
    block_input = scatter_about(streams_of[0], (MB, IMAGES, TOKPAD, D), 1.0, 6.0, ((1, 4), (2, 4)))
    out_cotangent = scatter_about(streams_of[1], (MB, IMAGES, TOKPAD, D), 1.0, 6.0, ((1, 4), (2, 4)))
    lengths = uneven_parts(streams_of[2], SHARDS, SEQ, CAP, 0).astype(jnp.int32)
    qkv_weight = scatter_about(streams_of[3], (SECTIONS, D, 3, D), D ** -0.5, 0.1875, ((0, 2), (1, 4), (3, 4)))
    qv_bias = scatter_about(streams_of[4], (SECTIONS, 2, D), 0.1, 0.59765625, ((0, 2), (2, 4)))
    proj_weight = scatter_about(streams_of[5], (SECTIONS, D, D), (max(D // 64, 1)) ** -0.5, 1.5, ((0, 2), (1, 4), (2, 4)))
    fc1_weight = scatter_about(streams_of[6], (SECTIONS, D, FF), D ** -0.5, 0.1875, ((0, 2), (1, 4), (2, 4)))
    fc1_bias = scatter_about(streams_of[7], (SECTIONS, FF), 0.3, 1.796875, ((0, 2), (1, 4)))
    fc2_weight = scatter_about(streams_of[8], (SECTIONS, FF, D), FF ** -0.5, 0.09375, ((0, 2), (1, 4), (2, 4)))
    gains = jnp.clip(0.5 + 1.0 * jax.random.uniform(streams_of[9], (SECTIONS, 4, D), jnp.float32) ** block_scale(streams_of[9], (SECTIONS, 4, D), ((0, 2), (2, 16)), -0.2, 0.2), 0.5, 1.5).astype(jnp.bfloat16)
    biases = scatter_about(streams_of[10], (SECTIONS, 4, D), 0.3, 1.796875, ((0, 2), (2, 16)))
    return {"block_input": block_input, "out_cotangent": out_cotangent, "lengths": lengths, "qkv_weight": qkv_weight, "qv_bias": qv_bias, "proj_weight": proj_weight, "fc1_weight": fc1_weight, "fc1_bias": fc1_bias, "fc2_weight": fc2_weight, "gains": gains, "biases": biases}


HIGH = lax.Precision.HIGHEST
EPS = 1e-06

@jax.custom_vjp
def low(v):
    return lax.optimization_barrier(v.astype(jnp.bfloat16)).astype(jnp.float32)

@jax.custom_vjp
def low_back(v):
    return v

def low_keep(v):
    return (low(v), None)

def low_pass(kept, grad):
    return (grad,)

def back_keep(v):
    return (v, None)

def back_low(kept, grad):
    return (low(grad),)
low.defvjp(low_keep, low_pass)
low_back.defvjp(back_keep, back_low)

def layer_norm(tok_rows, gain_row, shift_row):
    row_mean = lax.optimization_barrier(jnp.mean(tok_rows, axis=-1, keepdims=True))
    centred = tok_rows - row_mean
    spread = lax.optimization_barrier(jnp.mean(centred * centred, axis=-1, keepdims=True))
    return centred * lax.rsqrt(spread + EPS) * gain_row + shift_row

def attend(queries, key_rows, values, key_valid):
    scores = jnp.einsum('qhd,khd->hqk', queries, key_rows, precision=HIGH) * HD ** (-0.5)
    scores = low_back(scores)
    scores = jnp.where(key_valid[None, None, :], scores, -1000000000.0)
    attn_probs = low(jax.nn.softmax(scores, axis=-1))
    return jnp.einsum('hqk,khd->qhd', attn_probs, values, precision=HIGH)

def block(tok_rows, w_qkv, qv_bias, w_proj, w_up, up_bias, w_down, gain_rows, bias_rows, key_valid):
    tok_rows = low_back(tok_rows)
    image_count = tok_rows.shape[0]
    h_one = low(layer_norm(tok_rows, gain_rows[0], bias_rows[0]))
    qkv_all = jnp.einsum('bld,dtf->bltf', h_one, w_qkv, precision=HIGH)
    queries = low_back(low(qkv_all[:, :, 0] + qv_bias[0]))
    key_rows = low_back(low(qkv_all[:, :, 1]))
    values = low_back(low(qkv_all[:, :, 2] + qv_bias[1]))
    split_shape = (image_count, TOKPAD, HEADS, HD)
    head_fn = jax.checkpoint(lambda q_part, k_part, v_part: attend(q_part, k_part, v_part, key_valid))
    context = lax.map(lambda triple: head_fn(*triple), (queries.reshape(split_shape), key_rows.reshape(split_shape), values.reshape(split_shape)))
    context = low_back(low(context.reshape(image_count, TOKPAD, D)))
    attn_sum = low_back(jnp.einsum('blf,fd->bld', context, w_proj, precision=HIGH))
    mid_rows = tok_rows + gain_rows[1] * (attn_sum + bias_rows[1])
    h_two = low(layer_norm(mid_rows, gain_rows[2], bias_rows[2]))
    pre_act = low_back(jnp.einsum('bld,df->blf', h_two, w_up, precision=HIGH) + up_bias)
    act_low = low(jax.nn.gelu(pre_act, approximate=False))
    mlp_sum = low_back(jnp.einsum('blf,fd->bld', act_low, w_down, precision=HIGH))
    row_valid = key_valid.astype(jnp.float32)
    return row_valid[None, :, None] * (mid_rows + gain_rows[3] * (mlp_sum + bias_rows[3]))

def reference(block_input, out_cotangent, lengths, qkv_weight, qv_bias, proj_weight, fc1_weight, fc1_bias, fc2_weight, gains, biases):
    slot_ids = jnp.arange(CAP, dtype=jnp.int32)
    key_valid = (slot_ids[None, :] < lengths[:, None]).reshape(-1)
    first_in = block_input.reshape(MB * IMAGES, TOKPAD, D).astype(jnp.float32)
    cotangent = out_cotangent.reshape(MB * IMAGES, TOKPAD, D).astype(jnp.float32)

    def section_params(section_idx):
        return tuple((param[section_idx].astype(jnp.float32) for param in (qkv_weight, qv_bias, proj_weight, fc1_weight, fc1_bias, fc2_weight, gains, biases)))

    def run_block(tok_rows, *params):
        return block(tok_rows, *params, key_valid)
    out_one, pull_one = jax.vjp(run_block, first_in, *section_params(0))
    second = out_one.astype(jnp.bfloat16).astype(jnp.float32)
    out_two, pull_two = jax.vjp(run_block, second, *section_params(1))
    grads_two = pull_two(cotangent)
    back_two = grads_two[0].astype(jnp.bfloat16)
    grads_one = pull_one(back_two.astype(jnp.float32))
    out_shape = (MB, IMAGES, TOKPAD, D)
    section_out = jnp.stack([out_one.astype(jnp.bfloat16).reshape(out_shape), out_two.astype(jnp.bfloat16).reshape(out_shape)])
    input_grad = jnp.stack([grads_one[0].astype(jnp.bfloat16).reshape(out_shape), back_two.reshape(out_shape)])
    stacked = [jnp.stack([one_grad, two_grad]) for one_grad, two_grad in zip(grads_one[1:], grads_two[1:])]
    return (section_out, input_grad, stacked[0], stacked[1], stacked[2], stacked[3], stacked[4], stacked[5], stacked[6], stacked[7])
```

```python
from functools import partial

import jax
import jax.numpy as jnp
from jax import lax
from jax.experimental import pallas as pl
from jax.experimental.pallas import tpu as pltpu
from jax.sharding import PartitionSpec as P

HD = 64
LANES = 128
EPS = 1e-06
NEG = -1000000000.0
F32 = jnp.float32
BF = jnp.bfloat16
BOTH = ("dp", "tensor")
MIB = 2**20


def dot_nt(a, b):
    return lax.dot_general(a, b, (((1,), (1,)), ((), ())), preferred_element_type=F32)


def dot_nn(a, b):
    return lax.dot_general(a, b, (((1,), (0,)), ((), ())), preferred_element_type=F32)


def dot_tn(a, b):
    return lax.dot_general(a, b, (((0,), (0,)), ((), ())), preferred_element_type=F32)


def lane_ids(shape):
    return lax.broadcasted_iota(jnp.int32, shape, 1)


def attend_kernel(q_ref, k_ref, v_ref, mask_ref, o_ref, lse_ref):
    pairs = q_ref.shape[1] // LANES
    mask = mask_ref[...]
    k_lane = lane_ids((k_ref.shape[0], LANES))
    q_lane = lane_ids((q_ref.shape[0], LANES))
    units = [(pair, half) for pair in range(pairs) for half in range(2)]
    scores, probs, done = {}, {}, {}

    def cols(pair):
        return slice(pair * LANES, (pair + 1) * LANES)

    def score(unit):
        pair, half = unit
        spare = HD * (1 - half)
        low_q = (q_ref[:, cols(pair)].astype(F32) * HD**-0.5).astype(BF)
        q_one = jnp.where(q_lane == spare, 1.0, 0.0).astype(BF)
        k_bias = jnp.where(k_lane == spare, mask, 0.0).astype(BF)
        q_own = jnp.where((q_lane // HD) == half, low_q, q_one)
        k_own = jnp.where((k_lane // HD) == half, k_ref[:, cols(pair)], k_bias)
        scores[unit] = dot_nt(q_own, k_own)

    def soften(unit):
        rows = scores.pop(unit)
        top = jnp.max(rows, axis=1, keepdims=True)
        probs[unit] = (jnp.exp(rows - top).astype(BF), top)

    def mix(unit):
        pair, half = unit
        spare = HD * (1 - half)
        prob, top = probs.pop(unit)
        v_one = jnp.where(k_lane == spare, 1.0, 0.0).astype(BF)
        v_own = jnp.where((k_lane // HD) == half, v_ref[:, cols(pair)], v_one)
        out = dot_nn(prob, v_own)
        total = out[:, spare : spare + 1]
        done[unit] = (out * (1.0 / total), top + jnp.log(total))
        if half == 1:
            first, second = done.pop((pair, 0)), done.pop(unit)
            o_ref[:, cols(pair)] = jnp.where(q_lane < HD, first[0], second[0]).astype(BF)
            lse_ref[:, cols(pair)] = jnp.where(q_lane < HD, first[1], second[1])

    for at in range(len(units) + 2):
        if at < len(units):
            score(units[at])
        if 0 <= at - 1 < len(units):
            soften(units[at - 1])
        if 0 <= at - 2:
            mix(units[at - 2])


def attend(queries, key_rows, values, mask):
    rows, width = queries.shape
    keys = key_rows.shape[0]
    wide = 2 * LANES
    q_spec = pl.BlockSpec((rows, wide), lambda i: (0, i))
    k_spec = pl.BlockSpec((keys, wide), lambda i: (0, i))
    pairs = rows * keys * width
    return pl.pallas_call(
        attend_kernel,
        grid=(width // wide,),
        in_specs=[q_spec, k_spec, k_spec, pl.BlockSpec((keys, LANES), lambda i: (0, 0))],
        out_specs=[q_spec, q_spec],
        out_shape=[
            jax.ShapeDtypeStruct((rows, width), BF),
            jax.ShapeDtypeStruct((rows, width), F32),
        ],
        compiler_params=pltpu.CompilerParams(vmem_limit_bytes=48 * MIB),
        cost_estimate=pl.CostEstimate(
            flops=16 * pairs, bytes_accessed=4 * keys * width + 8 * rows * width, transcendentals=pairs // HD
        ),
        name="attend",
    )(queries, key_rows, values, mask)


def split_three(value):
    first = value.astype(BF)
    rest = value - first.astype(F32)
    second = rest.astype(BF)
    return first, second, (rest - second.astype(F32)).astype(BF)


def attend_back_kernel(
    q_ref, k_ref, v_ref, mask_ref, ctx_ref, do_ref, lse_ref, dq_ref, dk_ref, dv_ref
):
    queries, key_rows, values, d_out = q_ref[...], k_ref[...], v_ref[...], do_ref[...]
    mask, lse = mask_ref[...], lse_ref[...]
    q_lane, k_lane = lane_ids(queries.shape), lane_ids(key_rows.shape)
    low_q = (queries.astype(F32) * HD**-0.5).astype(BF)
    product = d_out.astype(F32) * ctx_ref[...].astype(F32)
    zero_q, one_q = jnp.zeros_like(queries), jnp.ones_like(queries)
    d_q, d_k, d_v = [], [], []
    for half in range(2):
        spare = HD * (1 - half)
        q_own, k_own = (q_lane // HD) == half, (k_lane // HD) == half
        l_one, l_two, l_three = split_three(-lse[:, HD * half : HD * half + 1])
        inner = jnp.sum(jnp.where(q_own, product, 0.0), axis=1, keepdims=True)
        i_one, i_two, _ = split_three(-inner)
        q_more = jnp.where(q_lane == spare + 2, l_two, jnp.where(q_lane == spare + 3, l_three, zero_q))
        q_more = jnp.where(q_lane == spare, one_q, jnp.where(q_lane == spare + 1, l_one, q_more))
        k_more = jnp.where((k_lane > spare) & (k_lane < spare + 4), 1.0, 0.0).astype(BF)
        k_more = jnp.where(k_lane == spare, mask, k_more)
        o_more = jnp.where(q_lane == spare, i_one, jnp.where(q_lane == spare + 1, i_two, zero_q))
        v_more = jnp.where((k_lane >= spare) & (k_lane < spare + 2), 1.0, 0.0).astype(BF)
        prob = jnp.exp(dot_nt(jnp.where(q_own, low_q, q_more), jnp.where(k_own, key_rows, k_more)))
        d_prob = dot_nt(jnp.where(q_own, d_out, o_more), jnp.where(k_own, values, v_more))
        d_score = (prob * d_prob).astype(BF)
        d_v.append(dot_tn(prob.astype(BF), d_out))
        d_k.append(dot_tn(d_score, low_q))
        d_q.append(dot_nn(d_score, key_rows))
    dq_ref[...] = (jnp.where(q_lane < HD, d_q[0], d_q[1]) * HD**-0.5).astype(BF)
    dk_ref[...] = jnp.where(k_lane < HD, d_k[0], d_k[1]).astype(BF)
    dv_ref[...] = jnp.where(k_lane < HD, d_v[0], d_v[1]).astype(BF)


def attend_back(queries, key_rows, values, mask, context, d_context, lse):
    rows, width = queries.shape
    keys = key_rows.shape[0]
    q_spec = pl.BlockSpec((rows, LANES), lambda i: (0, i))
    k_spec = pl.BlockSpec((keys, LANES), lambda i: (0, i))
    pairs = rows * keys * width
    return pl.pallas_call(
        attend_back_kernel,
        grid=(width // LANES,),
        in_specs=[
            q_spec,
            k_spec,
            k_spec,
            pl.BlockSpec((keys, LANES), lambda i: (0, 0)),
            q_spec,
            q_spec,
            q_spec,
        ],
        out_specs=[q_spec, k_spec, k_spec],
        out_shape=[
            jax.ShapeDtypeStruct((rows, width), BF),
            jax.ShapeDtypeStruct((keys, width), BF),
            jax.ShapeDtypeStruct((keys, width), BF),
        ],
        compiler_params=pltpu.CompilerParams(vmem_limit_bytes=56 * MIB),
        cost_estimate=pl.CostEstimate(
            flops=40 * pairs, bytes_accessed=8 * keys * width + 12 * rows * width, transcendentals=pairs // HD
        ),
        name="attend_back",
    )(queries, key_rows, values, mask, context, d_context, lse)


def normalize(rows):
    mean = jnp.mean(rows, axis=-1, keepdims=True)
    centred = rows - mean
    spread = jnp.mean(centred * centred, axis=-1, keepdims=True)
    inverse = lax.rsqrt(spread + EPS)
    return centred * inverse, inverse


def layer_norm(rows, gain, shift):
    return normalize(rows)[0] * gain + shift


def layer_norm_back(rows, gain, d_out):
    normed, inverse = normalize(rows)
    scaled = gain * d_out
    mean = jnp.mean(scaled, axis=-1, keepdims=True)
    along = jnp.mean(scaled * normed, axis=-1, keepdims=True)
    d_rows = inverse * (scaled - mean - normed * along)
    return d_rows, jnp.sum(d_out * normed, axis=0), jnp.sum(d_out, axis=0)


def gelu_and_slope(x):
    size = jnp.abs(x)
    t = 1.0 / (1.0 + (0.3275911 * 0.7071067811865476) * size)
    bell = jnp.exp(-0.5 * x * x)
    poly = 0.5 * 1.061405429
    for factor in (-1.453152027, 1.421413741, -0.284496736, 0.254829592):
        poly = poly * t + 0.5 * factor
    tail = poly * t * bell
    below = jnp.where(x < 0.0, tail, 1.0 - tail)
    return x * below, below + x * bell * 0.3989422804014327


def local(
    block_input,
    out_cotangent,
    lengths,
    qkv_weight,
    qv_bias,
    proj_weight,
    fc1_weight,
    fc1_bias,
    fc2_weight,
    gains,
    biases,
):
    section_idx = lax.axis_index("section")
    dp_count, shard_count = lax.axis_size("dp"), lax.axis_size("tensor")
    dp_idx, shard_idx = lax.axis_index("dp"), lax.axis_index("tensor")
    micro_count, _, slots, width = block_input.shape
    hidden = fc1_weight.shape[2] * shard_count
    first_section = section_idx == 0

    span = shard_count // 2
    odd, own_u = dp_idx % 2, shard_idx % span

    swap_pairs = [
        ((2 * j + a) * shard_count + b * span + u, (2 * j + b) * shard_count + a * span + u)
        for j in range(dp_count // 2)
        for a in range(2)
        for b in range(2)
        for u in range(span)
    ]
    mate_pairs = [(d, d + 1 - 2 * (d % 2)) for d in range(dp_count)]

    def turned(steps):
        return [
            (half * span + (u + steps) % span, half * span + u) for half in range(2) for u in range(span)
        ]

    def swapped(rows):
        return lax.ppermute(rows, BOTH, swap_pairs)

    def gather_group(rows):
        pieces = [rows] + [lax.ppermute(rows, "tensor", turned(r)) for r in range(1, span)]
        near = jnp.concatenate(pieces, axis=0)
        return jnp.concatenate([near, lax.ppermute(near, "dp", mate_pairs)], axis=0)

    def reduce_group(own_rows, near_rows, mate_rows):
        got = lax.ppermute(mate_rows, "dp", mate_pairs).astype(F32)
        total = own_rows + got[:slots]
        for r in range(1, span):
            piece = near_rows[(r - 1) * slots : r * slots].astype(F32) + got[r * slots : (r + 1) * slots]
            total = total + lax.ppermute(piece.astype(BF), "tensor", turned(-r)).astype(F32)
        return total

    shard_of = jnp.stack([((odd + a) % 2) * span + (own_u + r) % span for a in range(2) for r in range(span)])
    slot_ids = jnp.arange(slots, dtype=jnp.int32)
    live = slot_ids[None, :] < jnp.take(lengths, shard_of)[:, None]
    own_live = live[0].astype(F32)[:, None]
    mask = jnp.broadcast_to(jnp.where(live.reshape(-1, 1), 0.0, NEG).astype(BF), (live.size, LANES))

    small = jnp.concatenate(
        [gains[0].reshape(-1), biases[0].reshape(-1), qv_bias[0].reshape(-1), fc1_bias[0].reshape(-1)]
    )
    small = lax.all_gather(small, BOTH, axis=0, tiled=False)
    own = width // (dp_count * shard_count)
    vectors = small[:, : 8 * own].reshape(-1, 8, own).transpose(1, 0, 2).reshape(8, width).astype(F32)
    gain_rows, bias_rows = vectors[:4], vectors[4:]
    shared = small[:shard_count, 8 * own :]
    cut = 2 * width // shard_count
    qv_rows = shared[:, :cut].reshape(shard_count, 2, -1).transpose(1, 0, 2).reshape(2, width).astype(F32)
    up_bias = shared[:, cut:].reshape(hidden).astype(F32)

    def whole(part):
        return lax.all_gather(part, BOTH, axis=0, tiled=False).reshape(
            (dp_count, shard_count) + part.shape
        )

    w_qkv = whole(qkv_weight[0]).transpose(0, 2, 3, 1, 4).reshape(width, 3, width)
    w_proj = whole(proj_weight[0]).transpose(1, 2, 0, 3).reshape(width, width)
    w_up = whole(fc1_weight[0]).transpose(0, 2, 1, 3).reshape(width, hidden)
    w_down = whole(fc2_weight[0]).transpose(1, 2, 0, 3).reshape(hidden, width)
    w_q, w_k, w_v = w_qkv[:, 0], w_qkv[:, 1], w_qkv[:, 2]

    def forward(rows):
        rows = rows.astype(F32)
        h_one = layer_norm(rows, gain_rows[0], bias_rows[0]).astype(BF)
        h_all = gather_group(h_one)
        queries = (dot_nn(h_one, w_q) + qv_rows[0]).astype(BF)
        key_rows = dot_nn(h_all, w_k).astype(BF)
        values = (dot_nn(h_all, w_v) + qv_rows[1]).astype(BF)
        context, lse = attend(queries, key_rows, values, mask)
        attn_out = dot_nn(context, w_proj) + bias_rows[1]
        mid_rows = rows + gain_rows[1] * attn_out
        h_two = layer_norm(mid_rows, gain_rows[2], bias_rows[2]).astype(BF)
        act, slope = gelu_and_slope(dot_nn(h_two, w_up) + up_bias)
        act, slope = act.astype(BF), slope.astype(BF)
        mlp_out = dot_nn(act, w_down) + bias_rows[3]
        result = own_live * (mid_rows + gain_rows[3] * mlp_out)
        saved = (
            rows, h_one, h_all, queries, key_rows, values, context, lse,
            attn_out, mid_rows, h_two, act, slope, mlp_out,
        )
        return result.astype(BF), saved

    def backward(cotangent, saved):
        (
            rows, h_one, h_all, queries, key_rows, values, context, lse,
            attn_out, mid_rows, h_two, act, slope, mlp_out,
        ) = saved
        d_res = own_live * cotangent.astype(F32)
        d_scale_two = jnp.sum(d_res * mlp_out, axis=0)
        d_mlp_full = gain_rows[3] * d_res
        d_bias_three = jnp.sum(d_mlp_full, axis=0)
        d_mlp = d_mlp_full.astype(BF)
        d_pre = (dot_nt(d_mlp, w_down) * slope.astype(F32)).astype(BF)
        d_up_bias = jnp.sum(d_pre.astype(F32), axis=0)
        d_h_two = dot_nt(d_pre, w_up)
        d_mid_ln, d_gain_two, d_shift_two = layer_norm_back(mid_rows, gain_rows[2], d_h_two)
        d_mid = d_res + d_mid_ln
        d_scale_one = jnp.sum(d_mid * attn_out, axis=0)
        d_attn_full = gain_rows[1] * d_mid
        d_bias_one = jnp.sum(d_attn_full, axis=0)
        d_attn = d_attn_full.astype(BF)
        d_context = dot_nt(d_attn, w_proj).astype(BF)
        d_q, d_k, d_v = attend_back(queries, key_rows, values, mask, context, d_context, lse)
        d_qv = jnp.stack([jnp.sum(d_q.astype(F32), axis=0), jnp.sum(d_v.astype(F32), axis=0)])
        far = (dot_nt(d_k[slots:], w_k) + dot_nt(d_v[slots:], w_v)).astype(BF)
        own_part = dot_nt(d_k[:slots], w_k) + dot_nt(d_v[:slots], w_v) + dot_nt(d_q, w_q)
        d_h_one = reduce_group(own_part, far[: (span - 1) * slots], far[(span - 1) * slots :])
        d_rows_ln, d_gain_one, d_shift_one = layer_norm_back(rows, gain_rows[0], d_h_one)
        d_rows = (d_mid + d_rows_ln).astype(BF)
        sums = jnp.concatenate(
            [
                jnp.stack([d_gain_one, d_scale_one, d_gain_two, d_scale_two]).reshape(-1),
                jnp.stack([d_shift_one, d_bias_one, d_shift_two, d_bias_three]).reshape(-1),
                d_qv.reshape(-1),
                d_up_bias,
            ]
        )
        operands = (
            (act, d_mlp), (h_two, d_pre), (context, d_attn), (h_one, d_q), (h_all, d_k), (h_all, d_v)
        )
        return d_rows, sums, operands

    tokens = [swapped(block_input[m, 0]) for m in range(micro_count)]
    cotangents = [swapped(out_cotangent[m, 0]) for m in range(micro_count)]

    start_out, start_saved, received = [], None, []
    for m in range(micro_count):
        low, start_saved = forward(tokens[m])
        start_out.append(low)
        received.append(lax.ppermute(low, "section", [(0, 1)]))

    zero_rows = jnp.zeros_like(tokens[0])
    late_out, back_rows, sums, operands = [], [], [], []
    d_received = zero_rows
    for m in range(micro_count):
        low, saved = forward(jnp.where(first_section, tokens[max(m - 1, 0)], received[m]))
        late_out.append(low)
        d_low, part, pieces = backward(jnp.where(first_section, d_received, cotangents[m]), saved)
        d_received = lax.ppermute(d_low, "section", [(1, 0)])
        back_rows.append(d_low)
        sums.append(part)
        operands.append(pieces)
    d_low, part, pieces = backward(jnp.where(first_section, d_received, zero_rows), start_saved)
    back_rows.append(d_low)
    sums.append(part)
    operands.append(pieces)

    def joined(which, side):
        return jnp.concatenate([pieces[which][side] for pieces in operands], axis=0)

    def weight_grad(which):
        return dot_tn(joined(which, 0), joined(which, 1)).astype(BF)

    def scattered(grad):
        return lax.psum_scatter(grad, BOTH, scatter_dimension=0, tiled=False).astype(F32)

    rows_dp, rows_shard = width // dp_count, width // shard_count
    every = dp_count * shard_count
    d_down = scattered(
        weight_grad(0)
        .reshape(shard_count, hidden // shard_count, dp_count, rows_dp)
        .transpose(2, 0, 1, 3)
        .reshape(every, hidden // shard_count, rows_dp)
    )
    d_up = scattered(
        weight_grad(1)
        .reshape(dp_count, rows_dp, shard_count, hidden // shard_count)
        .transpose(0, 2, 1, 3)
        .reshape(every, rows_dp, hidden // shard_count)
    )
    d_proj = scattered(
        weight_grad(2)
        .reshape(shard_count, rows_shard, dp_count, rows_dp)
        .transpose(2, 0, 1, 3)
        .reshape(every, rows_shard, rows_dp)
    )
    d_qkv = scattered(
        jnp.stack([weight_grad(3), weight_grad(4), weight_grad(5)], axis=1)
        .reshape(dp_count, rows_dp, 3, shard_count, rows_shard)
        .transpose(0, 3, 1, 2, 4)
        .reshape(every, rows_dp, 3, rows_shard)
    )

    total = lax.psum(sum(sums), BOTH)
    place = (dp_idx * shard_count + shard_idx) * own
    gain_grad = lax.dynamic_slice_in_dim(total[: 4 * width].reshape(4, width), place, own, 1)
    bias_grad = lax.dynamic_slice_in_dim(total[4 * width : 8 * width].reshape(4, width), place, own, 1)
    qv_grad = lax.dynamic_slice_in_dim(
        total[8 * width : 10 * width].reshape(2, width), shard_idx * rows_shard, rows_shard, 1
    )
    up_bias_grad = lax.dynamic_slice_in_dim(
        total[10 * width :], shard_idx * (hidden // shard_count), hidden // shard_count, 0
    )

    section_out = jnp.stack(
        [swapped(jnp.where(first_section, start_out[m], late_out[m])) for m in range(micro_count)]
    )
    input_grad = jnp.stack(
        [swapped(jnp.where(first_section, back_rows[m + 1], back_rows[m])) for m in range(micro_count)]
    )
    return (
        section_out[None, :, None],
        input_grad[None, :, None],
        d_qkv[None],
        qv_grad[None],
        d_proj[None],
        d_up[None],
        up_bias_grad[None],
        d_down[None],
        gain_grad[None],
        bias_grad[None],
    )


def solution(mesh):
    in_specs = (
        P(None, "dp", "tensor", None),
        P(None, "dp", "tensor", None),
        P(),
        P("section", "dp", None, "tensor"),
        P("section", None, "tensor"),
        P("section", "tensor", "dp"),
        P("section", "dp", "tensor"),
        P("section", "tensor"),
        P("section", "tensor", "dp"),
        P("section", None, ("dp", "tensor")),
        P("section", None, ("dp", "tensor")),
    )
    out_specs = (
        P("section", None, "dp", "tensor", None),
        P("section", None, "dp", "tensor", None),
        P("section", "dp", None, "tensor"),
        P("section", None, "tensor"),
        P("section", "tensor", "dp"),
        P("section", "dp", "tensor"),
        P("section", "tensor"),
        P("section", "tensor", "dp"),
        P("section", None, ("dp", "tensor")),
        P("section", None, ("dp", "tensor")),
    )
    return jax.shard_map(local, mesh=mesh, in_specs=in_specs, out_specs=out_specs, check_vma=False)
```

```python
from functools import partial

import jax
import jax.numpy as jnp
from jax import lax
from jax.experimental import pallas as pl
from jax.experimental.pallas import tpu as pltpu
from jax.sharding import PartitionSpec as P

HD = 64
LANES = 128
EPS = 1e-06
NEG = -1000000000.0
F32 = jnp.float32
BF = jnp.bfloat16
BOTH = ("dp", "tensor")
MIB = 2**20


def dot_nt(a, b):
    return lax.dot_general(a, b, (((1,), (1,)), ((), ())), preferred_element_type=F32)


def dot_nn(a, b):
    return lax.dot_general(a, b, (((1,), (0,)), ((), ())), preferred_element_type=F32)


def dot_tn(a, b):
    return lax.dot_general(a, b, (((0,), (0,)), ((), ())), preferred_element_type=F32)


def normalize(rows):
    mean = jnp.mean(rows, axis=-1, keepdims=True)
    centred = rows - mean
    spread = jnp.mean(centred * centred, axis=-1, keepdims=True)
    inverse = lax.rsqrt(spread + EPS)
    return centred * inverse, inverse


def layer_norm(rows, gain, shift):
    return normalize(rows)[0] * gain + shift


def layer_norm_back(rows, gain, d_out):
    normed, inverse = normalize(rows)
    scaled = gain * d_out
    mean = jnp.mean(scaled, axis=-1, keepdims=True)
    along = jnp.mean(scaled * normed, axis=-1, keepdims=True)
    d_rows = inverse * (scaled - mean - normed * along)
    d_gain = jnp.sum(d_out * normed, axis=0, keepdims=True)
    return d_rows, d_gain, jnp.sum(d_out, axis=0, keepdims=True)


def gelu_and_slope(x):
    size = jnp.abs(x)
    t = 1.0 / (1.0 + (0.3275911 * 0.7071067811865476) * size)
    bell = jnp.exp(-0.5 * x * x)
    poly = 0.5 * 1.061405429
    for factor in (-1.453152027, 1.421413741, -0.284496736, 0.254829592):
        poly = poly * t + 0.5 * factor
    tail = poly * t * bell
    below = jnp.where(x < 0.0, tail, 1.0 - tail)
    return x * below, below + x * bell * 0.3989422804014327


def lane_ids(shape):
    return lax.broadcasted_iota(jnp.int32, shape, 1)


def staged(units, *stages):
    for at in range(len(units) + len(stages) - 1):
        for late, stage in enumerate(stages):
            if 0 <= at - late < len(units):
                stage(units[at - late])


def in_pairs(count, rise, bend, fall):
    waiting = []
    rise(0)
    for unit in range(count):
        if unit + 1 < count:
            rise(unit + 1)
        bend(unit)
        if unit % 2:
            waiting.append(unit)
        if waiting and (unit % 2 == 0 or unit + 1 == count):
            for ready in waiting:
                fall(ready)
            waiting = []


def stack_rows(blocks):
    return blocks.reshape(blocks.shape[0] * blocks.shape[1], blocks.shape[2])


def join_cols(blocks):
    return jnp.concatenate([blocks[i] for i in range(blocks.shape[0])], axis=1)


def call(kernel, grid, ins, outs, scratch, flops, name):
    arrays, in_specs = zip(*ins)
    shapes, out_specs = zip(*outs)
    moved = sum(a.size * a.dtype.itemsize for a in arrays) + sum(s.size * s.dtype.itemsize for s in shapes)
    return pl.pallas_call(
        kernel,
        grid=(grid,),
        in_specs=list(in_specs),
        out_specs=list(out_specs),
        out_shape=list(shapes),
        scratch_shapes=scratch,
        compiler_params=pltpu.CompilerParams(vmem_limit_bytes=60 * MIB),
        cost_estimate=pl.CostEstimate(flops=flops, bytes_accessed=moved, transcendentals=0),
        name=name,
    )(*arrays)


def fixed(shape):
    return pl.BlockSpec(shape, lambda i: (0,) * len(shape))


def by_cols(rows, cols):
    return pl.BlockSpec((rows, cols), lambda i: (0, i))


def by_shard(blocks, rows=None, at=0):
    dp, _, own_rows, cols = blocks.shape
    return pl.BlockSpec((dp, 1, rows or own_rows, cols), lambda i: (0, i, at, 0))


def attend_kernel(
    h_ref, h_all_ref, w_ref, bias_ref, mask_ref, q_ref, k_ref, v_ref, o_ref, lse_ref
):
    part = q_ref.shape[1]
    w_q, w_k, w_v = (stack_rows(w_ref[:, 0, n * part : (n + 1) * part]) for n in range(3))
    q_ref[...] = (dot_nn(h_ref[...], w_q) + bias_ref[0:1]).astype(BF)
    k_ref[...] = dot_nn(h_all_ref[...], w_k).astype(BF)
    v_ref[...] = (dot_nn(h_all_ref[...], w_v) + bias_ref[1:2]).astype(BF)
    mask = mask_ref[...]
    k_lane, q_lane = lane_ids((k_ref.shape[0], LANES)), lane_ids((q_ref.shape[0], LANES))
    units = [(pair, half) for pair in range(part // LANES) for half in range(2)]
    scores, probs, done = {}, {}, {}

    def cols(pair):
        return slice(pair * LANES, (pair + 1) * LANES)

    def score(unit):
        pair, half = unit
        spare = HD * (1 - half)
        low_q = (q_ref[:, cols(pair)].astype(F32) * HD**-0.5).astype(BF)
        q_one = jnp.where(q_lane == spare, 1.0, 0.0).astype(BF)
        k_bias = jnp.where(k_lane == spare, mask, 0.0).astype(BF)
        q_own = jnp.where((q_lane // HD) == half, low_q, q_one)
        k_own = jnp.where((k_lane // HD) == half, k_ref[:, cols(pair)], k_bias)
        scores[unit] = dot_nt(q_own, k_own)

    def soften(unit):
        rows = scores.pop(unit)
        top = jnp.max(rows, axis=1, keepdims=True)
        probs[unit] = (jnp.exp(rows - top).astype(BF), top)

    def mix(unit):
        pair, half = unit
        spare = HD * (1 - half)
        prob, top = probs.pop(unit)
        v_one = jnp.where(k_lane == spare, 1.0, 0.0).astype(BF)
        v_own = jnp.where((k_lane // HD) == half, v_ref[:, cols(pair)], v_one)
        out = dot_nn(prob, v_own)
        total = out[:, spare : spare + 1]
        done[unit] = (out * (1.0 / total), top + jnp.log(total))
        if half == 1:
            first, second = done.pop((pair, 0)), done.pop(unit)
            o_ref[:, cols(pair)] = jnp.where(q_lane < HD, first[0], second[0]).astype(BF)
            lse_ref[:, cols(pair)] = jnp.where(q_lane < HD, first[1], second[1])

    staged(units, score, soften, mix)


def attend(h_one, h_all, w_attn, qv_rows, mask):
    slots, width = h_one.shape
    keys = h_all.shape[0]
    part = w_attn.shape[3]
    own, every = by_cols(slots, part), by_cols(keys, part)
    row = jax.ShapeDtypeStruct((slots, width), BF)
    col = jax.ShapeDtypeStruct((keys, width), BF)
    return call(
        attend_kernel,
        w_attn.shape[1],
        [
            (h_one, fixed(h_one.shape)),
            (h_all, fixed(h_all.shape)),
            (w_attn, by_shard(w_attn, 3 * part)),
            (qv_rows, by_cols(2, part)),
            (mask, fixed(mask.shape)),
        ],
        [(row, own), (col, every), (col, every), (row, own), (jax.ShapeDtypeStruct(row.shape, F32), own)],
        [],
        width * (2 * width * (slots + 2 * keys) + 16 * slots * keys),
        "attend",
    )


def split_three(value):
    first = value.astype(BF)
    rest = value - first.astype(F32)
    second = rest.astype(BF)
    return first, second, (rest - second.astype(F32)).astype(BF)


def attend_back_kernel(
    d_attn_ref, w_proj_ref, w_ref, q_ref, k_ref, v_ref, ctx_ref, lse_ref, mask_ref,
    dq_ref, dk_ref, dv_ref, sums_ref, own_ref, near_ref, mate_ref,
    do_ref, acc_q, acc_k,
):
    slots, part = q_ref.shape
    do_ref[...] = dot_nt(d_attn_ref[...], join_cols(w_proj_ref[:, 0])).astype(BF)
    mask = mask_ref[...]
    q_lane, k_lane = lane_ids((slots, LANES)), lane_ids((k_ref.shape[0], LANES))
    units = [(pair, half) for pair in range(part // LANES) for half in range(2)]
    first_part, done = {}, {}

    def cols(pair):
        return slice(pair * LANES, (pair + 1) * LANES)

    def low_queries(pair):
        return (q_ref[:, cols(pair)].astype(F32) * HD**-0.5).astype(BF)

    def score(unit):
        pair, half = unit
        at = cols(pair)
        spare = HD * (1 - half)
        d_out, lse = do_ref[:, at], lse_ref[:, at]
        q_own, k_own = (q_lane // HD) == half, (k_lane // HD) == half
        zero_q, one_q = jnp.zeros(q_lane.shape, BF), jnp.ones(q_lane.shape, BF)
        l_one, l_two, l_three = split_three(-lse[:, HD * half : HD * half + 1])
        product = d_out.astype(F32) * ctx_ref[:, at].astype(F32)
        inner = jnp.sum(jnp.where(q_own, product, 0.0), axis=1, keepdims=True)
        i_one, i_two, _ = split_three(-inner)
        q_more = jnp.where(q_lane == spare + 2, l_two, jnp.where(q_lane == spare + 3, l_three, zero_q))
        q_more = jnp.where(q_lane == spare, one_q, jnp.where(q_lane == spare + 1, l_one, q_more))
        k_more = jnp.where((k_lane > spare) & (k_lane < spare + 4), 1.0, 0.0).astype(BF)
        k_more = jnp.where(k_lane == spare, mask, k_more)
        o_more = jnp.where(q_lane == spare, i_one, jnp.where(q_lane == spare + 1, i_two, zero_q))
        v_more = jnp.where((k_lane >= spare) & (k_lane < spare + 2), 1.0, 0.0).astype(BF)
        score = dot_nt(jnp.where(q_own, low_queries(pair), q_more), jnp.where(k_own, k_ref[:, at], k_more))
        d_prob = dot_nt(jnp.where(q_own, d_out, o_more), jnp.where(k_own, v_ref[:, at], v_more))
        prob = jnp.exp(score)
        first_part[unit] = (prob.astype(BF), (prob * d_prob).astype(BF))

    def mix(unit):
        pair, half = unit
        at = cols(pair)
        prob, d_score = first_part.pop(unit)
        done[unit] = (
            dot_nn(d_score, k_ref[:, at]) * HD**-0.5,
            dot_tn(d_score, low_queries(pair)),
            dot_tn(prob, do_ref[:, at]),
        )
        if half == 1:
            one, two = done.pop((pair, 0)), done.pop(unit)
            d_q = jnp.where(q_lane < HD, one[0], two[0]).astype(BF)
            d_k = jnp.where(k_lane < HD, one[1], two[1]).astype(BF)
            d_v = jnp.where(k_lane < HD, one[2], two[2]).astype(BF)
            dq_ref[:, at], dk_ref[:, at], dv_ref[:, at] = d_q, d_k, d_v
            sums_ref[0:1, at] = jnp.sum(d_q.astype(F32), axis=0, keepdims=True)
            sums_ref[1:2, at] = jnp.sum(d_v.astype(F32), axis=0, keepdims=True)

    staged(units, score, mix)
    w_q, w_k, w_v = (stack_rows(w_ref[:, 0, n * part : (n + 1) * part]) for n in range(3))
    from_q = dot_nt(dq_ref[...], w_q)
    from_k = dot_nt(
        jnp.concatenate([dk_ref[...], dv_ref[...]], axis=1), jnp.concatenate([w_k, w_v], axis=1)
    )

    @pl.when(pl.program_id(0) == 0)
    def _():
        acc_q[...] = from_q
        acc_k[...] = from_k

    @pl.when(pl.program_id(0) > 0)
    def _():
        acc_q[...] += from_q
        acc_k[...] += from_k

    @pl.when(pl.program_id(0) == pl.num_programs(0) - 1)
    def _():
        near = near_ref.shape[0]
        own_ref[...] = acc_q[...] + acc_k[0:slots]
        near_ref[...] = acc_k[slots : slots + near].astype(BF)
        mate_ref[...] = acc_k[slots + near :].astype(BF)


def attend_back(d_attn, w_attn, queries, key_rows, values, context, lse, mask):
    slots, width = queries.shape
    keys = key_rows.shape[0]
    part = w_attn.shape[3]
    own, every = by_cols(slots, part), by_cols(keys, part)
    row = jax.ShapeDtypeStruct((slots, width), BF)
    col = jax.ShapeDtypeStruct((keys, width), BF)
    near = jax.ShapeDtypeStruct((keys // 2 - slots, width), BF)
    mate = jax.ShapeDtypeStruct((keys // 2, width), BF)
    return call(
        attend_back_kernel,
        w_attn.shape[1],
        [
            (d_attn, fixed(d_attn.shape)),
            (w_attn, by_shard(w_attn, part, 3)),
            (w_attn, by_shard(w_attn, 3 * part)),
            (queries, own),
            (key_rows, every),
            (values, every),
            (context, own),
            (lse, own),
            (mask, fixed(mask.shape)),
        ],
        [
            (row, own),
            (col, every),
            (col, every),
            (jax.ShapeDtypeStruct((2, width), F32), by_cols(2, part)),
            (jax.ShapeDtypeStruct((slots, width), F32), fixed((slots, width))),
            (near, fixed(near.shape)),
            (mate, fixed(mate.shape)),
        ],
        [pltpu.VMEM((slots, part), BF), pltpu.VMEM((slots, width), F32), pltpu.VMEM((keys, width), F32)],
        width * (2 * width * (2 * slots + 2 * keys) + 40 * slots * keys),
        "attend_back",
    )


def mlp_kernel(
    ctx_ref, rows_ref, w_proj_ref, vec_ref, live_ref, bias_ref, w_up_ref, w_down_ref,
    attn_ref, mid_ref, h_ref, act_ref, slope_ref, out_ref, low_ref,
):
    dp, _, part, _ = w_up_ref.shape
    step = pl.program_id(0)

    @pl.when(step == 0)
    def _():
        context = ctx_ref[...]
        sides = [dot_nn(context, stack_rows(w_proj_ref[i])) for i in range(dp)]
        attn_out = jnp.concatenate(sides, axis=1) + vec_ref[5:6]
        attn_ref[...] = attn_out
        mid = rows_ref[...].astype(F32) + vec_ref[1:2] * attn_out
        mid_ref[...] = mid
        h_ref[...] = layer_norm(mid, vec_ref[2:3], vec_ref[6:7]).astype(BF)
        out_ref[...] = jnp.zeros_like(out_ref)

    h = h_ref[...]
    piece = w_up_ref.shape[3]
    pre, act = {}, {}

    def rise(unit):
        at = slice(unit * piece, (unit + 1) * piece)
        pre[unit] = dot_nn(h, stack_rows(w_up_ref[:, 0, at])) + bias_ref[:, at]

    def bend(unit):
        at = slice(unit * piece, (unit + 1) * piece)
        value, slope = gelu_and_slope(pre.pop(unit))
        act[unit] = value.astype(BF)
        act_ref[:, at] = act[unit]
        slope_ref[:, at] = slope.astype(BF)

    def fall(unit):
        at = slice((unit - 1) * piece, (unit + 1) * piece)
        both = jnp.concatenate([act.pop(unit - 1), act.pop(unit)], axis=1)
        out_ref[...] += dot_nn(both, join_cols(w_down_ref[:, 0, at]))

    in_pairs(part // piece, rise, bend, fall)

    @pl.when(step == pl.num_programs(0) - 1)
    def _():
        mlp_out = out_ref[...] + vec_ref[7:8]
        out_ref[...] = mlp_out
        low_ref[...] = (live_ref[:, 0:1] * (mid_ref[...] + vec_ref[3:4] * mlp_out)).astype(BF)


def mlp(context, rows, w_attn, vectors, live, up_bias, w_mlp):
    slots, width = rows.shape
    dp, shards, part, lanes = w_mlp.shape
    part = part // 2
    hidden = part * shards
    full = fixed((slots, width))
    wide = jax.ShapeDtypeStruct((slots, width), F32)
    low = jax.ShapeDtypeStruct((slots, width), BF)
    tall = jax.ShapeDtypeStruct((slots, hidden), BF)
    return call(
        mlp_kernel,
        shards,
        [
            (context, full),
            (rows, full),
            (w_attn, pl.BlockSpec((dp, shards, lanes, lanes), lambda i: (0, 0, 3, 0))),
            (vectors, fixed(vectors.shape)),
            (live, fixed(live.shape)),
            (up_bias, by_cols(1, part)),
            (w_mlp, by_shard(w_mlp, part)),
            (w_mlp, by_shard(w_mlp, part, 1)),
        ],
        [
            (wide, full),
            (wide, full),
            (low, full),
            (tall, by_cols(slots, part)),
            (tall, by_cols(slots, part)),
            (wide, full),
            (low, full),
        ],
        [],
        2 * slots * width * (width + 2 * hidden),
        "mlp",
    )


def mlp_back_kernel(
    cot_ref, live_ref, vec_ref, out_ref, mid_ref, attn_ref, slope_ref, w_up_ref, w_down_ref,
    d_mlp_ref, d_pre_ref, d_mid_ref, d_attn_ref, sums_ref, up_sum_ref,
    acc,
):
    part = slope_ref.shape[1]
    step = pl.program_id(0)

    @pl.when(step == 0)
    def _():
        d_res = live_ref[:, 0:1] * cot_ref[...].astype(F32)
        d_mlp = vec_ref[3:4] * d_res
        sums_ref[3:4] = jnp.sum(d_res * out_ref[...], axis=0, keepdims=True)
        sums_ref[7:8] = jnp.sum(d_mlp, axis=0, keepdims=True)
        d_mlp_ref[...] = d_mlp.astype(BF)
        acc[...] = jnp.zeros_like(acc)

    d_mlp = d_mlp_ref[...]
    piece = w_up_ref.shape[3]
    d_act, d_pre = {}, {}

    def rise(unit):
        at = slice(unit * piece, (unit + 1) * piece)
        d_act[unit] = dot_nt(d_mlp, join_cols(w_down_ref[:, 0, at]))

    def bend(unit):
        at = slice(unit * piece, (unit + 1) * piece)
        d_pre[unit] = (d_act.pop(unit) * slope_ref[:, at].astype(F32)).astype(BF)
        d_pre_ref[:, at] = d_pre[unit]
        up_sum_ref[:, at] = jnp.sum(d_pre[unit].astype(F32), axis=0, keepdims=True)

    def fall(unit):
        both = jnp.concatenate([d_pre.pop(unit - 1), d_pre.pop(unit)], axis=1)
        w_up = [stack_rows(w_up_ref[:, 0, u * piece : (u + 1) * piece]) for u in (unit - 1, unit)]
        acc[...] += dot_nt(both, jnp.concatenate(w_up, axis=1))

    in_pairs(part // piece, rise, bend, fall)

    @pl.when(step == pl.num_programs(0) - 1)
    def _():
        d_mid_ln, d_gain, d_shift = layer_norm_back(mid_ref[...], vec_ref[2:3], acc[...])
        d_mid = live_ref[:, 0:1] * cot_ref[...].astype(F32) + d_mid_ln
        d_attn = vec_ref[1:2] * d_mid
        d_mid_ref[...] = d_mid
        d_attn_ref[...] = d_attn.astype(BF)
        sums_ref[2:3] = d_gain
        sums_ref[6:7] = d_shift
        sums_ref[1:2] = jnp.sum(d_mid * attn_ref[...], axis=0, keepdims=True)
        sums_ref[5:6] = jnp.sum(d_attn, axis=0, keepdims=True)
        sums_ref[0:1] = jnp.zeros_like(d_gain)
        sums_ref[4:5] = jnp.zeros_like(d_gain)


def mlp_back(cotangent, live, vectors, mlp_out, mid_rows, attn_out, slope, w_mlp):
    slots, width = cotangent.shape
    part, shards = w_mlp.shape[2] // 2, w_mlp.shape[1]
    hidden = part * shards
    full = fixed((slots, width))
    low = jax.ShapeDtypeStruct((slots, width), BF)
    return call(
        mlp_back_kernel,
        shards,
        [
            (cotangent, full),
            (live, fixed(live.shape)),
            (vectors, fixed(vectors.shape)),
            (mlp_out, full),
            (mid_rows, full),
            (attn_out, full),
            (slope, by_cols(slots, part)),
            (w_mlp, by_shard(w_mlp, part)),
            (w_mlp, by_shard(w_mlp, part, 1)),
        ],
        [
            (low, full),
            (jax.ShapeDtypeStruct((slots, hidden), BF), by_cols(slots, part)),
            (jax.ShapeDtypeStruct((slots, width), F32), full),
            (low, full),
            (jax.ShapeDtypeStruct((8, width), F32), fixed((8, width))),
            (jax.ShapeDtypeStruct((1, hidden), F32), by_cols(1, part)),
        ],
        [pltpu.VMEM((slots, width), F32)],
        4 * slots * width * hidden,
        "mlp_back",
    )


def down_grad_kernel(steps, *refs):
    out_ref = refs[-1]
    total = sum(dot_tn(refs[2 * s][...], refs[2 * s + 1][...]) for s in range(steps))
    cols = out_ref.shape[3]
    for i in range(out_ref.shape[0]):
        out_ref[i, 0] = total[:, i * cols : (i + 1) * cols].astype(BF)


def up_grad_kernel(steps, *refs):
    out_ref = refs[-1]
    total = sum(dot_tn(refs[2 * s][...], refs[2 * s + 1][...]) for s in range(steps))
    out_ref[:, 0] = total.reshape(out_ref.shape[0], out_ref.shape[2], out_ref.shape[3]).astype(BF)


def attn_grad_kernel(steps, *refs):
    out_ref = refs[-1]
    dp, _, _, lanes = out_ref.shape
    groups = [refs[7 * s : 7 * s + 7] for s in range(steps)]
    for n, (left, right) in enumerate(((0, 2), (1, 3), (1, 4))):
        total = sum(dot_tn(g[left][...], g[right][...]) for g in groups)
        out_ref[:, 0, n * lanes : (n + 1) * lanes] = total.reshape(dp, lanes, lanes).astype(BF)
    total = sum(dot_tn(g[5][...], g[6][...]) for g in groups)
    for i in range(dp):
        out_ref[i, 0, 3 * lanes :] = total[:, i * lanes : (i + 1) * lanes].astype(BF)


def attn_grad(steps, dp, shards):
    ins, flops = [], 0
    lanes = steps[0][0].shape[1] // shards
    for h_one, h_all, d_q, d_k, d_v, context, d_attn in steps:
        ins += [(h_one, fixed(h_one.shape)), (h_all, fixed(h_all.shape))]
        ins += [(d, by_cols(d.shape[0], lanes)) for d in (d_q, d_k, d_v, context)]
        ins += [(d_attn, fixed(d_attn.shape))]
        flops += 4 * (h_one.size + h_all.size) * h_one.shape[1]
    out = jax.ShapeDtypeStruct((dp, shards, 4 * lanes, lanes), BF)
    return call(partial(attn_grad_kernel, len(steps)), shards, ins, [(out, by_shard(out))], [], flops, "attn_grad")[0]


def down_grad(pairs, dp, shards):
    rows, cols = pairs[0][0].shape[1] // shards, pairs[0][1].shape[1] // dp
    ins = []
    for left, right in pairs:
        ins += [(left, by_cols(left.shape[0], rows)), (right, fixed(right.shape))]
    out = jax.ShapeDtypeStruct((dp, shards, rows, cols), BF)
    flops = sum(2 * left.size * right.shape[1] for left, right in pairs)
    return call(partial(down_grad_kernel, len(pairs)), shards, ins, [(out, by_shard(out))], [], flops, "down_grad")[0]


def up_grad(pairs, dp, shards):
    rows, cols = pairs[0][0].shape[1] // dp, pairs[0][1].shape[1] // shards
    ins = []
    for left, right in pairs:
        ins += [(left, fixed(left.shape)), (right, by_cols(right.shape[0], cols))]
    out = jax.ShapeDtypeStruct((dp, shards, rows, cols), BF)
    flops = sum(2 * left.size * right.shape[1] for left, right in pairs)
    return call(partial(up_grad_kernel, len(pairs)), shards, ins, [(out, by_shard(out))], [], flops, "up_grad")[0]


def shed_order(count, place):
    return sorted(range(count), key=lambda t: (-abs(t - place), -t))


def scatter_kernel(dp, shards, kinds, *refs):
    parts, outs = refs[:kinds], refs[kinds : 2 * kinds]
    own, got, side, line = (refs[(2 + n) * kinds : (3 + n) * kinds] for n in range(4))
    load_sem, core_sem, side_sem, line_sem = refs[6 * kinds :]
    groups = dp // 2
    section, dp_idx, place = lax.axis_index("section"), lax.axis_index("dp"), lax.axis_index("tensor")
    group, odd = dp_idx // 2, dp_idx % 2
    mate = (section, group * 2 + 1 - odd, place)
    others = [(section, lax.rem(group + r, groups) * 2 + odd, place) for r in range(1, groups)]
    before, after = (section, dp_idx, place - 1), (section, dp_idx, place + 1)
    mesh_id = pl.DeviceIdType.MESH
    tables = [shed_order(shards, z) for z in range(shards)]

    def owner(step):
        return sum(jnp.where(place == z, tables[z][step], 0) for z in range(shards))

    barrier = pltpu.get_barrier_semaphore()
    for device in [mate] + others:
        pl.semaphore_signal(barrier, inc=1, device_id=device, device_id_type=mesh_id)

    @pl.when(place > 0)
    def _():
        pl.semaphore_signal(barrier, inc=1, device_id=before, device_id_type=mesh_id)

    @pl.when(place < shards - 1)
    def _():
        pl.semaphore_signal(barrier, inc=1, device_id=after, device_id_type=mesh_id)

    ends = jnp.where(place == 0, 1, 0) + jnp.where(place == shards - 1, 1, 0)
    pl.semaphore_wait(barrier, groups + 2 - ends)

    def core_copy(step, kind):
        return pltpu.make_async_remote_copy(
            src_ref=parts[kind].at[:, 1 - odd, owner(step)],
            dst_ref=got[kind].at[step],
            send_sem=core_sem.at[0, step, kind],
            recv_sem=core_sem.at[1, step, kind],
            device_id=mate,
            device_id_type=mesh_id,
        )

    def load(step, kind):
        return pltpu.make_async_copy(
            parts[kind].at[:, odd, owner(step)], own[kind].at[step], load_sem.at[step, kind]
        )

    def side_copy(step, kind, r):
        return pltpu.make_async_remote_copy(
            src_ref=own[kind].at[step, lax.rem(group + r, groups)],
            dst_ref=side[kind].at[step, r - 1],
            send_sem=side_sem.at[0, step, kind, r - 1],
            recv_sem=side_sem.at[1, step, kind, r - 1],
            device_id=others[r - 1],
            device_id_type=mesh_id,
        )

    def line_copy(step, kind, ahead):
        target = owner(step)
        slot = target + 1 if ahead else target
        return pltpu.make_async_remote_copy(
            src_ref=own[kind].at[step, group],
            dst_ref=line[kind].at[slot],
            send_sem=line_sem.at[0, slot, kind],
            recv_sem=line_sem.at[1, slot, kind],
            device_id=after if ahead else before,
            device_id_type=mesh_id,
        )

    def add(one, two):
        return (one.astype(F32) + two.astype(F32)).astype(one.dtype)

    units = [(step, kind) for step in range(shards) for kind in range(kinds)]
    for step, kind in units:
        core_copy(step, kind).start()
        load(step, kind).start()

    def meet(unit):
        step, kind = unit
        load(step, kind).wait()
        core_copy(step, kind).wait_recv()
        for r in range(1, groups):
            at = lax.rem(group + r, groups)
            own[kind][step, at] = add(own[kind][step, at], got[kind][step, at])
            side_copy(step, kind, r).start()
        own[kind][step, group] = add(own[kind][step, group], got[kind][step, group])

    def pass_on(unit):
        step, kind = unit
        mine = own[kind][step, group].astype(F32)
        for r in range(1, groups):
            side_copy(step, kind, r).wait_recv()
            mine = mine + side[kind][step, r - 1].astype(F32)
        own[kind][step, group] = mine.astype(own[kind].dtype)
        target = owner(step)

        @pl.when((target >= place) & (place > 0))
        def _():
            line_copy(step, kind, True).wait_recv()
            slot = target + 1
            own[kind][step, group] = add(own[kind][step, group], line[kind][slot])

        @pl.when((target <= place) & (place < shards - 1))
        def _():
            line_copy(step, kind, False).wait_recv()
            own[kind][step, group] = add(own[kind][step, group], line[kind][target])

        @pl.when(target > place)
        def _():
            line_copy(step, kind, True).start()

        @pl.when(target < place)
        def _():
            line_copy(step, kind, False).start()

        if step == shards - 1:
            outs[kind][...] = own[kind][step, group].astype(F32)

    lag = kinds
    for at in range(len(units) + lag):
        if at < len(units):
            meet(units[at])
        if at >= lag:
            pass_on(units[at - lag])

    for step, kind in units:
        core_copy(step, kind).wait_send()
        for r in range(1, groups):
            side_copy(step, kind, r).wait_send()
        if step < shards - 1:
            target = owner(step)

            @pl.when(target > place)
            def _():
                line_copy(step, kind, True).wait_send()

            @pl.when(target < place)
            def _():
                line_copy(step, kind, False).wait_send()


def scatter_sums(parts, dp, shards):
    kinds, groups = len(parts), dp // 2
    split = [p.reshape((groups, 2) + p.shape[1:]) for p in parts]
    blocks = [p.shape[2:] for p in parts]
    scratch = []
    for lead in ((shards, groups), (shards, groups), (shards, max(groups - 1, 1)), (shards + 1,)):
        scratch += [pltpu.VMEM(lead + b, p.dtype) for p, b in zip(parts, blocks)]
    scratch += [
        pltpu.SemaphoreType.DMA((shards, kinds)),
        pltpu.SemaphoreType.DMA((2, shards, kinds)),
        pltpu.SemaphoreType.DMA((2, shards, kinds, max(groups - 1, 1))),
        pltpu.SemaphoreType.DMA((2, shards + 1, kinds)),
    ]
    return pl.pallas_call(
        partial(scatter_kernel, dp, shards, kinds),
        in_specs=[pl.BlockSpec(memory_space=pl.ANY)] * kinds,
        out_specs=[pl.BlockSpec(memory_space=pltpu.VMEM)] * kinds,
        out_shape=[jax.ShapeDtypeStruct(b, F32) for b in blocks],
        scratch_shapes=scratch,
        compiler_params=pltpu.CompilerParams(
            vmem_limit_bytes=60 * MIB, collective_id=1, has_side_effects=True
        ),
        cost_estimate=pl.CostEstimate(
            flops=0, bytes_accessed=sum(4 * p.size * p.dtype.itemsize for p in parts), transcendentals=0
        ),
        name="scatter_sums",
    )(*split)


def local(
    block_input,
    out_cotangent,
    lengths,
    qkv_weight,
    qv_bias,
    proj_weight,
    fc1_weight,
    fc1_bias,
    fc2_weight,
    gains,
    biases,
):
    section_idx = lax.axis_index("section")
    dp_count, shard_count = lax.axis_size("dp"), lax.axis_size("tensor")
    dp_idx, shard_idx = lax.axis_index("dp"), lax.axis_index("tensor")
    micro_count, _, slots, width = block_input.shape
    hidden = fc1_weight.shape[2] * shard_count
    first_section = section_idx == 0

    span = shard_count // 2
    odd, own_u = dp_idx % 2, shard_idx % span

    swap_pairs = [
        ((2 * j + a) * shard_count + b * span + u, (2 * j + b) * shard_count + a * span + u)
        for j in range(dp_count // 2)
        for a in range(2)
        for b in range(2)
        for u in range(span)
    ]
    mate_pairs = [(d, d + 1 - 2 * (d % 2)) for d in range(dp_count)]

    def turned(steps):
        return [
            (half * span + (u + steps) % span, half * span + u) for half in range(2) for u in range(span)
        ]

    def swapped(rows):
        return lax.ppermute(rows, BOTH, swap_pairs)

    def near_group(rows):
        pieces = [rows] + [lax.ppermute(rows, "tensor", turned(r)) for r in range(1, span)]
        return jnp.concatenate(pieces, axis=0)

    def with_mate(near):
        return jnp.concatenate([near, lax.ppermute(near, "dp", mate_pairs)], axis=0)

    def reduce_near(own_rows, near_rows, mate_rows):
        got = lax.ppermute(mate_rows, "dp", mate_pairs).astype(F32)
        parts = [own_rows + got[:slots]]
        for r in range(1, span):
            piece = near_rows[(r - 1) * slots : r * slots].astype(F32) + got[r * slots : (r + 1) * slots]
            parts.append(lax.ppermute(piece.astype(BF), "tensor", turned(-r)))
        return parts

    shard_of = jnp.stack([((odd + a) % 2) * span + (own_u + r) % span for a in range(2) for r in range(span)])
    slot_ids = jnp.arange(slots, dtype=jnp.int32)
    live = slot_ids[None, :] < jnp.take(lengths, shard_of)[:, None]
    own_live = live[0].astype(F32)[:, None]
    live_cols = jnp.broadcast_to(own_live, (slots, LANES))
    mask = jnp.broadcast_to(jnp.where(live.reshape(-1, 1), 0.0, NEG).astype(BF), (live.size, LANES))

    small = jnp.concatenate(
        [gains[0].reshape(-1), biases[0].reshape(-1), qv_bias[0].reshape(-1), fc1_bias[0].reshape(-1)]
    )
    rows_dp, rows_shard = width // dp_count, width // shard_count

    def whole(part):
        return lax.all_gather(part, BOTH, axis=0, tiled=False).reshape(
            (dp_count, shard_count) + part.shape
        )

    qkv_rows = qkv_weight[0].transpose(1, 0, 2).reshape(-1, rows_dp)
    w_attn = whole(jnp.concatenate([qkv_rows, proj_weight[0], small.reshape(-1, rows_dp)], axis=0))
    up_rows = fc1_weight[0].reshape(rows_dp, -1, rows_dp).transpose(1, 0, 2).reshape(-1, rows_dp)
    w_mlp = whole(jnp.concatenate([up_rows, fc2_weight[0]], axis=0))
    small = w_attn[:, :, 4 * rows_dp :].reshape(dp_count * shard_count, -1)
    own = width // (dp_count * shard_count)
    vectors = small[:, : 8 * own].reshape(-1, 8, own).transpose(1, 0, 2).reshape(8, width).astype(F32)
    shared = small[:shard_count, 8 * own :]
    cut = 2 * rows_shard
    qv_rows = shared[:, :cut].reshape(shard_count, 2, -1).transpose(1, 0, 2).reshape(2, width).astype(F32)
    up_bias = shared[:, cut:].reshape(1, hidden).astype(F32)

    def after(value, *others):
        return lax.optimization_barrier((value,) + others)[0]

    def forward_attend(rows, rows_all):
        h_one = layer_norm(rows.astype(F32), vectors[0], vectors[4]).astype(BF)
        h_all = layer_norm(rows_all.astype(F32), vectors[0], vectors[4]).astype(BF)
        return (h_one, h_all) + tuple(attend(h_one, h_all, w_attn, qv_rows, mask))

    def forward_mlp(rows, attended):
        return mlp(attended[5], rows, w_attn, vectors, live_cols, up_bias, w_mlp)

    def backward(cotangent, attended, risen):
        h_one, h_all, queries, key_rows, values, context, lse = attended
        attn_out, mid_rows, h_two, act, slope, mlp_out, _ = risen
        d_mlp, d_pre, d_mid, d_attn, row_sums, d_up_bias = mlp_back(
            cotangent, live_cols, vectors, mlp_out, mid_rows, attn_out, slope, w_mlp
        )
        d_q, d_k, d_v, d_qv, own_part, near, mate = attend_back(
            d_attn, w_attn, queries, key_rows, values, context, lse, mask
        )
        operands = ((act, d_mlp), (h_two, d_pre), (h_one, h_all, d_q, d_k, d_v, context, d_attn))
        return (d_mid, own_part, near, mate), (row_sums, d_qv, d_up_bias), operands

    def finish(rows, d_mid, parts, sums):
        d_h_one = sum(p.astype(F32) for p in parts)
        d_rows_ln, d_gain, d_shift = layer_norm_back(rows.astype(F32), vectors[0], d_h_one)
        row_sums, d_qv, d_up_bias = sums
        none = jnp.zeros((3, width), F32)
        row_sums = row_sums + jnp.concatenate([d_gain, none, d_shift, none], axis=0)
        return (d_mid + d_rows_ln).astype(BF), (row_sums, d_qv, d_up_bias)

    tokens = [swapped(block_input[m, 0]) for m in range(micro_count)]
    tokens_all = [with_mate(near_group(rows)) for rows in tokens]
    start_attended = [forward_attend(rows, every) for rows, every in zip(tokens, tokens_all)]
    start_risen = [None] * micro_count
    start_risen[0] = forward_mlp(tokens[0], start_attended[0])
    received = [lax.ppermute(start_risen[0][6], "section", [(0, 1)])]
    late_cot, _ = lax.optimization_barrier((out_cotangent, start_risen[0][6]))
    cotangents = [swapped(late_cot[m, 0]) for m in range(micro_count)]
    beside = received[0]
    for m in range(1, micro_count):
        start_risen[m] = forward_mlp(tokens[m], start_attended[m])
        received.append(lax.ppermute(start_risen[m][6], "section", [(0, 1)]))
        if m == 1:
            rows = jnp.where(first_section, tokens[0], after(received[0], start_risen[1][6]))
            near_rows = near_group(rows)
    near_rows = after(near_rows, start_risen[-1][6])

    zero_rows = jnp.zeros_like(tokens[0])
    late_out, back_rows, sums, operands = [], [], [], []
    d_received, pending = zero_rows, None
    for m in range(micro_count):
        attended = forward_attend(rows, with_mate(near_rows))
        if pending is not None:
            old_rows, d_mid, parts, part_sums = pending
            parts = [parts[0]] + [after(p, attended[5]) for p in parts[1:]]
            d_low, part_sums = finish(old_rows, d_mid, parts, part_sums)
            back_rows.append(d_low)
            sums.append(part_sums)
            d_received = lax.ppermute(d_low, "section", [(1, 0)])
        risen = forward_mlp(rows, attended)
        late_out.append(risen[6])
        if pending is not None:
            d_received = after(d_received, risen[6])
        cotangent = jnp.where(first_section, d_received, cotangents[m])
        if m + 1 < micro_count:
            next_rows = jnp.where(first_section, tokens[m], received[m + 1])
            near_rows = near_group(next_rows)
        (d_mid, own_part, near, mate), part_sums, pieces = backward(cotangent, attended, risen)
        operands.append(pieces)
        if m + 1 < micro_count:
            near_rows = after(near_rows, mate)
        pending = (rows, d_mid, reduce_near(own_part, near, mate), part_sums)
        rows = next_rows
    d_low, part_sums = finish(*pending)
    back_rows.append(d_low)
    sums.append(part_sums)
    d_received = lax.ppermute(d_low, "section", [(1, 0)])
    (d_mid, own_part, near, mate), part_sums, pieces = backward(
        jnp.where(first_section, d_received, zero_rows), start_attended[-1], start_risen[-1]
    )
    operands.append(pieces)
    d_low, part_sums = finish(tokens[-1], d_mid, reduce_near(own_part, near, mate), part_sums)
    back_rows.append(d_low)
    sums.append(part_sums)

    def weight_grads(steps):
        return (
            down_grad([step[0] for step in steps], dp_count, shard_count),
            up_grad([step[1] for step in steps], dp_count, shard_count),
            attn_grad([step[2] for step in steps], dp_count, shard_count),
        )

    grads = lax.cond(
        first_section, lambda steps: weight_grads(steps[1:]), lambda steps: weight_grads(steps[:-1]), operands
    )
    row_sums, d_qv, d_up_bias = (sum(step[n] for step in sums) for n in range(3))
    whole_grid = (dp_count, shard_count)
    small_sums = jnp.concatenate(
        [
            row_sums.reshape((8,) + whole_grid + (own,)).transpose(1, 2, 0, 3).reshape(whole_grid + (-1,)),
            jnp.broadcast_to(
                d_qv.reshape(2, shard_count, rows_dp).transpose(1, 0, 2).reshape(1, shard_count, -1),
                whole_grid + (2 * rows_dp,),
            ),
            jnp.broadcast_to(d_up_bias.reshape(1, shard_count, -1), whole_grid + (hidden // shard_count,)),
        ],
        axis=2,
    ).reshape(whole_grid + (-1, rows_dp))
    d_down, d_up, d_attn, small_total = scatter_sums(list(grads) + [small_sums], dp_count, shard_count)
    d_qkv = d_attn[: 3 * rows_dp].reshape(3, rows_dp, rows_dp).transpose(1, 0, 2)
    d_proj = d_attn[3 * rows_dp :]
    small_total = small_total.reshape(-1)
    gain_grad = small_total[: 4 * own].reshape(4, own)
    bias_grad = small_total[4 * own : 8 * own].reshape(4, own)
    qv_grad = small_total[8 * own : 8 * own + 2 * rows_dp].reshape(2, rows_dp)
    up_bias_grad = small_total[8 * own + 2 * rows_dp :]

    section_out = jnp.stack(
        [swapped(jnp.where(first_section, start_risen[m][6], late_out[m])) for m in range(micro_count)]
    )
    input_grad = jnp.stack(
        [swapped(jnp.where(first_section, back_rows[m + 1], back_rows[m])) for m in range(micro_count)]
    )
    return (
        section_out[None, :, None],
        input_grad[None, :, None],
        d_qkv[None],
        qv_grad[None],
        d_proj[None],
        d_up[None],
        up_bias_grad[None],
        d_down[None],
        gain_grad[None],
        bias_grad[None],
    )


def solution(mesh):
    in_specs = (
        P(None, "dp", "tensor", None),
        P(None, "dp", "tensor", None),
        P(),
        P("section", "dp", None, "tensor"),
        P("section", None, "tensor"),
        P("section", "tensor", "dp"),
        P("section", "dp", "tensor"),
        P("section", "tensor"),
        P("section", "tensor", "dp"),
        P("section", None, ("dp", "tensor")),
        P("section", None, ("dp", "tensor")),
    )
    out_specs = (
        P("section", None, "dp", "tensor", None),
        P("section", None, "dp", "tensor", None),
        P("section", "dp", None, "tensor"),
        P("section", None, "tensor"),
        P("section", "tensor", "dp"),
        P("section", "dp", "tensor"),
        P("section", "tensor"),
        P("section", "tensor", "dp"),
        P("section", None, ("dp", "tensor")),
        P("section", None, ("dp", "tensor")),
    )
    return jax.shard_map(local, mesh=mesh, in_specs=in_specs, out_specs=out_specs, check_vma=False)
```

```python
from functools import partial

import jax
import jax.numpy as jnp
from jax import lax
from jax.experimental import pallas as pl
from jax.experimental.pallas import tpu as pltpu
from jax.sharding import PartitionSpec as P

HD = 64
LANES = 128
EPS = 1e-06
NEG = -1000000000.0
F32 = jnp.float32
BF = jnp.bfloat16
BOTH = ("dp", "tensor")
MIB = 2**20


def dot_nt(a, b):
    return lax.dot_general(a, b, (((1,), (1,)), ((), ())), preferred_element_type=F32)


def dot_nn(a, b):
    return lax.dot_general(a, b, (((1,), (0,)), ((), ())), preferred_element_type=F32)


def dot_tn(a, b):
    return lax.dot_general(a, b, (((0,), (0,)), ((), ())), preferred_element_type=F32)


def normalize(rows):
    mean = jnp.mean(rows, axis=-1, keepdims=True)
    centred = rows - mean
    spread = jnp.mean(centred * centred, axis=-1, keepdims=True)
    inverse = lax.rsqrt(spread + EPS)
    return centred * inverse, inverse


def layer_norm(rows, gain, shift):
    return normalize(rows)[0] * gain + shift


def layer_norm_back(rows, gain, d_out):
    normed, inverse = normalize(rows)
    scaled = gain * d_out
    mean = jnp.mean(scaled, axis=-1, keepdims=True)
    along = jnp.mean(scaled * normed, axis=-1, keepdims=True)
    d_rows = inverse * (scaled - mean - normed * along)
    d_gain = jnp.sum(d_out * normed, axis=0, keepdims=True)
    return d_rows, d_gain, jnp.sum(d_out, axis=0, keepdims=True)


def gelu_and_slope(x):
    size = jnp.abs(x)
    t = 1.0 / (1.0 + (0.3275911 * 0.7071067811865476) * size)
    bell = jnp.exp(-0.5 * x * x)
    poly = 0.5 * 1.061405429
    for factor in (-1.453152027, 1.421413741, -0.284496736, 0.254829592):
        poly = poly * t + 0.5 * factor
    tail = poly * t * bell
    below = jnp.where(x < 0.0, tail, 1.0 - tail)
    return x * below, below + x * bell * 0.3989422804014327


def lane_ids(shape):
    return lax.broadcasted_iota(jnp.int32, shape, 1)


def staged(units, *stages):
    for at in range(len(units) + len(stages) - 1):
        for late, stage in enumerate(stages):
            if 0 <= at - late < len(units):
                stage(units[at - late])


def in_pairs(count, rise, bend, fall):
    waiting = []
    rise(0)
    for unit in range(count):
        if unit + 1 < count:
            rise(unit + 1)
        bend(unit)
        if unit % 2:
            waiting.append(unit)
        if waiting and (unit % 2 == 0 or unit + 1 == count):
            for ready in waiting:
                fall(ready)
            waiting = []


def stack_rows(blocks):
    return blocks.reshape(blocks.shape[0] * blocks.shape[1], blocks.shape[2])


def join_cols(blocks):
    return jnp.concatenate([blocks[i] for i in range(blocks.shape[0])], axis=1)


def call(kernel, grid, ins, outs, scratch, flops, name, grant=32):
    arrays, in_specs = zip(*ins)
    shapes, out_specs = zip(*outs)
    moved = sum(a.size * a.dtype.itemsize for a in arrays) + sum(s.size * s.dtype.itemsize for s in shapes)
    return pl.pallas_call(
        kernel,
        grid=(grid,),
        in_specs=list(in_specs),
        out_specs=list(out_specs),
        out_shape=list(shapes),
        scratch_shapes=scratch,
        compiler_params=pltpu.CompilerParams(vmem_limit_bytes=grant * MIB),
        cost_estimate=pl.CostEstimate(flops=flops, bytes_accessed=moved, transcendentals=0),
        name=name,
    )(*arrays)


def fixed(shape):
    return pl.BlockSpec(shape, lambda i: (0,) * len(shape))


def by_cols(rows, cols):
    return pl.BlockSpec((rows, cols), lambda i: (0, i))


def by_shard(blocks, rows=None, at=0):
    dp, _, own_rows, cols = blocks.shape
    return pl.BlockSpec((dp, 1, rows or own_rows, cols), lambda i: (0, i, at, 0))


def attend_kernel(
    h_ref, h_all_ref, w_ref, bias_ref, mask_ref, q_ref, k_ref, v_ref, o_ref, lse_ref
):
    part = q_ref.shape[1]
    w_q, w_k, w_v = (stack_rows(w_ref[:, 0, n * part : (n + 1) * part]) for n in range(3))
    q_ref[...] = (dot_nn(h_ref[...], w_q) + bias_ref[0:1]).astype(BF)
    k_ref[...] = dot_nn(h_all_ref[...], w_k).astype(BF)
    v_ref[...] = (dot_nn(h_all_ref[...], w_v) + bias_ref[1:2]).astype(BF)
    mask = mask_ref[...]
    k_lane, q_lane = lane_ids((k_ref.shape[0], LANES)), lane_ids((q_ref.shape[0], LANES))
    units = [(pair, half) for pair in range(part // LANES) for half in range(2)]
    scores, probs, done = {}, {}, {}

    def cols(pair):
        return slice(pair * LANES, (pair + 1) * LANES)

    def score(unit):
        pair, half = unit
        spare = HD * (1 - half)
        low_q = (q_ref[:, cols(pair)].astype(F32) * HD**-0.5).astype(BF)
        q_one = jnp.where(q_lane == spare, 1.0, 0.0).astype(BF)
        k_bias = jnp.where(k_lane == spare, mask, 0.0).astype(BF)
        q_own = jnp.where((q_lane // HD) == half, low_q, q_one)
        k_own = jnp.where((k_lane // HD) == half, k_ref[:, cols(pair)], k_bias)
        scores[unit] = dot_nt(q_own, k_own)

    def soften(unit):
        rows = scores.pop(unit)
        top = jnp.max(rows, axis=1, keepdims=True)
        probs[unit] = (jnp.exp(rows - top).astype(BF), top)

    def mix(unit):
        pair, half = unit
        spare = HD * (1 - half)
        prob, top = probs.pop(unit)
        v_one = jnp.where(k_lane == spare, 1.0, 0.0).astype(BF)
        v_own = jnp.where((k_lane // HD) == half, v_ref[:, cols(pair)], v_one)
        out = dot_nn(prob, v_own)
        total = out[:, spare : spare + 1]
        done[unit] = (out * (1.0 / total), top + jnp.log(total))
        if half == 1:
            first, second = done.pop((pair, 0)), done.pop(unit)
            o_ref[:, cols(pair)] = jnp.where(q_lane < HD, first[0], second[0]).astype(BF)
            lse_ref[:, cols(pair)] = jnp.where(q_lane < HD, first[1], second[1])

    staged(units, score, soften, mix)


def attend(h_one, h_all, w_attn, qv_rows, mask):
    slots, width = h_one.shape
    keys = h_all.shape[0]
    part = w_attn.shape[3]
    own, every = by_cols(slots, part), by_cols(keys, part)
    row = jax.ShapeDtypeStruct((slots, width), BF)
    col = jax.ShapeDtypeStruct((keys, width), BF)
    return call(
        attend_kernel,
        w_attn.shape[1],
        [
            (h_one, fixed(h_one.shape)),
            (h_all, fixed(h_all.shape)),
            (w_attn, by_shard(w_attn, 3 * part)),
            (qv_rows, by_cols(2, part)),
            (mask, fixed(mask.shape)),
        ],
        [(row, own), (col, every), (col, every), (row, own), (jax.ShapeDtypeStruct(row.shape, F32), own)],
        [],
        width * (2 * width * (slots + 2 * keys) + 16 * slots * keys),
        "attend",
    )


def split_three(value):
    first = value.astype(BF)
    rest = value - first.astype(F32)
    second = rest.astype(BF)
    return first, second, (rest - second.astype(F32)).astype(BF)


def attend_back_kernel(
    d_attn_ref, w_proj_ref, w_ref, q_ref, k_ref, v_ref, ctx_ref, lse_ref, mask_ref,
    dq_ref, dk_ref, dv_ref, sums_ref, own_ref, near_ref, mate_ref,
    do_ref, acc_q, acc_k,
):
    slots, part = q_ref.shape
    do_ref[...] = dot_nt(d_attn_ref[...], join_cols(w_proj_ref[:, 0])).astype(BF)
    mask = mask_ref[...]
    q_lane, k_lane = lane_ids((slots, LANES)), lane_ids((k_ref.shape[0], LANES))
    units = [(pair, half) for pair in range(part // LANES) for half in range(2)]
    first_part, done = {}, {}

    def cols(pair):
        return slice(pair * LANES, (pair + 1) * LANES)

    def low_queries(pair):
        return (q_ref[:, cols(pair)].astype(F32) * HD**-0.5).astype(BF)

    def score(unit):
        pair, half = unit
        at = cols(pair)
        spare = HD * (1 - half)
        d_out, lse = do_ref[:, at], lse_ref[:, at]
        q_own, k_own = (q_lane // HD) == half, (k_lane // HD) == half
        zero_q, one_q = jnp.zeros(q_lane.shape, BF), jnp.ones(q_lane.shape, BF)
        l_one, l_two, l_three = split_three(-lse[:, HD * half : HD * half + 1])
        product = d_out.astype(F32) * ctx_ref[:, at].astype(F32)
        inner = jnp.sum(jnp.where(q_own, product, 0.0), axis=1, keepdims=True)
        i_one, i_two, _ = split_three(-inner)
        q_more = jnp.where(q_lane == spare + 2, l_two, jnp.where(q_lane == spare + 3, l_three, zero_q))
        q_more = jnp.where(q_lane == spare, one_q, jnp.where(q_lane == spare + 1, l_one, q_more))
        k_more = jnp.where((k_lane > spare) & (k_lane < spare + 4), 1.0, 0.0).astype(BF)
        k_more = jnp.where(k_lane == spare, mask, k_more)
        o_more = jnp.where(q_lane == spare, i_one, jnp.where(q_lane == spare + 1, i_two, zero_q))
        v_more = jnp.where((k_lane >= spare) & (k_lane < spare + 2), 1.0, 0.0).astype(BF)
        score = dot_nt(jnp.where(q_own, low_queries(pair), q_more), jnp.where(k_own, k_ref[:, at], k_more))
        d_prob = dot_nt(jnp.where(q_own, d_out, o_more), jnp.where(k_own, v_ref[:, at], v_more))
        prob = jnp.exp(score)
        first_part[unit] = (prob.astype(BF), (prob * d_prob).astype(BF))

    def mix(unit):
        pair, half = unit
        at = cols(pair)
        prob, d_score = first_part.pop(unit)
        done[unit] = (
            dot_nn(d_score, k_ref[:, at]) * HD**-0.5,
            dot_tn(d_score, low_queries(pair)),
            dot_tn(prob, do_ref[:, at]),
        )
        if half == 1:
            one, two = done.pop((pair, 0)), done.pop(unit)
            d_q = jnp.where(q_lane < HD, one[0], two[0]).astype(BF)
            d_k = jnp.where(k_lane < HD, one[1], two[1]).astype(BF)
            d_v = jnp.where(k_lane < HD, one[2], two[2]).astype(BF)
            dq_ref[:, at], dk_ref[:, at], dv_ref[:, at] = d_q, d_k, d_v
            sums_ref[0:1, at] = jnp.sum(d_q.astype(F32), axis=0, keepdims=True)
            sums_ref[1:2, at] = jnp.sum(d_v.astype(F32), axis=0, keepdims=True)

    staged(units, score, mix)
    w_q, w_k, w_v = (stack_rows(w_ref[:, 0, n * part : (n + 1) * part]) for n in range(3))
    from_q = dot_nt(dq_ref[...], w_q)
    from_k = dot_nt(
        jnp.concatenate([dk_ref[...], dv_ref[...]], axis=1), jnp.concatenate([w_k, w_v], axis=1)
    )

    @pl.when(pl.program_id(0) == 0)
    def _():
        acc_q[...] = from_q
        acc_k[...] = from_k

    @pl.when(pl.program_id(0) > 0)
    def _():
        acc_q[...] += from_q
        acc_k[...] += from_k

    @pl.when(pl.program_id(0) == pl.num_programs(0) - 1)
    def _():
        near = near_ref.shape[0]
        own_ref[...] = acc_q[...] + acc_k[0:slots]
        near_ref[...] = acc_k[slots : slots + near].astype(BF)
        mate_ref[...] = acc_k[slots + near :].astype(BF)


def attend_back(d_attn, w_attn, queries, key_rows, values, context, lse, mask):
    slots, width = queries.shape
    keys = key_rows.shape[0]
    part = w_attn.shape[3]
    own, every = by_cols(slots, part), by_cols(keys, part)
    row = jax.ShapeDtypeStruct((slots, width), BF)
    col = jax.ShapeDtypeStruct((keys, width), BF)
    near = jax.ShapeDtypeStruct((keys // 2 - slots, width), BF)
    mate = jax.ShapeDtypeStruct((keys // 2, width), BF)
    return call(
        attend_back_kernel,
        w_attn.shape[1],
        [
            (d_attn, fixed(d_attn.shape)),
            (w_attn, by_shard(w_attn, part, 3)),
            (w_attn, by_shard(w_attn, 3 * part)),
            (queries, own),
            (key_rows, every),
            (values, every),
            (context, own),
            (lse, own),
            (mask, fixed(mask.shape)),
        ],
        [
            (row, own),
            (col, every),
            (col, every),
            (jax.ShapeDtypeStruct((2, width), F32), by_cols(2, part)),
            (jax.ShapeDtypeStruct((slots, width), F32), fixed((slots, width))),
            (near, fixed(near.shape)),
            (mate, fixed(mate.shape)),
        ],
        [pltpu.VMEM((slots, part), BF), pltpu.VMEM((slots, width), F32), pltpu.VMEM((keys, width), F32)],
        width * (2 * width * (2 * slots + 2 * keys) + 40 * slots * keys),
        "attend_back",
    )


def mlp_kernel(
    ctx_ref, rows_ref, w_proj_ref, vec_ref, live_ref, bias_ref, w_up_ref, w_down_ref,
    attn_ref, mid_ref, h_ref, act_ref, slope_ref, out_ref, low_ref,
):
    dp, _, part, _ = w_up_ref.shape
    step = pl.program_id(0)

    @pl.when(step == 0)
    def _():
        context = ctx_ref[...]
        sides = [dot_nn(context, stack_rows(w_proj_ref[i])) for i in range(dp)]
        attn_out = jnp.concatenate(sides, axis=1) + vec_ref[5:6]
        attn_ref[...] = attn_out
        mid = rows_ref[...].astype(F32) + vec_ref[1:2] * attn_out
        mid_ref[...] = mid
        h_ref[...] = layer_norm(mid, vec_ref[2:3], vec_ref[6:7]).astype(BF)
        out_ref[...] = jnp.zeros_like(out_ref)

    h = h_ref[...]
    piece = w_up_ref.shape[3]
    pre, act = {}, {}

    def rise(unit):
        at = slice(unit * piece, (unit + 1) * piece)
        pre[unit] = dot_nn(h, stack_rows(w_up_ref[:, 0, at])) + bias_ref[:, at]

    def bend(unit):
        at = slice(unit * piece, (unit + 1) * piece)
        value, slope = gelu_and_slope(pre.pop(unit))
        act[unit] = value.astype(BF)
        act_ref[:, at] = act[unit]
        slope_ref[:, at] = slope.astype(BF)

    def fall(unit):
        at = slice((unit - 1) * piece, (unit + 1) * piece)
        both = jnp.concatenate([act.pop(unit - 1), act.pop(unit)], axis=1)
        out_ref[...] += dot_nn(both, join_cols(w_down_ref[:, 0, at]))

    in_pairs(part // piece, rise, bend, fall)

    @pl.when(step == pl.num_programs(0) - 1)
    def _():
        mlp_out = out_ref[...] + vec_ref[7:8]
        out_ref[...] = mlp_out
        low_ref[...] = (live_ref[:, 0:1] * (mid_ref[...] + vec_ref[3:4] * mlp_out)).astype(BF)


def mlp(context, rows, w_attn, vectors, live, up_bias, w_mlp):
    slots, width = rows.shape
    dp, shards, part, lanes = w_mlp.shape
    part = part // 2
    hidden = part * shards
    full = fixed((slots, width))
    wide = jax.ShapeDtypeStruct((slots, width), F32)
    low = jax.ShapeDtypeStruct((slots, width), BF)
    tall = jax.ShapeDtypeStruct((slots, hidden), BF)
    return call(
        mlp_kernel,
        shards,
        [
            (context, full),
            (rows, full),
            (w_attn, pl.BlockSpec((dp, shards, lanes, lanes), lambda i: (0, 0, 3, 0))),
            (vectors, fixed(vectors.shape)),
            (live, fixed(live.shape)),
            (up_bias, by_cols(1, part)),
            (w_mlp, by_shard(w_mlp, part)),
            (w_mlp, by_shard(w_mlp, part, 1)),
        ],
        [
            (wide, full),
            (wide, full),
            (low, full),
            (tall, by_cols(slots, part)),
            (tall, by_cols(slots, part)),
            (wide, full),
            (low, full),
        ],
        [],
        2 * slots * width * (width + 2 * hidden),
        "mlp",
    )


def mlp_back_kernel(
    cot_ref, live_ref, vec_ref, out_ref, mid_ref, attn_ref, slope_ref, w_up_ref, w_down_ref,
    d_mlp_ref, d_pre_ref, d_mid_ref, d_attn_ref, sums_ref, up_sum_ref,
    acc,
):
    part = slope_ref.shape[1]
    step = pl.program_id(0)

    @pl.when(step == 0)
    def _():
        d_res = live_ref[:, 0:1] * cot_ref[...].astype(F32)
        d_mlp = vec_ref[3:4] * d_res
        sums_ref[3:4] = jnp.sum(d_res * out_ref[...], axis=0, keepdims=True)
        sums_ref[7:8] = jnp.sum(d_mlp, axis=0, keepdims=True)
        d_mlp_ref[...] = d_mlp.astype(BF)
        acc[...] = jnp.zeros_like(acc)

    d_mlp = d_mlp_ref[...]
    piece = w_up_ref.shape[3]
    d_act, d_pre = {}, {}

    def rise(unit):
        at = slice(unit * piece, (unit + 1) * piece)
        d_act[unit] = dot_nt(d_mlp, join_cols(w_down_ref[:, 0, at]))

    def bend(unit):
        at = slice(unit * piece, (unit + 1) * piece)
        d_pre[unit] = (d_act.pop(unit) * slope_ref[:, at].astype(F32)).astype(BF)
        d_pre_ref[:, at] = d_pre[unit]
        up_sum_ref[:, at] = jnp.sum(d_pre[unit].astype(F32), axis=0, keepdims=True)

    def fall(unit):
        both = jnp.concatenate([d_pre.pop(unit - 1), d_pre.pop(unit)], axis=1)
        w_up = [stack_rows(w_up_ref[:, 0, u * piece : (u + 1) * piece]) for u in (unit - 1, unit)]
        acc[...] += dot_nt(both, jnp.concatenate(w_up, axis=1))

    in_pairs(part // piece, rise, bend, fall)

    @pl.when(step == pl.num_programs(0) - 1)
    def _():
        d_mid_ln, d_gain, d_shift = layer_norm_back(mid_ref[...], vec_ref[2:3], acc[...])
        d_mid = live_ref[:, 0:1] * cot_ref[...].astype(F32) + d_mid_ln
        d_attn = vec_ref[1:2] * d_mid
        d_mid_ref[...] = d_mid
        d_attn_ref[...] = d_attn.astype(BF)
        sums_ref[2:3] = d_gain
        sums_ref[6:7] = d_shift
        sums_ref[1:2] = jnp.sum(d_mid * attn_ref[...], axis=0, keepdims=True)
        sums_ref[5:6] = jnp.sum(d_attn, axis=0, keepdims=True)
        sums_ref[0:1] = jnp.zeros_like(d_gain)
        sums_ref[4:5] = jnp.zeros_like(d_gain)


def mlp_back(cotangent, live, vectors, mlp_out, mid_rows, attn_out, slope, w_mlp):
    slots, width = cotangent.shape
    part, shards = w_mlp.shape[2] // 2, w_mlp.shape[1]
    hidden = part * shards
    full = fixed((slots, width))
    low = jax.ShapeDtypeStruct((slots, width), BF)
    return call(
        mlp_back_kernel,
        shards,
        [
            (cotangent, full),
            (live, fixed(live.shape)),
            (vectors, fixed(vectors.shape)),
            (mlp_out, full),
            (mid_rows, full),
            (attn_out, full),
            (slope, by_cols(slots, part)),
            (w_mlp, by_shard(w_mlp, part)),
            (w_mlp, by_shard(w_mlp, part, 1)),
        ],
        [
            (low, full),
            (jax.ShapeDtypeStruct((slots, hidden), BF), by_cols(slots, part)),
            (jax.ShapeDtypeStruct((slots, width), F32), full),
            (low, full),
            (jax.ShapeDtypeStruct((8, width), F32), fixed((8, width))),
            (jax.ShapeDtypeStruct((1, hidden), F32), by_cols(1, part)),
        ],
        [pltpu.VMEM((slots, width), F32)],
        4 * slots * width * hidden,
        "mlp_back",
    )


def summed(refs, steps, stride, left, right):
    return sum(dot_tn(refs[stride * s + left][...], refs[stride * s + right][...]) for s in range(steps))


def put(out_ref, base, i, at, value):
    if base:
        value = value + base[0][i, 0, at]
    out_ref[i, 0, at] = value.astype(out_ref.dtype)


def down_grad_kernel(steps, *refs):
    base, out_ref = refs[2 * steps : -1], refs[-1]
    total = summed(refs, steps, 2, 0, 1)
    cols = out_ref.shape[3]
    for i in range(out_ref.shape[0]):
        put(out_ref, base, i, slice(None), total[:, i * cols : (i + 1) * cols])


def up_grad_kernel(steps, *refs):
    base, out_ref = refs[2 * steps : -1], refs[-1]
    total = summed(refs, steps, 2, 0, 1)
    rows = out_ref.shape[2]
    for i in range(out_ref.shape[0]):
        put(out_ref, base, i, slice(None), total[i * rows : (i + 1) * rows])


def attn_grad_kernel(steps, *refs):
    base, out_ref = refs[7 * steps : -1], refs[-1]
    dp, _, _, lanes = out_ref.shape
    for n, (left, right) in enumerate(((0, 2), (1, 3), (1, 4))):
        total = summed(refs, steps, 7, left, right)
        for i in range(dp):
            put(out_ref, base, i, slice(n * lanes, (n + 1) * lanes), total[i * lanes : (i + 1) * lanes])
    total = summed(refs, steps, 7, 5, 6)
    for i in range(dp):
        put(out_ref, base, i, slice(3 * lanes, 4 * lanes), total[:, i * lanes : (i + 1) * lanes])


def grad_call(kernel, steps, shards, ins, shape, base, flops, name):
    out = jax.ShapeDtypeStruct(shape, F32 if base is None else BF)
    if base is not None:
        ins = ins + [(base, by_shard(base))]
    return call(partial(kernel, steps), shards, ins, [(out, by_shard(out))], [], flops, name, 60)[0]


def attn_grad(steps, dp, shards, base):
    ins, flops = [], 0
    lanes = steps[0][0].shape[1] // shards
    for h_one, h_all, d_q, d_k, d_v, context, d_attn in steps:
        ins += [(h_one, fixed(h_one.shape)), (h_all, fixed(h_all.shape))]
        ins += [(d, by_cols(d.shape[0], lanes)) for d in (d_q, d_k, d_v, context)]
        ins += [(d_attn, fixed(d_attn.shape))]
        flops += 4 * (h_one.size + h_all.size) * h_one.shape[1]
    shape = (dp, shards, 4 * lanes, lanes)
    return grad_call(attn_grad_kernel, len(steps), shards, ins, shape, base, flops, "attn_grad")


def down_grad(pairs, dp, shards, base):
    ins = []
    for left, right in pairs:
        ins += [(left, by_cols(left.shape[0], left.shape[1] // shards)), (right, fixed(right.shape))]
    shape = (dp, shards, pairs[0][0].shape[1] // shards, pairs[0][1].shape[1] // dp)
    flops = sum(2 * left.size * right.shape[1] for left, right in pairs)
    return grad_call(down_grad_kernel, len(pairs), shards, ins, shape, base, flops, "down_grad")


def up_grad(pairs, dp, shards, base):
    ins = []
    for left, right in pairs:
        ins += [(left, fixed(left.shape)), (right, by_cols(right.shape[0], right.shape[1] // shards))]
    shape = (dp, shards, pairs[0][0].shape[1] // dp, pairs[0][1].shape[1] // shards)
    flops = sum(2 * left.size * right.shape[1] for left, right in pairs)
    return grad_call(up_grad_kernel, len(pairs), shards, ins, shape, base, flops, "up_grad")


def gather_kernel(
    dp, shards, micro, shard_ref, rows_ref, whole_ref, every_ref,
    swap_sem, near_sem, token_sem, pass_sem, line_sem, side_sem, core_sem, local_sem,
):
    groups, span = dp // 2, shards // 2
    section, dp_idx, place = lax.axis_index("section"), lax.axis_index("dp"), lax.axis_index("tensor")
    group, odd = dp_idx // 2, dp_idx % 2
    half, own_u = place // span, place % span
    mesh_id = pl.DeviceIdType.MESH
    mate = (section, group * 2 + 1 - odd, place)
    others = [(section, lax.rem(group + r, groups) * 2 + odd, place) for r in range(1, groups)]
    near = [(section, dp_idx, half * span + lax.rem(own_u + r, span)) for r in range(1, span)]
    swap = (section, group * 2 + half, odd * span + own_u)
    before, after = (section, dp_idx, place - 1), (section, dp_idx, place + 1)
    moves, has_before, has_after = odd != half, place > 0, place < shards - 1
    first, partner = section == 0, (1 - section, dp_idx, place)

    def remote(src, dst, sems, at, device):
        return pltpu.make_async_remote_copy(
            src_ref=src,
            dst_ref=dst,
            send_sem=sems.at[(0,) + at],
            recv_sem=sems.at[(1,) + at],
            device_id=device,
            device_id_type=mesh_id,
        )

    barrier = pltpu.get_barrier_semaphore()

    def greet(device):
        pl.semaphore_signal(barrier, inc=1, device_id=device, device_id_type=mesh_id)

    for device in [mate, partner] + others + near:
        greet(device)
    pl.when(moves)(lambda: greet(swap))
    pl.when(has_before)(lambda: greet(before))
    pl.when(has_after)(lambda: greet(after))
    count = 2 + len(others) + len(near)
    for there in (moves, has_before, has_after):
        count = count + jnp.where(there, 1, 0)
    pl.semaphore_wait(barrier, count)

    def swap_copy(m):
        return remote(rows_ref.at[m], every_ref.at[m, 0], swap_sem, (m,), swap)

    def stay_copy(m):
        return pltpu.make_async_copy(rows_ref.at[m], every_ref.at[m, 0], local_sem.at[m])

    def pass_copy(m):
        return remote(every_ref.at[m, 0], every_ref.at[m, 0], pass_sem, (m,), partner)

    def near_copy(m, r, early=False):
        source = rows_ref.at[m] if early else every_ref.at[m, 0]
        return remote(source, every_ref.at[m, r], near_sem, (m, r - 1), near[span - 1 - r])

    def token_copy(m):
        return remote(
            every_ref.at[m, pl.ds(0, span)], every_ref.at[m, pl.ds(span, span)], token_sem, (m,), mate
        )

    def own_copy():
        return pltpu.make_async_copy(shard_ref, whole_ref.at[dp_idx, place], local_sem.at[micro])

    def source(t, own):
        return shard_ref if own else whole_ref.at[dp_idx, t]

    def line_copy(t, distance, ahead, own=False):
        return remote(
            source(t, own),
            whole_ref.at[dp_idx, t],
            line_sem,
            (0 if ahead else 1, distance - 1),
            after if ahead else before,
        )

    def side_copy(t, r, own=False):
        return remote(source(t, own), whole_ref.at[dp_idx, t], side_sem, (r - 1, t), others[r - 1])

    def core_copy(t, r, own=False):
        j = lax.rem(group + r, groups)
        at = whole_ref.at[j * 2 + odd, t]
        return remote(shard_ref if own else at, at, core_sem, (j, t), mate)

    stays = jnp.logical_not(moves)

    def set_out(m):
        pl.when(moves)(lambda: swap_copy(m).start())
        pl.when(stays)(lambda: stay_copy(m).start())

    def in_place(m):
        pl.when(moves)(lambda: swap_copy(m).wait_recv())
        pl.when(stays)(lambda: stay_copy(m).wait())

    def first_stage(m):
        if m:
            pass_copy(m).wait_recv()
        else:
            pl.when(moves)(lambda: swap_copy(m).wait_recv())
        for r in range(1, span):
            if m:
                near_copy(m, r).start()
            else:
                pl.when(moves)(lambda r=r: near_copy(m, r).start())
                pl.when(stays)(lambda r=r: near_copy(m, r, True).start())

    def second_stage(m, following):
        in_place(m)
        if following is not None:
            set_out(following)
        if m:
            pass_copy(m).start()

    order = [(m + 1) % micro for m in range(micro)] + [None]

    def token_stage(n):
        pl.when(first)(lambda: first_stage(n))
        pl.when(jnp.logical_not(first))(lambda: second_stage(order[n], order[n + 1]))

    pl.when(first)(lambda: set_out(0))
    pl.when(jnp.logical_not(first))(lambda: set_out(order[0]))
    own_copy().start()
    pl.when(has_after)(lambda: line_copy(place, 1, True, True).start())
    pl.when(has_before)(lambda: line_copy(place, 1, False, True).start())
    for r in range(1, groups):
        side_copy(place, r, True).start()
    core_copy(place, 0, True).start()

    def share(t):
        for r in range(1, groups):
            side_copy(t, r).start()
        core_copy(t, 0).start()

    def from_before(distance):
        t = place - distance
        line_copy(t, distance, True).wait_recv()
        if distance + 1 < shards:
            pl.when(has_after)(lambda: line_copy(t, distance + 1, True).start())
        share(t)

    def from_after(distance):
        t = place + distance
        line_copy(t, distance, False).wait_recv()
        if distance + 1 < shards:
            pl.when(has_before)(lambda: line_copy(t, distance + 1, False).start())
        share(t)

    for distance in range(1, shards):
        pl.when(place >= distance)(lambda d=distance: from_before(d))
        pl.when(place + distance < shards)(lambda d=distance: from_after(d))
        if distance <= micro:
            token_stage(distance - 1)
    for n in range(shards - 1, micro):
        token_stage(n)

    def from_side(t, r):
        j = lax.rem(group + r, groups)
        at = whole_ref.at[j * 2 + odd, t]
        remote(at, at, side_sem, (groups - 1 - r, t), others[r - 1]).wait_recv()
        core_copy(t, r).start()

    for r in range(1, groups):
        for distance in range(shards):
            pl.when(place >= distance)(lambda d=distance, r=r: from_side(place - d, r))
            if distance:
                pl.when(place + distance < shards)(lambda d=distance, r=r: from_side(place + d, r))

    @pl.when(first)
    def _():
        pl.when(stays)(lambda: stay_copy(0).wait())
        for m in range(micro):
            for r in range(1, span):
                near_copy(m, r).wait_recv()
            token_copy(m).start()

    own_copy().wait()

    @pl.when(first)
    def _():
        pl.when(moves)(lambda: swap_copy(0).wait_send())
        for m in range(micro):
            token_copy(m).wait()
            for r in range(1, span):
                near_copy(m, r).wait_send()

    @pl.when(jnp.logical_not(first))
    def _():
        for m in range(micro):
            pl.when(moves)(lambda m=m: swap_copy(m).wait_send())
            if m:
                pass_copy(m).wait_send()

    for t in range(shards):
        for r in range(1, groups):
            side_copy(t, r).wait_send()
        for r in range(groups):
            core_copy(t, r).wait()
    for distance in range(1, shards):
        if distance > 1:
            pl.when(has_after & (place >= distance - 1))(
                lambda d=distance: line_copy(place - d + 1, d, True).wait_send()
            )
            pl.when(has_before & (place + distance - 1 < shards))(
                lambda d=distance: line_copy(place + d - 1, d, False).wait_send()
            )
        else:
            pl.when(has_after)(lambda: line_copy(place, 1, True).wait_send())
            pl.when(has_before)(lambda: line_copy(place, 1, False).wait_send())


def gather_first(shard, rows, dp, shards):
    micro, slots, width = rows.shape
    groups, span = dp // 2, shards // 2
    dma = pltpu.SemaphoreType.DMA
    return pl.pallas_call(
        partial(gather_kernel, dp, shards, micro),
        in_specs=[pl.BlockSpec(memory_space=pl.ANY)] * 2,
        out_specs=[pl.BlockSpec(memory_space=pl.ANY)] * 2,
        out_shape=[
            jax.ShapeDtypeStruct((dp, shards) + shard.shape, BF),
            jax.ShapeDtypeStruct((micro, 2 * span, slots, width), BF),
        ],
        scratch_shapes=[
            dma((2, micro)),
            dma((2, micro, max(span - 1, 1))),
            dma((2, micro)),
            dma((2, micro)),
            dma((2, 2, max(shards - 1, 1))),
            dma((2, max(groups - 1, 1), shards)),
            dma((2, groups, shards)),
            dma((micro + 1,)),
        ],
        compiler_params=pltpu.CompilerParams(collective_id=2, has_side_effects=True),
        cost_estimate=pl.CostEstimate(
            flops=0, bytes_accessed=2 * dp * shards * shard.size * 2, transcendentals=0
        ),
        name="gather_first",
    )(shard, rows)


def shed_order(count, place):
    return sorted(range(count), key=lambda t: (-abs(t - place), -t))


def scatter_kernel(dp, shards, kinds, *refs):
    parts, outs = refs[:kinds], refs[kinds : 2 * kinds]
    own, got, side, line = (refs[(2 + n) * kinds : (3 + n) * kinds] for n in range(4))
    load_sem, core_sem, side_sem, line_sem = refs[6 * kinds :]
    groups = dp // 2
    section, dp_idx, place = lax.axis_index("section"), lax.axis_index("dp"), lax.axis_index("tensor")
    group, odd = dp_idx // 2, dp_idx % 2
    mate = (section, group * 2 + 1 - odd, place)
    others = [(section, lax.rem(group + r, groups) * 2 + odd, place) for r in range(1, groups)]
    before, after = (section, dp_idx, place - 1), (section, dp_idx, place + 1)
    mesh_id = pl.DeviceIdType.MESH
    tables = [shed_order(shards, z) for z in range(shards)]

    def owner(step):
        return sum(jnp.where(place == z, tables[z][step], 0) for z in range(shards))

    barrier = pltpu.get_barrier_semaphore()
    for device in [mate] + others:
        pl.semaphore_signal(barrier, inc=1, device_id=device, device_id_type=mesh_id)

    @pl.when(place > 0)
    def _():
        pl.semaphore_signal(barrier, inc=1, device_id=before, device_id_type=mesh_id)

    @pl.when(place < shards - 1)
    def _():
        pl.semaphore_signal(barrier, inc=1, device_id=after, device_id_type=mesh_id)

    ends = jnp.where(place == 0, 1, 0) + jnp.where(place == shards - 1, 1, 0)
    pl.semaphore_wait(barrier, groups + 2 - ends)

    def core_copy(step, kind):
        return pltpu.make_async_remote_copy(
            src_ref=parts[kind].at[:, 1 - odd, owner(step)],
            dst_ref=got[kind].at[step],
            send_sem=core_sem.at[0, step, kind],
            recv_sem=core_sem.at[1, step, kind],
            device_id=mate,
            device_id_type=mesh_id,
        )

    def load(step, kind):
        return pltpu.make_async_copy(
            parts[kind].at[:, odd, owner(step)], own[kind].at[step], load_sem.at[step, kind]
        )

    def side_copy(step, kind, r):
        return pltpu.make_async_remote_copy(
            src_ref=own[kind].at[step, lax.rem(group + r, groups)],
            dst_ref=side[kind].at[step, r - 1],
            send_sem=side_sem.at[0, step, kind, r - 1],
            recv_sem=side_sem.at[1, step, kind, r - 1],
            device_id=others[r - 1],
            device_id_type=mesh_id,
        )

    def line_copy(step, kind, ahead):
        target = owner(step)
        slot = target + 1 if ahead else target
        return pltpu.make_async_remote_copy(
            src_ref=own[kind].at[step, group],
            dst_ref=line[kind].at[slot],
            send_sem=line_sem.at[0, slot, kind],
            recv_sem=line_sem.at[1, slot, kind],
            device_id=after if ahead else before,
            device_id_type=mesh_id,
        )

    def add(one, two):
        return (one.astype(F32) + two.astype(F32)).astype(one.dtype)

    units = [(step, kind) for step in range(shards) for kind in range(kinds)]
    for step, kind in units:
        core_copy(step, kind).start()
        load(step, kind).start()

    def meet(unit):
        step, kind = unit
        load(step, kind).wait()
        core_copy(step, kind).wait_recv()
        for r in range(1, groups):
            at = lax.rem(group + r, groups)
            own[kind][step, at] = add(own[kind][step, at], got[kind][step, at])
            side_copy(step, kind, r).start()
        own[kind][step, group] = add(own[kind][step, group], got[kind][step, group])

    def pass_on(unit):
        step, kind = unit
        mine = own[kind][step, group].astype(F32)
        for r in range(1, groups):
            side_copy(step, kind, r).wait_recv()
            mine = mine + side[kind][step, r - 1].astype(F32)
        own[kind][step, group] = mine.astype(own[kind].dtype)
        target = owner(step)

        @pl.when((target >= place) & (place > 0))
        def _():
            line_copy(step, kind, True).wait_recv()
            slot = target + 1
            own[kind][step, group] = add(own[kind][step, group], line[kind][slot])

        @pl.when((target <= place) & (place < shards - 1))
        def _():
            line_copy(step, kind, False).wait_recv()
            own[kind][step, group] = add(own[kind][step, group], line[kind][target])

        @pl.when(target > place)
        def _():
            line_copy(step, kind, True).start()

        @pl.when(target < place)
        def _():
            line_copy(step, kind, False).start()

        if step == shards - 1:
            outs[kind][...] = own[kind][step, group].astype(F32)

    lag = kinds
    for at in range(len(units) + lag):
        if at < len(units):
            meet(units[at])
        if at >= lag:
            pass_on(units[at - lag])

    for step, kind in units:
        core_copy(step, kind).wait_send()
        for r in range(1, groups):
            side_copy(step, kind, r).wait_send()
        if step < shards - 1:
            target = owner(step)

            @pl.when(target > place)
            def _():
                line_copy(step, kind, True).wait_send()

            @pl.when(target < place)
            def _():
                line_copy(step, kind, False).wait_send()


def scatter_sums(parts, dp, shards):
    kinds, groups = len(parts), dp // 2
    split = [p.reshape((groups, 2) + p.shape[1:]) for p in parts]
    blocks = [p.shape[2:] for p in parts]
    scratch = []
    for lead in ((shards, groups), (shards, groups), (shards, max(groups - 1, 1)), (shards + 1,)):
        scratch += [pltpu.VMEM(lead + b, p.dtype) for p, b in zip(parts, blocks)]
    scratch += [
        pltpu.SemaphoreType.DMA((shards, kinds)),
        pltpu.SemaphoreType.DMA((2, shards, kinds)),
        pltpu.SemaphoreType.DMA((2, shards, kinds, max(groups - 1, 1))),
        pltpu.SemaphoreType.DMA((2, shards + 1, kinds)),
    ]
    return pl.pallas_call(
        partial(scatter_kernel, dp, shards, kinds),
        in_specs=[pl.BlockSpec(memory_space=pl.ANY)] * kinds,
        out_specs=[pl.BlockSpec(memory_space=pltpu.VMEM)] * kinds,
        out_shape=[jax.ShapeDtypeStruct(b, F32) for b in blocks],
        scratch_shapes=scratch,
        compiler_params=pltpu.CompilerParams(
            vmem_limit_bytes=60 * MIB, collective_id=1, has_side_effects=True
        ),
        cost_estimate=pl.CostEstimate(
            flops=0, bytes_accessed=sum(4 * p.size * p.dtype.itemsize for p in parts), transcendentals=0
        ),
        name="scatter_sums",
    )(*split)


def local(
    block_input,
    out_cotangent,
    lengths,
    qkv_weight,
    qv_bias,
    proj_weight,
    fc1_weight,
    fc1_bias,
    fc2_weight,
    gains,
    biases,
):
    section_idx = lax.axis_index("section")
    dp_count, shard_count = lax.axis_size("dp"), lax.axis_size("tensor")
    dp_idx, shard_idx = lax.axis_index("dp"), lax.axis_index("tensor")
    micro_count, _, slots, width = block_input.shape
    hidden = fc1_weight.shape[2] * shard_count
    first_section = section_idx == 0

    span = shard_count // 2
    odd, own_u = dp_idx % 2, shard_idx % span

    swap_pairs = [
        ((2 * j + a) * shard_count + b * span + u, (2 * j + b) * shard_count + a * span + u)
        for j in range(dp_count // 2)
        for a in range(2)
        for b in range(2)
        for u in range(span)
    ]
    mate_pairs = [(d, d + 1 - 2 * (d % 2)) for d in range(dp_count)]

    def turned(steps):
        return [
            (half * span + (u + steps) % span, half * span + u) for half in range(2) for u in range(span)
        ]

    def swapped(rows):
        return lax.ppermute(rows, BOTH, swap_pairs)

    def near_group(rows):
        pieces = [rows] + [lax.ppermute(rows, "tensor", turned(r)) for r in range(1, span)]
        return jnp.concatenate(pieces, axis=0)

    def with_mate(near):
        return jnp.concatenate([near, lax.ppermute(near, "dp", mate_pairs)], axis=0)

    def reduce_near(own_rows, near_rows, mate_rows):
        got = lax.ppermute(mate_rows, "dp", mate_pairs).astype(F32)
        parts = [own_rows + got[:slots]]
        for r in range(1, span):
            piece = near_rows[(r - 1) * slots : r * slots].astype(F32) + got[r * slots : (r + 1) * slots]
            parts.append(lax.ppermute(piece.astype(BF), "tensor", turned(-r)))
        return parts

    shard_of = jnp.stack([((odd + a) % 2) * span + (own_u + r) % span for a in range(2) for r in range(span)])
    slot_ids = jnp.arange(slots, dtype=jnp.int32)
    live = slot_ids[None, :] < jnp.take(lengths, shard_of)[:, None]
    own_live = live[0].astype(F32)[:, None]
    live_cols = jnp.broadcast_to(own_live, (slots, LANES))
    mask = jnp.broadcast_to(jnp.where(live.reshape(-1, 1), 0.0, NEG).astype(BF), (live.size, LANES))

    small = jnp.concatenate(
        [gains[0].reshape(-1), biases[0].reshape(-1), qv_bias[0].reshape(-1), fc1_bias[0].reshape(-1)]
    )
    rows_dp, rows_shard = width // dp_count, width // shard_count

    def whole(part):
        return lax.all_gather(part, BOTH, axis=0, tiled=False).reshape(
            (dp_count, shard_count) + part.shape
        )

    qkv_rows = qkv_weight[0].transpose(1, 0, 2).reshape(-1, rows_dp)
    shard = jnp.concatenate([qkv_rows, proj_weight[0], small.reshape(-1, rows_dp)], axis=0)
    shard = jnp.pad(shard, ((0, -shard.shape[0] % 16), (0, 0)))
    w_attn, tokens_all = gather_first(shard, block_input[:, 0], dp_count, shard_count)
    up_rows = fc1_weight[0].reshape(rows_dp, -1, rows_dp).transpose(1, 0, 2).reshape(-1, rows_dp)
    mlp_rows = jnp.concatenate([up_rows, fc2_weight[0]], axis=0)
    mlp_rows, w_attn = lax.optimization_barrier((mlp_rows, w_attn))
    w_mlp = whole(mlp_rows)
    small = w_attn[:, :, 4 * rows_dp :].reshape(dp_count * shard_count, -1)[:, : small.size]
    own = width // (dp_count * shard_count)
    vectors = small[:, : 8 * own].reshape(-1, 8, own).transpose(1, 0, 2).reshape(8, width).astype(F32)
    shared = small[:shard_count, 8 * own :]
    cut = 2 * rows_shard
    qv_rows = shared[:, :cut].reshape(shard_count, 2, -1).transpose(1, 0, 2).reshape(2, width).astype(F32)
    up_bias = shared[:, cut:].reshape(1, hidden).astype(F32)

    def tied(*values):
        return lax.optimization_barrier(values)

    def forward_attend(rows, rows_all):
        h_one = layer_norm(rows.astype(F32), vectors[0], vectors[4]).astype(BF)
        h_all = layer_norm(rows_all.astype(F32), vectors[0], vectors[4]).astype(BF)
        return (h_one, h_all) + tuple(attend(h_one, h_all, w_attn, qv_rows, mask))

    def forward_mlp(rows, attended):
        return mlp(attended[5], rows, w_attn, vectors, live_cols, up_bias, w_mlp)

    def backward(cotangent, attended, risen):
        h_one, h_all, queries, key_rows, values, context, lse = attended
        attn_out, mid_rows, h_two, act, slope, mlp_out, _ = risen
        d_mlp, d_pre, d_mid, d_attn, row_sums, d_up_bias = mlp_back(
            cotangent, live_cols, vectors, mlp_out, mid_rows, attn_out, slope, w_mlp
        )
        d_q, d_k, d_v, d_qv, own_part, near, mate = attend_back(
            d_attn, w_attn, queries, key_rows, values, context, lse, mask
        )
        operands = ((act, d_mlp), (h_two, d_pre), (h_one, h_all, d_q, d_k, d_v, context, d_attn))
        return (d_mid, own_part, near, mate), (row_sums, d_qv, d_up_bias), operands

    def finish(rows, d_mid, parts, sums):
        d_h_one = sum(p.astype(F32) for p in parts)
        d_rows_ln, d_gain, d_shift = layer_norm_back(rows.astype(F32), vectors[0], d_h_one)
        row_sums, d_qv, d_up_bias = sums
        none = jnp.zeros((3, width), F32)
        row_sums = row_sums + jnp.concatenate([d_gain, none, d_shift, none], axis=0)
        return (d_mid + d_rows_ln).astype(BF), (row_sums, d_qv, d_up_bias)

    tokens_all = [jnp.where(first_section, every, 0.0) for every in tokens_all]
    tokens = [every[0] for every in tokens_all]
    tokens_all = [every.reshape(-1, width) for every in tokens_all]
    start_attended = [forward_attend(rows, every) for rows, every in zip(tokens, tokens_all)]
    w_mlp, contexts = tied(w_mlp, [attended[5] for attended in start_attended])
    start_attended = [a[:5] + (context,) + a[6:] for a, context in zip(start_attended, contexts)]
    start_risen = [None] * micro_count
    start_risen[0] = forward_mlp(tokens[0], start_attended[0])
    late_cot, low = tied(out_cotangent, start_risen[0][6])
    received = [lax.ppermute(low, "section", [(0, 1)])]
    cotangents = [swapped(late_cot[m, 0]) for m in range(micro_count)]
    for m in range(1, micro_count):
        attended = start_attended[m]
        start_risen[m] = forward_mlp(tokens[m], attended)
        low = start_risen[m][6]
        if m == 1:
            received[0], low = tied(received[0], low)
            rows = jnp.where(first_section, tokens[0], received[0])
            near_rows = near_group(rows)
        elif m == 2:
            near_rows, low = tied(near_rows, low)
        received.append(lax.ppermute(low, "section", [(0, 1)]))

    zero_rows = jnp.zeros_like(tokens[0])
    section_out, input_grad, back_rows, sums, operands = [], [], [], [], []
    d_received, pending = zero_rows, None
    for m in range(micro_count):
        attended = forward_attend(rows, with_mate(near_rows))
        if pending is not None:
            old_rows, d_mid, parts, part_sums = pending
            parts, context = tied(parts, attended[5])
            attended = attended[:5] + (context,) + attended[6:]
            d_low, part_sums = finish(old_rows, d_mid, parts, part_sums)
            back_rows.append(d_low)
            sums.append(part_sums)
            d_received = lax.ppermute(d_low, "section", [(1, 0)])
        if m + 1 < micro_count:
            received[m + 1], context = tied(received[m + 1], attended[5])
            attended = attended[:5] + (context,) + attended[6:]
            next_rows = jnp.where(first_section, tokens[m], received[m + 1])
            near_rows = near_group(next_rows)
        risen = forward_mlp(rows, attended)
        near_rows, d_received, slope = tied(near_rows, d_received, risen[4])
        risen = risen[:4] + (slope,) + risen[5:]
        section_out.append(swapped(jnp.where(first_section, start_risen[m][6], risen[6])))
        cotangent = jnp.where(first_section, d_received, cotangents[m])
        (d_mid, own_part, near, mate), part_sums, pieces = backward(cotangent, attended, risen)
        operands.append(pieces)
        section_out[m], mate = lax.optimization_barrier((section_out[m], mate))
        if m >= 2:
            done_rows = swapped(jnp.where(first_section, back_rows[m - 1], back_rows[m - 2]))
            done_rows, mate = lax.optimization_barrier((done_rows, mate))
            input_grad.append(done_rows)
        pending = (rows, d_mid, reduce_near(own_part, near, mate), part_sums)
        rows = next_rows
    full_steps = operands[1:]
    early_attn = attn_grad([step[2] for step in full_steps], dp_count, shard_count, None)
    old_rows, d_mid, parts, part_sums = pending
    parts, early_attn = tied(parts, early_attn)
    d_low, part_sums = finish(old_rows, d_mid, parts, part_sums)
    back_rows.append(d_low)
    sums.append(part_sums)
    held, d_low = tied([step[:2] for step in full_steps], d_low)
    d_received = lax.ppermute(d_low, "section", [(1, 0)])
    early_down = down_grad([step[0] for step in held], dp_count, shard_count, None)
    early_up = up_grad([step[1] for step in held], dp_count, shard_count, None)
    d_received, early_down, early_up = tied(d_received, early_down, early_up)
    if micro_count >= 2:
        input_grad.append(swapped(jnp.where(first_section, back_rows[-1], back_rows[-2])))
    (d_mid, own_part, near, mate), part_sums, pieces = backward(
        jnp.where(first_section, d_received, zero_rows), start_attended[-1], start_risen[-1]
    )
    last_steps = [operands[0], pieces]
    if micro_count >= 2:
        input_grad[-1], mate = lax.optimization_barrier((input_grad[-1], mate))
    d_low, part_sums = finish(tokens[-1], d_mid, reduce_near(own_part, near, mate), part_sums)
    input_grad.append(swapped(jnp.where(first_section, d_low, back_rows[-1])))
    sums.append(part_sums)

    grads = [
        down_grad([step[0] for step in last_steps], dp_count, shard_count, early_down),
        up_grad([step[1] for step in last_steps], dp_count, shard_count, early_up),
        attn_grad([step[2] for step in last_steps], dp_count, shard_count, early_attn),
    ]
    grads, input_grad[-1] = lax.optimization_barrier((grads, input_grad[-1]))
    row_sums, d_qv, d_up_bias = (sum(step[n] for step in sums) for n in range(3))
    whole_grid = (dp_count, shard_count)
    small_sums = jnp.concatenate(
        [
            row_sums.reshape((8,) + whole_grid + (own,)).transpose(1, 2, 0, 3).reshape(whole_grid + (-1,)),
            jnp.broadcast_to(
                d_qv.reshape(2, shard_count, rows_dp).transpose(1, 0, 2).reshape(1, shard_count, -1),
                whole_grid + (2 * rows_dp,),
            ),
            jnp.broadcast_to(d_up_bias.reshape(1, shard_count, -1), whole_grid + (hidden // shard_count,)),
        ],
        axis=2,
    ).reshape(whole_grid + (-1, rows_dp))
    d_down, d_up, d_attn, small_total = scatter_sums(list(grads) + [small_sums], dp_count, shard_count)
    d_qkv = d_attn[: 3 * rows_dp].reshape(3, rows_dp, rows_dp).transpose(1, 0, 2)
    d_proj = d_attn[3 * rows_dp :]
    small_total = small_total.reshape(-1)
    gain_grad = small_total[: 4 * own].reshape(4, own)
    bias_grad = small_total[4 * own : 8 * own].reshape(4, own)
    qv_grad = small_total[8 * own : 8 * own + 2 * rows_dp].reshape(2, rows_dp)
    up_bias_grad = small_total[8 * own + 2 * rows_dp :]

    section_out, input_grad = jnp.stack(section_out), jnp.stack(input_grad)
    return (
        section_out[None, :, None],
        input_grad[None, :, None],
        d_qkv[None],
        qv_grad[None],
        d_proj[None],
        d_up[None],
        up_bias_grad[None],
        d_down[None],
        gain_grad[None],
        bias_grad[None],
    )


def solution(mesh):
    in_specs = (
        P(None, "dp", "tensor", None),
        P(None, "dp", "tensor", None),
        P(),
        P("section", "dp", None, "tensor"),
        P("section", None, "tensor"),
        P("section", "tensor", "dp"),
        P("section", "dp", "tensor"),
        P("section", "tensor"),
        P("section", "tensor", "dp"),
        P("section", None, ("dp", "tensor")),
        P("section", None, ("dp", "tensor")),
    )
    out_specs = (
        P("section", None, "dp", "tensor", None),
        P("section", None, "dp", "tensor", None),
        P("section", "dp", None, "tensor"),
        P("section", None, "tensor"),
        P("section", "tensor", "dp"),
        P("section", "dp", "tensor"),
        P("section", "tensor"),
        P("section", "tensor", "dp"),
        P("section", None, ("dp", "tensor")),
        P("section", None, ("dp", "tensor")),
    )
    return jax.shard_map(local, mesh=mesh, in_specs=in_specs, out_specs=out_specs, check_vma=False)
```

```python
from functools import partial

import jax
import jax.numpy as jnp
from jax import lax
from jax.experimental import pallas as pl
from jax.experimental.pallas import tpu as pltpu
from jax.sharding import PartitionSpec as P

HD = 64
LANES = 128
EPS = 1e-06
NEG = -1000000000.0
F32 = jnp.float32
BF = jnp.bfloat16
BOTH = ("dp", "tensor")
MIB = 2**20


def dot_nt(a, b):
    return lax.dot_general(a, b, (((1,), (1,)), ((), ())), preferred_element_type=F32)


def dot_nn(a, b):
    return lax.dot_general(a, b, (((1,), (0,)), ((), ())), preferred_element_type=F32)


def dot_tn(a, b):
    return lax.dot_general(a, b, (((0,), (0,)), ((), ())), preferred_element_type=F32)


def normalize(rows):
    mean = jnp.mean(rows, axis=-1, keepdims=True)
    centred = rows - mean
    spread = jnp.mean(centred * centred, axis=-1, keepdims=True)
    inverse = lax.rsqrt(spread + EPS)
    return centred * inverse, inverse


def layer_norm(rows, gain, shift):
    return normalize(rows)[0] * gain + shift


def layer_norm_back(rows, gain, d_out):
    normed, inverse = normalize(rows)
    scaled = gain * d_out
    mean = jnp.mean(scaled, axis=-1, keepdims=True)
    along = jnp.mean(scaled * normed, axis=-1, keepdims=True)
    d_rows = inverse * (scaled - mean - normed * along)
    d_gain = jnp.sum(d_out * normed, axis=0, keepdims=True)
    return d_rows, d_gain, jnp.sum(d_out, axis=0, keepdims=True)


def gelu_and_slope(x):
    size = jnp.abs(x)
    t = 1.0 / (1.0 + (0.3275911 * 0.7071067811865476) * size)
    bell = jnp.exp(-0.5 * x * x)
    poly = 0.5 * 1.061405429
    for factor in (-1.453152027, 1.421413741, -0.284496736, 0.254829592):
        poly = poly * t + 0.5 * factor
    tail = poly * t * bell
    below = jnp.where(x < 0.0, tail, 1.0 - tail)
    return x * below, below + x * bell * 0.3989422804014327


def lane_ids(shape):
    return lax.broadcasted_iota(jnp.int32, shape, 1)


def staged(units, *stages):
    for at in range(len(units) + len(stages) - 1):
        for late, stage in enumerate(stages):
            if 0 <= at - late < len(units):
                stage(units[at - late])


def in_pairs(count, rise, bend, fall):
    waiting = []
    rise(0)
    for unit in range(count):
        if unit + 1 < count:
            rise(unit + 1)
        bend(unit)
        if unit % 2:
            waiting.append(unit)
        if waiting and (unit % 2 == 0 or unit + 1 == count):
            for ready in waiting:
                fall(ready)
            waiting = []


def stack_rows(blocks):
    return blocks.reshape(blocks.shape[0] * blocks.shape[1], blocks.shape[2])


def join_cols(blocks):
    return jnp.concatenate([blocks[i] for i in range(blocks.shape[0])], axis=1)


def call(kernel, grid, ins, outs, scratch, flops, name, grant=32, far=()):
    arrays, in_specs = zip(*ins)
    shapes, out_specs = zip(*outs)
    shapes = [pltpu.HBM(o.shape, o.dtype) if n in far else o for n, o in enumerate(shapes)]
    moved = sum(a.size * a.dtype.itemsize for a in arrays) + sum(s.size * s.dtype.itemsize for s, _ in outs)
    return pl.pallas_call(
        kernel,
        grid=(grid,),
        in_specs=list(in_specs),
        out_specs=list(out_specs),
        out_shape=list(shapes),
        scratch_shapes=scratch,
        compiler_params=pltpu.CompilerParams(vmem_limit_bytes=grant * MIB),
        cost_estimate=pl.CostEstimate(flops=flops, bytes_accessed=moved, transcendentals=0),
        name=name,
    )(*arrays)


def fixed(shape):
    return pl.BlockSpec(shape, lambda i: (0,) * len(shape))


def by_cols(rows, cols):
    return pl.BlockSpec((rows, cols), lambda i: (0, i))


def by_shard(blocks, rows=None, at=0):
    dp, _, own_rows, cols = blocks.shape
    return pl.BlockSpec((dp, 1, rows or own_rows, cols), lambda i: (0, i, at, 0))


def attend_kernel(
    h_ref, h_all_ref, w_ref, bias_ref, mask_ref, q_ref, k_ref, v_ref, o_ref, lse_ref
):
    part = q_ref.shape[1]
    w_q, w_k, w_v = (stack_rows(w_ref[:, 0, n * part : (n + 1) * part]) for n in range(3))
    q_ref[...] = (dot_nn(h_ref[...], w_q) + bias_ref[0:1]).astype(BF)
    k_ref[...] = dot_nn(h_all_ref[...], w_k).astype(BF)
    v_ref[...] = (dot_nn(h_all_ref[...], w_v) + bias_ref[1:2]).astype(BF)
    mask = mask_ref[...]
    k_lane, q_lane = lane_ids((k_ref.shape[0], LANES)), lane_ids((q_ref.shape[0], LANES))
    units = [(pair, half) for pair in range(part // LANES) for half in range(2)]
    scores, probs, done = {}, {}, {}

    def cols(pair):
        return slice(pair * LANES, (pair + 1) * LANES)

    def score(unit):
        pair, half = unit
        spare = HD * (1 - half)
        low_q = (q_ref[:, cols(pair)].astype(F32) * HD**-0.5).astype(BF)
        q_one = jnp.where(q_lane == spare, 1.0, 0.0).astype(BF)
        k_bias = jnp.where(k_lane == spare, mask, 0.0).astype(BF)
        q_own = jnp.where((q_lane // HD) == half, low_q, q_one)
        k_own = jnp.where((k_lane // HD) == half, k_ref[:, cols(pair)], k_bias)
        scores[unit] = dot_nt(q_own, k_own)

    def soften(unit):
        rows = scores.pop(unit)
        top = jnp.max(rows, axis=1, keepdims=True)
        probs[unit] = (jnp.exp(rows - top).astype(BF), top)

    def mix(unit):
        pair, half = unit
        spare = HD * (1 - half)
        prob, top = probs.pop(unit)
        v_one = jnp.where(k_lane == spare, 1.0, 0.0).astype(BF)
        v_own = jnp.where((k_lane // HD) == half, v_ref[:, cols(pair)], v_one)
        out = dot_nn(prob, v_own)
        total = out[:, spare : spare + 1]
        done[unit] = (out * (1.0 / total), top + jnp.log(total))
        if half == 1:
            first, second = done.pop((pair, 0)), done.pop(unit)
            o_ref[:, cols(pair)] = jnp.where(q_lane < HD, first[0], second[0]).astype(BF)
            lse_ref[:, cols(pair)] = jnp.where(q_lane < HD, first[1], second[1])

    staged(units, score, soften, mix)


def attend(h_one, h_all, w_attn, qv_rows, mask):
    slots, width = h_one.shape
    keys = h_all.shape[0]
    part = w_attn.shape[3]
    own, every = by_cols(slots, part), by_cols(keys, part)
    row = jax.ShapeDtypeStruct((slots, width), BF)
    col = jax.ShapeDtypeStruct((keys, width), BF)
    return call(
        attend_kernel,
        w_attn.shape[1],
        [
            (h_one, fixed(h_one.shape)),
            (h_all, fixed(h_all.shape)),
            (w_attn, by_shard(w_attn, 3 * part)),
            (qv_rows, by_cols(2, part)),
            (mask, fixed(mask.shape)),
        ],
        [(row, own), (col, every), (col, every), (row, own), (jax.ShapeDtypeStruct(row.shape, F32), own)],
        [],
        width * (2 * width * (slots + 2 * keys) + 16 * slots * keys),
        "attend",
        far=(1, 2),
    )


def split_three(value):
    first = value.astype(BF)
    rest = value - first.astype(F32)
    second = rest.astype(BF)
    return first, second, (rest - second.astype(F32)).astype(BF)


def attend_back_kernel(
    d_attn_ref, w_proj_ref, w_ref, q_ref, k_ref, v_ref, ctx_ref, lse_ref, mask_ref,
    dq_ref, dk_ref, dv_ref, sums_ref, own_ref, near_ref, mate_ref,
    do_ref, acc_q, acc_k,
):
    slots, part = q_ref.shape
    do_ref[...] = dot_nt(d_attn_ref[...], join_cols(w_proj_ref[:, 0])).astype(BF)
    mask = mask_ref[...]
    q_lane, k_lane = lane_ids((slots, LANES)), lane_ids((k_ref.shape[0], LANES))
    units = [(pair, half) for pair in range(part // LANES) for half in range(2)]
    first_part, done = {}, {}

    def cols(pair):
        return slice(pair * LANES, (pair + 1) * LANES)

    def low_queries(pair):
        return (q_ref[:, cols(pair)].astype(F32) * HD**-0.5).astype(BF)

    def score(unit):
        pair, half = unit
        at = cols(pair)
        spare = HD * (1 - half)
        d_out, lse = do_ref[:, at], lse_ref[:, at]
        q_own, k_own = (q_lane // HD) == half, (k_lane // HD) == half
        zero_q, one_q = jnp.zeros(q_lane.shape, BF), jnp.ones(q_lane.shape, BF)
        l_one, l_two, l_three = split_three(-lse[:, HD * half : HD * half + 1])
        product = d_out.astype(F32) * ctx_ref[:, at].astype(F32)
        inner = jnp.sum(jnp.where(q_own, product, 0.0), axis=1, keepdims=True)
        i_one, i_two, _ = split_three(-inner)
        q_more = jnp.where(q_lane == spare + 2, l_two, jnp.where(q_lane == spare + 3, l_three, zero_q))
        q_more = jnp.where(q_lane == spare, one_q, jnp.where(q_lane == spare + 1, l_one, q_more))
        k_more = jnp.where((k_lane > spare) & (k_lane < spare + 4), 1.0, 0.0).astype(BF)
        k_more = jnp.where(k_lane == spare, mask, k_more)
        o_more = jnp.where(q_lane == spare, i_one, jnp.where(q_lane == spare + 1, i_two, zero_q))
        v_more = jnp.where((k_lane >= spare) & (k_lane < spare + 2), 1.0, 0.0).astype(BF)
        score = dot_nt(jnp.where(q_own, low_queries(pair), q_more), jnp.where(k_own, k_ref[:, at], k_more))
        d_prob = dot_nt(jnp.where(q_own, d_out, o_more), jnp.where(k_own, v_ref[:, at], v_more))
        prob = jnp.exp(score)
        first_part[unit] = (prob.astype(BF), (prob * d_prob).astype(BF))

    def mix(unit):
        pair, half = unit
        at = cols(pair)
        prob, d_score = first_part.pop(unit)
        done[unit] = (
            dot_nn(d_score, k_ref[:, at]) * HD**-0.5,
            dot_tn(d_score, low_queries(pair)),
            dot_tn(prob, do_ref[:, at]),
        )
        if half == 1:
            one, two = done.pop((pair, 0)), done.pop(unit)
            d_q = jnp.where(q_lane < HD, one[0], two[0]).astype(BF)
            d_k = jnp.where(k_lane < HD, one[1], two[1]).astype(BF)
            d_v = jnp.where(k_lane < HD, one[2], two[2]).astype(BF)
            dq_ref[:, at], dk_ref[:, at], dv_ref[:, at] = d_q, d_k, d_v
            sums_ref[0:1, at] = jnp.sum(d_q.astype(F32), axis=0, keepdims=True)
            sums_ref[1:2, at] = jnp.sum(d_v.astype(F32), axis=0, keepdims=True)

    staged(units, score, mix)
    w_q, w_k, w_v = (stack_rows(w_ref[:, 0, n * part : (n + 1) * part]) for n in range(3))
    from_q = dot_nt(dq_ref[...], w_q)
    from_k = dot_nt(
        jnp.concatenate([dk_ref[...], dv_ref[...]], axis=1), jnp.concatenate([w_k, w_v], axis=1)
    )

    @pl.when(pl.program_id(0) == 0)
    def _():
        acc_q[...] = from_q
        acc_k[...] = from_k

    @pl.when(pl.program_id(0) > 0)
    def _():
        acc_q[...] += from_q
        acc_k[...] += from_k

    @pl.when(pl.program_id(0) == pl.num_programs(0) - 1)
    def _():
        near = near_ref.shape[0]
        own_ref[...] = acc_q[...] + acc_k[0:slots]
        near_ref[...] = acc_k[slots : slots + near].astype(BF)
        mate_ref[...] = acc_k[slots + near :].astype(BF)


def attend_back(d_attn, w_attn, queries, key_rows, values, context, lse, mask):
    slots, width = queries.shape
    keys = key_rows.shape[0]
    part = w_attn.shape[3]
    own, every = by_cols(slots, part), by_cols(keys, part)
    row = jax.ShapeDtypeStruct((slots, width), BF)
    col = jax.ShapeDtypeStruct((keys, width), BF)
    near = jax.ShapeDtypeStruct((keys // 2 - slots, width), BF)
    mate = jax.ShapeDtypeStruct((keys // 2, width), BF)
    return call(
        attend_back_kernel,
        w_attn.shape[1],
        [
            (d_attn, fixed(d_attn.shape)),
            (w_attn, by_shard(w_attn, part, 3)),
            (w_attn, by_shard(w_attn, 3 * part)),
            (queries, own),
            (key_rows, every),
            (values, every),
            (context, own),
            (lse, own),
            (mask, fixed(mask.shape)),
        ],
        [
            (row, own),
            (col, every),
            (col, every),
            (jax.ShapeDtypeStruct((2, width), F32), by_cols(2, part)),
            (jax.ShapeDtypeStruct((slots, width), F32), fixed((slots, width))),
            (near, fixed(near.shape)),
            (mate, fixed(mate.shape)),
        ],
        [pltpu.VMEM((slots, part), BF), pltpu.VMEM((slots, width), F32), pltpu.VMEM((keys, width), F32)],
        width * (2 * width * (2 * slots + 2 * keys) + 40 * slots * keys),
        "attend_back",
        far=(0, 1, 2),
    )


def mlp_kernel(
    ctx_ref, rows_ref, w_proj_ref, vec_ref, live_ref, bias_ref, w_up_ref, w_down_ref,
    attn_ref, mid_ref, h_ref, act_ref, slope_ref, out_ref, low_ref,
):
    dp, _, part, _ = w_up_ref.shape
    step = pl.program_id(0)

    @pl.when(step == 0)
    def _():
        context = ctx_ref[...]
        sides = [dot_nn(context, stack_rows(w_proj_ref[i])) for i in range(dp)]
        attn_out = jnp.concatenate(sides, axis=1) + vec_ref[5:6]
        attn_ref[...] = attn_out
        mid = rows_ref[...].astype(F32) + vec_ref[1:2] * attn_out
        mid_ref[...] = mid
        h_ref[...] = layer_norm(mid, vec_ref[2:3], vec_ref[6:7]).astype(BF)
        out_ref[...] = jnp.zeros_like(out_ref)

    h = h_ref[...]
    piece = w_up_ref.shape[3]
    pre, act = {}, {}

    def rise(unit):
        at = slice(unit * piece, (unit + 1) * piece)
        pre[unit] = dot_nn(h, stack_rows(w_up_ref[:, 0, at])) + bias_ref[:, at]

    def bend(unit):
        at = slice(unit * piece, (unit + 1) * piece)
        value, slope = gelu_and_slope(pre.pop(unit))
        act[unit] = value.astype(BF)
        act_ref[:, at] = act[unit]
        slope_ref[:, at] = slope.astype(BF)

    def fall(unit):
        at = slice((unit - 1) * piece, (unit + 1) * piece)
        both = jnp.concatenate([act.pop(unit - 1), act.pop(unit)], axis=1)
        out_ref[...] += dot_nn(both, join_cols(w_down_ref[:, 0, at]))

    in_pairs(part // piece, rise, bend, fall)

    @pl.when(step == pl.num_programs(0) - 1)
    def _():
        mlp_out = out_ref[...] + vec_ref[7:8]
        out_ref[...] = mlp_out
        low_ref[...] = (live_ref[:, 0:1] * (mid_ref[...] + vec_ref[3:4] * mlp_out)).astype(BF)


def mlp(context, rows, w_attn, vectors, live, up_bias, w_mlp):
    slots, width = rows.shape
    dp, shards, part, lanes = w_mlp.shape
    part = part // 2
    hidden = part * shards
    full = fixed((slots, width))
    wide = jax.ShapeDtypeStruct((slots, width), F32)
    low = jax.ShapeDtypeStruct((slots, width), BF)
    tall = jax.ShapeDtypeStruct((slots, hidden), BF)
    return call(
        mlp_kernel,
        shards,
        [
            (context, full),
            (rows, full),
            (w_attn, pl.BlockSpec((dp, shards, lanes, lanes), lambda i: (0, 0, 3, 0))),
            (vectors, fixed(vectors.shape)),
            (live, fixed(live.shape)),
            (up_bias, by_cols(1, part)),
            (w_mlp, by_shard(w_mlp, part)),
            (w_mlp, by_shard(w_mlp, part, 1)),
        ],
        [
            (wide, full),
            (wide, full),
            (low, full),
            (tall, by_cols(slots, part)),
            (tall, by_cols(slots, part)),
            (wide, full),
            (low, full),
        ],
        [],
        2 * slots * width * (width + 2 * hidden),
        "mlp",
        far=(2, 3),
    )


def mlp_back_kernel(
    cot_ref, live_ref, vec_ref, out_ref, mid_ref, attn_ref, slope_ref, w_up_ref, w_down_ref,
    d_mlp_ref, d_pre_ref, d_mid_ref, d_attn_ref, sums_ref, up_sum_ref,
    acc,
):
    part = slope_ref.shape[1]
    step = pl.program_id(0)

    @pl.when(step == 0)
    def _():
        d_res = live_ref[:, 0:1] * cot_ref[...].astype(F32)
        d_mlp = vec_ref[3:4] * d_res
        sums_ref[3:4] = jnp.sum(d_res * out_ref[...], axis=0, keepdims=True)
        sums_ref[7:8] = jnp.sum(d_mlp, axis=0, keepdims=True)
        d_mlp_ref[...] = d_mlp.astype(BF)
        acc[...] = jnp.zeros_like(acc)

    d_mlp = d_mlp_ref[...]
    piece = w_up_ref.shape[3]
    d_act, d_pre = {}, {}

    def rise(unit):
        at = slice(unit * piece, (unit + 1) * piece)
        d_act[unit] = dot_nt(d_mlp, join_cols(w_down_ref[:, 0, at]))

    def bend(unit):
        at = slice(unit * piece, (unit + 1) * piece)
        d_pre[unit] = (d_act.pop(unit) * slope_ref[:, at].astype(F32)).astype(BF)
        d_pre_ref[:, at] = d_pre[unit]
        up_sum_ref[:, at] = jnp.sum(d_pre[unit].astype(F32), axis=0, keepdims=True)

    def fall(unit):
        both = jnp.concatenate([d_pre.pop(unit - 1), d_pre.pop(unit)], axis=1)
        w_up = [stack_rows(w_up_ref[:, 0, u * piece : (u + 1) * piece]) for u in (unit - 1, unit)]
        acc[...] += dot_nt(both, jnp.concatenate(w_up, axis=1))

    in_pairs(part // piece, rise, bend, fall)

    @pl.when(step == pl.num_programs(0) - 1)
    def _():
        d_mid_ln, d_gain, d_shift = layer_norm_back(mid_ref[...], vec_ref[2:3], acc[...])
        d_mid = live_ref[:, 0:1] * cot_ref[...].astype(F32) + d_mid_ln
        d_attn = vec_ref[1:2] * d_mid
        d_mid_ref[...] = d_mid
        d_attn_ref[...] = d_attn.astype(BF)
        sums_ref[2:3] = d_gain
        sums_ref[6:7] = d_shift
        sums_ref[1:2] = jnp.sum(d_mid * attn_ref[...], axis=0, keepdims=True)
        sums_ref[5:6] = jnp.sum(d_attn, axis=0, keepdims=True)
        sums_ref[0:1] = jnp.zeros_like(d_gain)
        sums_ref[4:5] = jnp.zeros_like(d_gain)


def mlp_back(cotangent, live, vectors, mlp_out, mid_rows, attn_out, slope, w_mlp):
    slots, width = cotangent.shape
    part, shards = w_mlp.shape[2] // 2, w_mlp.shape[1]
    hidden = part * shards
    full = fixed((slots, width))
    low = jax.ShapeDtypeStruct((slots, width), BF)
    return call(
        mlp_back_kernel,
        shards,
        [
            (cotangent, full),
            (live, fixed(live.shape)),
            (vectors, fixed(vectors.shape)),
            (mlp_out, full),
            (mid_rows, full),
            (attn_out, full),
            (slope, by_cols(slots, part)),
            (w_mlp, by_shard(w_mlp, part)),
            (w_mlp, by_shard(w_mlp, part, 1)),
        ],
        [
            (low, full),
            (jax.ShapeDtypeStruct((slots, hidden), BF), by_cols(slots, part)),
            (jax.ShapeDtypeStruct((slots, width), F32), full),
            (low, full),
            (jax.ShapeDtypeStruct((8, width), F32), fixed((8, width))),
            (jax.ShapeDtypeStruct((1, hidden), F32), by_cols(1, part)),
        ],
        [pltpu.VMEM((slots, width), F32)],
        4 * slots * width * hidden,
        "mlp_back",
        far=(0, 1),
    )


def summed(refs, steps, stride, left, right, base):
    if base:
        late = lax.axis_index("section") == 0
        return dot_tn(refs[left][...], jnp.where(late, refs[stride + right][...], refs[right][...]))
    return sum(dot_tn(refs[stride * s + left][...], refs[stride * s + right][...]) for s in range(steps))


def put(out_ref, base, i, at, value):
    if base:
        value = value + base[0][i, 0, at].astype(F32)
    out_ref[i, 0, at] = value.astype(out_ref.dtype)


def down_grad_kernel(steps, *refs):
    base, out_ref = refs[2 * steps : -1], refs[-1]
    total = summed(refs, steps, 2, 0, 1, base)
    cols = out_ref.shape[3]
    for i in range(out_ref.shape[0]):
        put(out_ref, base, i, slice(None), total[:, i * cols : (i + 1) * cols])


def up_grad_kernel(steps, *refs):
    base, out_ref = refs[2 * steps : -1], refs[-1]
    total = summed(refs, steps, 2, 0, 1, base)
    rows = out_ref.shape[2]
    for i in range(out_ref.shape[0]):
        put(out_ref, base, i, slice(None), total[i * rows : (i + 1) * rows])


def attn_grad_kernel(steps, *refs):
    base, out_ref = refs[7 * steps : -1], refs[-1]
    dp, _, _, lanes = out_ref.shape
    for n, (left, right) in enumerate(((0, 2), (1, 3), (1, 4))):
        total = summed(refs, steps, 7, left, right, base)
        for i in range(dp):
            put(out_ref, base, i, slice(n * lanes, (n + 1) * lanes), total[i * lanes : (i + 1) * lanes])
    total = summed(refs, steps, 7, 5, 6, base)
    for i in range(dp):
        put(out_ref, base, i, slice(3 * lanes, 4 * lanes), total[:, i * lanes : (i + 1) * lanes])


def grad_call(kernel, steps, shards, ins, shape, base, flops, name):
    out = jax.ShapeDtypeStruct(shape, BF)
    if base is not None:
        ins = ins + [(base, by_shard(base))]
    return call(partial(kernel, steps), shards, ins, [(out, by_shard(out))], [], flops, name, 60)[0]


def attn_grad(steps, dp, shards, base):
    ins, flops = [], 0
    lanes = steps[0][0].shape[1] // shards
    for h_one, h_all, d_q, d_k, d_v, context, d_attn in steps:
        ins += [(h_one, fixed(h_one.shape)), (h_all, fixed(h_all.shape))]
        ins += [(d, by_cols(d.shape[0], lanes)) for d in (d_q, d_k, d_v, context)]
        ins += [(d_attn, fixed(d_attn.shape))]
        flops += 4 * (h_one.size + h_all.size) * h_one.shape[1]
    shape = (dp, shards, 4 * lanes, lanes)
    return grad_call(attn_grad_kernel, len(steps), shards, ins, shape, base, flops, "attn_grad")


def down_grad(pairs, dp, shards, base):
    ins = []
    for left, right in pairs:
        ins += [(left, by_cols(left.shape[0], left.shape[1] // shards)), (right, fixed(right.shape))]
    shape = (dp, shards, pairs[0][0].shape[1] // shards, pairs[0][1].shape[1] // dp)
    flops = sum(2 * left.size * right.shape[1] for left, right in pairs)
    return grad_call(down_grad_kernel, len(pairs), shards, ins, shape, base, flops, "down_grad")


def up_grad(pairs, dp, shards, base):
    ins = []
    for left, right in pairs:
        ins += [(left, fixed(left.shape)), (right, by_cols(right.shape[0], right.shape[1] // shards))]
    shape = (dp, shards, pairs[0][0].shape[1] // dp, pairs[0][1].shape[1] // shards)
    flops = sum(2 * left.size * right.shape[1] for left, right in pairs)
    return grad_call(up_grad_kernel, len(pairs), shards, ins, shape, base, flops, "up_grad")


def gather_kernel(
    dp, shards, micro, shard_ref, rows_ref, whole_ref, every_ref,
    swap_sem, near_sem, token_sem, pass_sem, line_sem, side_sem, core_sem, local_sem,
):
    groups, span = dp // 2, shards // 2
    section, dp_idx, place = lax.axis_index("section"), lax.axis_index("dp"), lax.axis_index("tensor")
    group, odd = dp_idx // 2, dp_idx % 2
    half, own_u = place // span, place % span
    mesh_id = pl.DeviceIdType.MESH
    mate = (section, group * 2 + 1 - odd, place)
    others = [(section, lax.rem(group + r, groups) * 2 + odd, place) for r in range(1, groups)]
    near = [(section, dp_idx, half * span + lax.rem(own_u + r, span)) for r in range(1, span)]
    swap = (section, group * 2 + half, odd * span + own_u)
    before, after = (section, dp_idx, place - 1), (section, dp_idx, place + 1)
    moves, has_before, has_after = odd != half, place > 0, place < shards - 1
    first, partner = section == 0, (1 - section, dp_idx, place)

    def remote(src, dst, sems, at, device):
        return pltpu.make_async_remote_copy(
            src_ref=src,
            dst_ref=dst,
            send_sem=sems.at[(0,) + at],
            recv_sem=sems.at[(1,) + at],
            device_id=device,
            device_id_type=mesh_id,
        )

    barrier = pltpu.get_barrier_semaphore()

    def greet(device):
        pl.semaphore_signal(barrier, inc=1, device_id=device, device_id_type=mesh_id)

    for device in [mate, partner] + others + near:
        greet(device)
    pl.when(moves)(lambda: greet(swap))
    pl.when(has_before)(lambda: greet(before))
    pl.when(has_after)(lambda: greet(after))
    count = 2 + len(others) + len(near)
    for there in (moves, has_before, has_after):
        count = count + jnp.where(there, 1, 0)
    pl.semaphore_wait(barrier, count)

    def swap_copy(m):
        return remote(rows_ref.at[m], every_ref.at[m, 0], swap_sem, (m,), swap)

    def stay_copy(m):
        return pltpu.make_async_copy(rows_ref.at[m], every_ref.at[m, 0], local_sem.at[m])

    def pass_copy(m):
        return remote(every_ref.at[m, 0], every_ref.at[m, 0], pass_sem, (m,), partner)

    def near_copy(m, r, early=False):
        source = rows_ref.at[m] if early else every_ref.at[m, 0]
        return remote(source, every_ref.at[m, r], near_sem, (m, r - 1), near[span - 1 - r])

    def token_copy(m):
        return remote(
            every_ref.at[m, pl.ds(0, span)], every_ref.at[m, pl.ds(span, span)], token_sem, (m,), mate
        )

    def own_copy():
        return pltpu.make_async_copy(shard_ref, whole_ref.at[dp_idx, place], local_sem.at[micro])

    def source(t, own):
        return shard_ref if own else whole_ref.at[dp_idx, t]

    def line_copy(t, distance, ahead, own=False):
        return remote(
            source(t, own),
            whole_ref.at[dp_idx, t],
            line_sem,
            (0 if ahead else 1, distance - 1),
            after if ahead else before,
        )

    def side_copy(t, r, own=False):
        return remote(source(t, own), whole_ref.at[dp_idx, t], side_sem, (r - 1, t), others[r - 1])

    def core_copy(t, r, own=False):
        j = lax.rem(group + r, groups)
        at = whole_ref.at[j * 2 + odd, t]
        return remote(shard_ref if own else at, at, core_sem, (j, t), mate)

    stays = jnp.logical_not(moves)

    def set_out(m):
        pl.when(moves)(lambda: swap_copy(m).start())
        pl.when(stays)(lambda: stay_copy(m).start())

    def in_place(m):
        pl.when(moves)(lambda: swap_copy(m).wait_recv())
        pl.when(stays)(lambda: stay_copy(m).wait())

    def first_stage(m):
        if m:
            pass_copy(m).wait_recv()
        else:
            pl.when(moves)(lambda: swap_copy(m).wait_recv())
        for r in range(1, span):
            if m:
                near_copy(m, r).start()
            else:
                pl.when(moves)(lambda r=r: near_copy(m, r).start())
                pl.when(stays)(lambda r=r: near_copy(m, r, True).start())

    def second_stage(m, following):
        in_place(m)
        if following is not None:
            set_out(following)
        if m:
            pass_copy(m).start()

    order = [(m + 1) % micro for m in range(micro)] + [None]

    def token_stage(n):
        pl.when(first)(lambda: first_stage(n))
        pl.when(jnp.logical_not(first))(lambda: second_stage(order[n], order[n + 1]))

    pl.when(first)(lambda: set_out(0))
    pl.when(jnp.logical_not(first))(lambda: set_out(order[0]))
    own_copy().start()
    pl.when(has_after)(lambda: line_copy(place, 1, True, True).start())
    pl.when(has_before)(lambda: line_copy(place, 1, False, True).start())
    for r in range(1, groups):
        side_copy(place, r, True).start()
    core_copy(place, 0, True).start()

    def share(t):
        for r in range(1, groups):
            side_copy(t, r).start()
        core_copy(t, 0).start()

    def from_before(distance):
        t = place - distance
        line_copy(t, distance, True).wait_recv()
        if distance + 1 < shards:
            pl.when(has_after)(lambda: line_copy(t, distance + 1, True).start())
        share(t)

    def from_after(distance):
        t = place + distance
        line_copy(t, distance, False).wait_recv()
        if distance + 1 < shards:
            pl.when(has_before)(lambda: line_copy(t, distance + 1, False).start())
        share(t)

    for distance in range(1, shards):
        pl.when(place >= distance)(lambda d=distance: from_before(d))
        pl.when(place + distance < shards)(lambda d=distance: from_after(d))
        if distance <= micro:
            token_stage(distance - 1)
    for n in range(shards - 1, micro):
        token_stage(n)

    def from_side(t, r):
        j = lax.rem(group + r, groups)
        at = whole_ref.at[j * 2 + odd, t]
        remote(at, at, side_sem, (groups - 1 - r, t), others[r - 1]).wait_recv()
        core_copy(t, r).start()

    for r in range(1, groups):
        for distance in range(shards):
            pl.when(place >= distance)(lambda d=distance, r=r: from_side(place - d, r))
            if distance:
                pl.when(place + distance < shards)(lambda d=distance, r=r: from_side(place + d, r))

    @pl.when(first)
    def _():
        pl.when(stays)(lambda: stay_copy(0).wait())
        for m in range(micro):
            for r in range(1, span):
                near_copy(m, r).wait_recv()
            token_copy(m).start()

    own_copy().wait()

    @pl.when(first)
    def _():
        pl.when(moves)(lambda: swap_copy(0).wait_send())
        for m in range(micro):
            token_copy(m).wait()
            for r in range(1, span):
                near_copy(m, r).wait_send()

    @pl.when(jnp.logical_not(first))
    def _():
        for m in range(micro):
            pl.when(moves)(lambda m=m: swap_copy(m).wait_send())
            if m:
                pass_copy(m).wait_send()

    for t in range(shards):
        for r in range(1, groups):
            side_copy(t, r).wait_send()
        for r in range(groups):
            core_copy(t, r).wait()
    for distance in range(1, shards):
        if distance > 1:
            pl.when(has_after & (place >= distance - 1))(
                lambda d=distance: line_copy(place - d + 1, d, True).wait_send()
            )
            pl.when(has_before & (place + distance - 1 < shards))(
                lambda d=distance: line_copy(place + d - 1, d, False).wait_send()
            )
        else:
            pl.when(has_after)(lambda: line_copy(place, 1, True).wait_send())
            pl.when(has_before)(lambda: line_copy(place, 1, False).wait_send())


def gather_first(shard, rows, micro, dp, shards):
    _, slots, width = rows.shape
    groups, span = dp // 2, shards // 2
    dma = pltpu.SemaphoreType.DMA
    return pl.pallas_call(
        partial(gather_kernel, dp, shards, micro),
        in_specs=[pl.BlockSpec(memory_space=pl.ANY)] * 2,
        out_specs=[pl.BlockSpec(memory_space=pl.ANY)] * 2,
        out_shape=[
            jax.ShapeDtypeStruct((dp, shards) + shard.shape, BF),
            jax.ShapeDtypeStruct((micro, 2 * span, slots, width), BF),
        ],
        scratch_shapes=[
            dma((2, micro)),
            dma((2, micro, max(span - 1, 1))),
            dma((2, micro)),
            dma((2, micro)),
            dma((2, 2, max(shards - 1, 1))),
            dma((2, max(groups - 1, 1), shards)),
            dma((2, groups, shards)),
            dma((micro + 1,)),
        ],
        compiler_params=pltpu.CompilerParams(collective_id=2, has_side_effects=True),
        cost_estimate=pl.CostEstimate(
            flops=0, bytes_accessed=2 * dp * shards * shard.size * 2, transcendentals=0
        ),
        name="gather_first",
    )(shard, rows)


def shed_order(count, place):
    return sorted(range(count), key=lambda t: (-abs(t - place), -t))


def scatter_kernel(dp, shards, kinds, *refs):
    parts, outs = refs[:kinds], refs[kinds : 2 * kinds]
    own, got, side, line = (refs[(2 + n) * kinds : (3 + n) * kinds] for n in range(4))
    load_sem, core_sem, side_sem, line_sem = refs[6 * kinds :]
    groups = dp // 2
    section, dp_idx, place = lax.axis_index("section"), lax.axis_index("dp"), lax.axis_index("tensor")
    group, odd = dp_idx // 2, dp_idx % 2
    mate = (section, group * 2 + 1 - odd, place)
    others = [(section, lax.rem(group + r, groups) * 2 + odd, place) for r in range(1, groups)]
    before, after = (section, dp_idx, place - 1), (section, dp_idx, place + 1)
    mesh_id = pl.DeviceIdType.MESH
    tables = [shed_order(shards, z) for z in range(shards)]

    def owner(step):
        return sum(jnp.where(place == z, tables[z][step], 0) for z in range(shards))

    barrier = pltpu.get_barrier_semaphore()
    for device in [mate] + others:
        pl.semaphore_signal(barrier, inc=1, device_id=device, device_id_type=mesh_id)

    @pl.when(place > 0)
    def _():
        pl.semaphore_signal(barrier, inc=1, device_id=before, device_id_type=mesh_id)

    @pl.when(place < shards - 1)
    def _():
        pl.semaphore_signal(barrier, inc=1, device_id=after, device_id_type=mesh_id)

    ends = jnp.where(place == 0, 1, 0) + jnp.where(place == shards - 1, 1, 0)
    pl.semaphore_wait(barrier, groups + 2 - ends)

    def core_copy(step, kind):
        return pltpu.make_async_remote_copy(
            src_ref=parts[kind].at[:, 1 - odd, owner(step)],
            dst_ref=got[kind].at[step],
            send_sem=core_sem.at[0, step, kind],
            recv_sem=core_sem.at[1, step, kind],
            device_id=mate,
            device_id_type=mesh_id,
        )

    def load(step, kind):
        return pltpu.make_async_copy(
            parts[kind].at[:, odd, owner(step)], own[kind].at[step], load_sem.at[step, kind]
        )

    def side_copy(step, kind, r):
        return pltpu.make_async_remote_copy(
            src_ref=own[kind].at[step, lax.rem(group + r, groups)],
            dst_ref=side[kind].at[step, r - 1],
            send_sem=side_sem.at[0, step, kind, r - 1],
            recv_sem=side_sem.at[1, step, kind, r - 1],
            device_id=others[r - 1],
            device_id_type=mesh_id,
        )

    def line_copy(step, kind, ahead):
        target = owner(step)
        slot = target + 1 if ahead else target
        return pltpu.make_async_remote_copy(
            src_ref=own[kind].at[step, group],
            dst_ref=line[kind].at[slot],
            send_sem=line_sem.at[0, slot, kind],
            recv_sem=line_sem.at[1, slot, kind],
            device_id=after if ahead else before,
            device_id_type=mesh_id,
        )

    def add(one, two):
        return (one.astype(F32) + two.astype(F32)).astype(one.dtype)

    units = [(step, kind) for step in range(shards) for kind in range(kinds)]
    for step, kind in units:
        core_copy(step, kind).start()
        load(step, kind).start()

    def meet(unit):
        step, kind = unit
        load(step, kind).wait()
        core_copy(step, kind).wait_recv()
        for r in range(1, groups):
            at = lax.rem(group + r, groups)
            own[kind][step, at] = add(own[kind][step, at], got[kind][step, at])
            side_copy(step, kind, r).start()
        own[kind][step, group] = add(own[kind][step, group], got[kind][step, group])

    def pass_on(unit):
        step, kind = unit
        mine = own[kind][step, group].astype(F32)
        for r in range(1, groups):
            side_copy(step, kind, r).wait_recv()
            mine = mine + side[kind][step, r - 1].astype(F32)
        own[kind][step, group] = mine.astype(own[kind].dtype)
        target = owner(step)

        @pl.when((target >= place) & (place > 0))
        def _():
            line_copy(step, kind, True).wait_recv()
            slot = target + 1
            own[kind][step, group] = add(own[kind][step, group], line[kind][slot])

        @pl.when((target <= place) & (place < shards - 1))
        def _():
            line_copy(step, kind, False).wait_recv()
            own[kind][step, group] = add(own[kind][step, group], line[kind][target])

        @pl.when(target > place)
        def _():
            line_copy(step, kind, True).start()

        @pl.when(target < place)
        def _():
            line_copy(step, kind, False).start()

        if step == shards - 1:
            outs[kind][...] = own[kind][step, group].astype(F32)

    lag = kinds
    for at in range(len(units) + lag):
        if at < len(units):
            meet(units[at])
        if at >= lag:
            pass_on(units[at - lag])

    for step, kind in units:
        core_copy(step, kind).wait_send()
        for r in range(1, groups):
            side_copy(step, kind, r).wait_send()
        if step < shards - 1:
            target = owner(step)

            @pl.when(target > place)
            def _():
                line_copy(step, kind, True).wait_send()

            @pl.when(target < place)
            def _():
                line_copy(step, kind, False).wait_send()


def scatter_sums(parts, dp, shards):
    kinds, groups = len(parts), dp // 2
    split = [p.reshape((groups, 2) + p.shape[1:]) for p in parts]
    blocks = [p.shape[2:] for p in parts]
    scratch = []
    for lead in ((shards, groups), (shards, groups), (shards, max(groups - 1, 1)), (shards + 1,)):
        scratch += [pltpu.VMEM(lead + b, p.dtype) for p, b in zip(parts, blocks)]
    scratch += [
        pltpu.SemaphoreType.DMA((shards, kinds)),
        pltpu.SemaphoreType.DMA((2, shards, kinds)),
        pltpu.SemaphoreType.DMA((2, shards, kinds, max(groups - 1, 1))),
        pltpu.SemaphoreType.DMA((2, shards + 1, kinds)),
    ]
    return pl.pallas_call(
        partial(scatter_kernel, dp, shards, kinds),
        in_specs=[pl.BlockSpec(memory_space=pl.ANY)] * kinds,
        out_specs=[pl.BlockSpec(memory_space=pltpu.VMEM)] * kinds,
        out_shape=[jax.ShapeDtypeStruct(b, F32) for b in blocks],
        scratch_shapes=scratch,
        compiler_params=pltpu.CompilerParams(
            vmem_limit_bytes=60 * MIB, collective_id=1, has_side_effects=True
        ),
        cost_estimate=pl.CostEstimate(
            flops=0, bytes_accessed=sum(4 * p.size * p.dtype.itemsize for p in parts), transcendentals=0
        ),
        name="scatter_sums",
    )(*split)


def local(
    block_input,
    out_cotangent,
    lengths,
    qkv_weight,
    qv_bias,
    proj_weight,
    fc1_weight,
    fc1_bias,
    fc2_weight,
    gains,
    biases,
):
    section_idx = lax.axis_index("section")
    dp_count, shard_count = lax.axis_size("dp"), lax.axis_size("tensor")
    dp_idx, shard_idx = lax.axis_index("dp"), lax.axis_index("tensor")
    micro_count, _, slots, width = block_input.shape
    hidden = fc1_weight.shape[2] * shard_count
    first_section = section_idx == 0

    span = shard_count // 2
    odd, own_u = dp_idx % 2, shard_idx % span

    swap_pairs = [
        ((2 * j + a) * shard_count + b * span + u, (2 * j + b) * shard_count + a * span + u)
        for j in range(dp_count // 2)
        for a in range(2)
        for b in range(2)
        for u in range(span)
    ]
    mate_pairs = [(d, d + 1 - 2 * (d % 2)) for d in range(dp_count)]

    def turned(steps):
        return [
            (half * span + (u + steps) % span, half * span + u) for half in range(2) for u in range(span)
        ]

    def swapped(rows):
        return lax.ppermute(rows, BOTH, swap_pairs)

    def near_group(rows):
        pieces = [rows] + [lax.ppermute(rows, "tensor", turned(r)) for r in range(1, span)]
        return jnp.concatenate(pieces, axis=0)

    def with_mate(near):
        return jnp.concatenate([near, lax.ppermute(near, "dp", mate_pairs)], axis=0)

    def reduce_near(own_rows, near_rows, mate_rows):
        got = lax.ppermute(mate_rows, "dp", mate_pairs).astype(F32)
        parts = [own_rows + got[:slots]]
        for r in range(1, span):
            piece = near_rows[(r - 1) * slots : r * slots].astype(F32) + got[r * slots : (r + 1) * slots]
            parts.append(lax.ppermute(piece.astype(BF), "tensor", turned(-r)))
        return parts

    shard_of = jnp.stack([((odd + a) % 2) * span + (own_u + r) % span for a in range(2) for r in range(span)])
    slot_ids = jnp.arange(slots, dtype=jnp.int32)
    live = slot_ids[None, :] < jnp.take(lengths, shard_of)[:, None]
    own_live = live[0].astype(F32)[:, None]
    live_cols = jnp.broadcast_to(own_live, (slots, LANES))
    mask = jnp.broadcast_to(jnp.where(live.reshape(-1, 1), 0.0, NEG).astype(BF), (live.size, LANES))

    small = jnp.concatenate(
        [gains[0].reshape(-1), biases[0].reshape(-1), qv_bias[0].reshape(-1), fc1_bias[0].reshape(-1)]
    )
    rows_dp, rows_shard = width // dp_count, width // shard_count

    def whole(part):
        return lax.all_gather(part, BOTH, axis=0, tiled=False).reshape(
            (dp_count, shard_count) + part.shape
        )

    qkv_rows = qkv_weight[0].transpose(1, 0, 2).reshape(-1, rows_dp)
    shard = jnp.concatenate([qkv_rows, proj_weight[0], small.reshape(-1, rows_dp)], axis=0)
    shard = jnp.pad(shard, ((0, -shard.shape[0] % 16), (0, 0)))
    w_attn, tokens_all = gather_first(
        shard, block_input[:, 0], micro_count - 1, dp_count, shard_count
    )
    up_rows = fc1_weight[0].reshape(rows_dp, -1, rows_dp).transpose(1, 0, 2).reshape(-1, rows_dp)
    mlp_rows = jnp.concatenate([up_rows, fc2_weight[0]], axis=0)
    mlp_rows, w_attn = lax.optimization_barrier((mlp_rows, w_attn))
    w_mlp = whole(mlp_rows)
    small = w_attn[:, :, 4 * rows_dp :].reshape(dp_count * shard_count, -1)[:, : small.size]
    own = width // (dp_count * shard_count)
    vectors = small[:, : 8 * own].reshape(-1, 8, own).transpose(1, 0, 2).reshape(8, width).astype(F32)
    shared = small[:shard_count, 8 * own :]
    cut = 2 * rows_shard
    qv_rows = shared[:, :cut].reshape(shard_count, 2, -1).transpose(1, 0, 2).reshape(2, width).astype(F32)
    up_bias = shared[:, cut:].reshape(1, hidden).astype(F32)

    def tied(*values):
        return lax.optimization_barrier(values)

    def forward_attend(rows, rows_all):
        h_one = layer_norm(rows.astype(F32), vectors[0], vectors[4]).astype(BF)
        h_all = layer_norm(rows_all.astype(F32), vectors[0], vectors[4]).astype(BF)
        return (h_one, h_all) + tuple(attend(h_one, h_all, w_attn, qv_rows, mask))

    def forward_mlp(rows, attended):
        return mlp(attended[5], rows, w_attn, vectors, live_cols, up_bias, w_mlp)

    def backward(cotangent, attended, risen):
        h_one, h_all, queries, key_rows, values, context, lse = attended
        attn_out, mid_rows, h_two, act, slope, mlp_out, _ = risen
        d_mlp, d_pre, d_mid, d_attn, row_sums, d_up_bias = mlp_back(
            cotangent, live_cols, vectors, mlp_out, mid_rows, attn_out, slope, w_mlp
        )
        d_q, d_k, d_v, d_qv, own_part, near, mate = attend_back(
            d_attn, w_attn, queries, key_rows, values, context, lse, mask
        )
        operands = ((act, d_mlp), (h_two, d_pre), (h_one, h_all, d_q, d_k, d_v, context, d_attn))
        return (d_mid, own_part, near, mate), (row_sums, d_qv, d_up_bias), operands

    def finish(rows, d_mid, parts, sums):
        d_h_one = sum(p.astype(F32) for p in parts)
        d_rows_ln, d_gain, d_shift = layer_norm_back(rows.astype(F32), vectors[0], d_h_one)
        row_sums, d_qv, d_up_bias = sums
        none = jnp.zeros((3, width), F32)
        row_sums = row_sums + jnp.concatenate([d_gain, none, d_shift, none], axis=0)
        return (d_mid + d_rows_ln).astype(BF), (row_sums, d_qv, d_up_bias)

    tokens_all = [jnp.where(first_section, every, 0.0) for every in tokens_all]
    tokens = [every[0] for every in tokens_all]
    tokens_all = [every.reshape(-1, width) for every in tokens_all]
    start_attended = [forward_attend(rows, every) for rows, every in zip(tokens, tokens_all)]
    w_mlp, contexts = tied(w_mlp, [attended[5] for attended in start_attended])
    start_attended = [a[:5] + (context,) + a[6:] for a, context in zip(start_attended, contexts)]
    start_risen = [None] * micro_count
    start_risen[0] = forward_mlp(tokens[0], start_attended[0])
    last = micro_count - 1
    late_rows, low = tied(block_input[last, 0], start_risen[0][6])
    received = [lax.ppermute(low, "section", [(0, 1)])]
    tokens.append(swapped(late_rows))
    start_low = [low]
    for m in range(1, last):
        start_risen[m] = forward_mlp(tokens[m], start_attended[m])
        low = start_risen[m][6]
        if m == 1:
            received[0], low = tied(received[0], low)
        start_low.append(low)
        received.append(lax.ppermute(low, "section", [(0, 1)]))
    rows = jnp.where(first_section, tokens[last], received[0])
    near_rows = near_group(rows)

    zero_rows = jnp.zeros_like(tokens[0])
    section_out, input_grad, back_rows, sums, operands = [], [], [], [], []
    d_received, pending, kept = zero_rows, None, None
    for m in range(micro_count):
        near_rows, cotangent = tied(near_rows, out_cotangent[m, 0])
        cotangent = swapped(cotangent)
        attended = forward_attend(rows, with_mate(near_rows))
        if pending is not None:
            old_rows, d_mid, parts, part_sums = pending
            parts, context = tied(parts, attended[5])
            attended = attended[:5] + (context,) + attended[6:]
            d_low, part_sums = finish(old_rows, d_mid, parts, part_sums)
            back_rows.append(d_low)
            sums.append(part_sums)
            d_received = lax.ppermute(d_low, "section", [(1, 0)])
        if m < last:
            received[m + 1], context = tied(received[m + 1], attended[5])
            attended = attended[:5] + (context,) + attended[6:]
            next_rows = jnp.where(first_section, tokens[m], received[m + 1])
            near_rows = near_group(next_rows)
        risen = forward_mlp(rows, attended)
        near_rows, d_received, cotangent, slope = tied(near_rows, d_received, cotangent, risen[4])
        risen = risen[:4] + (slope,) + risen[5:]
        if m == 0:
            received.append(lax.ppermute(risen[6], "section", [(0, 1)]))
            kept = (rows, attended, risen)
        section_out.append(swapped(jnp.where(first_section, (start_low + [kept[2][6]])[m], risen[6])))
        cotangent = jnp.where(first_section, d_received, cotangent)
        (d_mid, own_part, near, mate), part_sums, pieces = backward(cotangent, attended, risen)
        operands.append(pieces)
        section_out[m], mate = tied(section_out[m], mate)
        if m >= 2:
            done_rows = swapped(jnp.where(first_section, back_rows[m - 1], back_rows[m - 2]))
            done_rows, mate = tied(done_rows, mate)
            input_grad.append(done_rows)
        pending = (rows, d_mid, reduce_near(own_part, near, mate), part_sums)
        rows = next_rows
    full_steps = operands[1:]
    early_attn = attn_grad([step[2] for step in full_steps], dp_count, shard_count, None)
    old_rows, d_mid, parts, part_sums = pending
    parts, early_attn = tied(parts, early_attn)
    d_low, part_sums = finish(old_rows, d_mid, parts, part_sums)
    back_rows.append(d_low)
    sums.append(part_sums)
    held, d_low = tied([step[:2] for step in full_steps], d_low)
    d_received = lax.ppermute(d_low, "section", [(1, 0)])
    early_down = down_grad([step[0] for step in held], dp_count, shard_count, None)
    early_up = up_grad([step[1] for step in held], dp_count, shard_count, None)
    d_received, early_down, early_up = tied(d_received, early_down, early_up)
    if micro_count >= 2:
        input_grad.append(swapped(jnp.where(first_section, back_rows[-1], back_rows[-2])))
    rows, attended, risen = kept
    (d_mid, own_part, near, mate), part_sums, pieces = backward(
        jnp.where(first_section, d_received, zero_rows), attended, risen
    )
    last_steps = [operands[0], pieces]
    if micro_count >= 2:
        input_grad[-1], mate = tied(input_grad[-1], mate)
    parts = reduce_near(own_part, near, mate)
    late_attn = attn_grad([step[2] for step in last_steps], dp_count, shard_count, early_attn)
    parts, late_attn = tied(parts, late_attn)
    d_low, part_sums = finish(rows, d_mid, parts, part_sums)
    sums.append(part_sums)
    d_low, held = tied(d_low, [step[:2] for step in last_steps])
    input_grad.append(swapped(jnp.where(first_section, d_low, back_rows[-1])))

    grads = [
        down_grad([step[0] for step in held], dp_count, shard_count, early_down),
        up_grad([step[1] for step in held], dp_count, shard_count, early_up),
        late_attn,
    ]
    grads, input_grad[-1] = lax.optimization_barrier((grads, input_grad[-1]))
    row_sums, d_qv, d_up_bias = (sum(step[n] for step in sums) for n in range(3))
    whole_grid = (dp_count, shard_count)
    small_sums = jnp.concatenate(
        [
            row_sums.reshape((8,) + whole_grid + (own,)).transpose(1, 2, 0, 3).reshape(whole_grid + (-1,)),
            jnp.broadcast_to(
                d_qv.reshape(2, shard_count, rows_dp).transpose(1, 0, 2).reshape(1, shard_count, -1),
                whole_grid + (2 * rows_dp,),
            ),
            jnp.broadcast_to(d_up_bias.reshape(1, shard_count, -1), whole_grid + (hidden // shard_count,)),
        ],
        axis=2,
    ).reshape(whole_grid + (-1, rows_dp))
    d_down, d_up, d_attn, small_total = scatter_sums(list(grads) + [small_sums], dp_count, shard_count)
    d_qkv = d_attn[: 3 * rows_dp].reshape(3, rows_dp, rows_dp).transpose(1, 0, 2)
    d_proj = d_attn[3 * rows_dp :]
    small_total = small_total.reshape(-1)
    gain_grad = small_total[: 4 * own].reshape(4, own)
    bias_grad = small_total[4 * own : 8 * own].reshape(4, own)
    qv_grad = small_total[8 * own : 8 * own + 2 * rows_dp].reshape(2, rows_dp)
    up_bias_grad = small_total[8 * own + 2 * rows_dp :]

    section_out, input_grad = jnp.stack(section_out), jnp.stack(input_grad)
    return (
        section_out[None, :, None],
        input_grad[None, :, None],
        d_qkv[None],
        qv_grad[None],
        d_proj[None],
        d_up[None],
        up_bias_grad[None],
        d_down[None],
        gain_grad[None],
        bias_grad[None],
    )


def solution(mesh):
    in_specs = (
        P(None, "dp", "tensor", None),
        P(None, "dp", "tensor", None),
        P(),
        P("section", "dp", None, "tensor"),
        P("section", None, "tensor"),
        P("section", "tensor", "dp"),
        P("section", "dp", "tensor"),
        P("section", "tensor"),
        P("section", "tensor", "dp"),
        P("section", None, ("dp", "tensor")),
        P("section", None, ("dp", "tensor")),
    )
    out_specs = (
        P("section", None, "dp", "tensor", None),
        P("section", None, "dp", "tensor", None),
        P("section", "dp", None, "tensor"),
        P("section", None, "tensor"),
        P("section", "tensor", "dp"),
        P("section", "dp", "tensor"),
        P("section", "tensor"),
        P("section", "tensor", "dp"),
        P("section", None, ("dp", "tensor")),
        P("section", None, ("dp", "tensor")),
    )
    return jax.shard_map(local, mesh=mesh, in_specs=in_specs, out_specs=out_specs, check_vma=False)
```

```python
from functools import partial

import jax
import jax.numpy as jnp
from jax import lax
from jax.experimental import pallas as pl
from jax.experimental.pallas import tpu as pltpu
from jax.sharding import PartitionSpec as P

HD = 64
LANES = 128
EPS = 1e-06
NEG = -1000000000.0
F32 = jnp.float32
BF = jnp.bfloat16
BOTH = ("dp", "tensor")
MIB = 2**20


def dot_nt(a, b):
    return lax.dot_general(a, b, (((1,), (1,)), ((), ())), preferred_element_type=F32)


def dot_nn(a, b):
    return lax.dot_general(a, b, (((1,), (0,)), ((), ())), preferred_element_type=F32)


def dot_tn(a, b):
    return lax.dot_general(a, b, (((0,), (0,)), ((), ())), preferred_element_type=F32)


def normalize(rows):
    mean = jnp.mean(rows, axis=-1, keepdims=True)
    centred = rows - mean
    spread = jnp.mean(centred * centred, axis=-1, keepdims=True)
    inverse = lax.rsqrt(spread + EPS)
    return centred * inverse, inverse


def layer_norm(rows, gain, shift):
    return normalize(rows)[0] * gain + shift


def layer_norm_back(rows, gain, d_out):
    normed, inverse = normalize(rows)
    scaled = gain * d_out
    mean = jnp.mean(scaled, axis=-1, keepdims=True)
    along = jnp.mean(scaled * normed, axis=-1, keepdims=True)
    d_rows = inverse * (scaled - mean - normed * along)
    d_gain = jnp.sum(d_out * normed, axis=0, keepdims=True)
    return d_rows, d_gain, jnp.sum(d_out, axis=0, keepdims=True)


def gelu_and_slope(x):
    size = jnp.abs(x)
    t = 1.0 / (1.0 + (0.3275911 * 0.7071067811865476) * size)
    bell = jnp.exp(-0.5 * x * x)
    poly = 0.5 * 1.061405429
    for factor in (-1.453152027, 1.421413741, -0.284496736, 0.254829592):
        poly = poly * t + 0.5 * factor
    tail = poly * t * bell
    below = jnp.where(x < 0.0, tail, 1.0 - tail)
    return x * below, below + x * bell * 0.3989422804014327


def lane_ids(shape):
    return lax.broadcasted_iota(jnp.int32, shape, 1)


def staged(units, *stages):
    for at in range(len(units) + len(stages) - 1):
        for late, stage in enumerate(stages):
            if 0 <= at - late < len(units):
                stage(units[at - late])


def in_pairs(count, rise, bend, fall):
    waiting = []
    rise(0)
    for unit in range(count):
        if unit + 1 < count:
            rise(unit + 1)
        bend(unit)
        if unit % 2:
            waiting.append(unit)
        if waiting and (unit % 2 == 0 or unit + 1 == count):
            for ready in waiting:
                fall(ready)
            waiting = []


def stack_rows(blocks):
    return blocks.reshape(blocks.shape[0] * blocks.shape[1], blocks.shape[2])


def join_cols(blocks):
    return jnp.concatenate([blocks[i] for i in range(blocks.shape[0])], axis=1)


def call(kernel, grid, ins, outs, scratch, flops, name, grant=32, far=()):
    arrays, in_specs = zip(*ins)
    shapes, out_specs = zip(*outs)
    shapes = [pltpu.HBM(o.shape, o.dtype) if n in far else o for n, o in enumerate(shapes)]
    moved = sum(a.size * a.dtype.itemsize for a in arrays) + sum(s.size * s.dtype.itemsize for s, _ in outs)
    return pl.pallas_call(
        kernel,
        grid=(grid,),
        in_specs=list(in_specs),
        out_specs=list(out_specs),
        out_shape=list(shapes),
        scratch_shapes=scratch,
        compiler_params=pltpu.CompilerParams(vmem_limit_bytes=grant * MIB),
        cost_estimate=pl.CostEstimate(flops=flops, bytes_accessed=moved, transcendentals=0),
        name=name,
    )(*arrays)


def fixed(shape):
    return pl.BlockSpec(shape, lambda i: (0,) * len(shape))


def by_cols(rows, cols):
    return pl.BlockSpec((rows, cols), lambda i: (0, i))


def by_shard(blocks, rows=None, at=0):
    dp, _, own_rows, cols = blocks.shape
    return pl.BlockSpec((dp, 1, rows or own_rows, cols), lambda i: (0, i, at, 0))


def attend_kernel(
    h_ref, h_all_ref, w_q_ref, w_k_ref, w_v_ref, bias_ref, mask_ref, q_ref, k_ref, v_ref, o_ref, lse_ref
):
    part = q_ref.shape[1]
    w_q, w_k, w_v = (stack_rows(w[:, 0]) for w in (w_q_ref, w_k_ref, w_v_ref))
    q_ref[...] = (dot_nn(h_ref[...], w_q) + bias_ref[0:1]).astype(BF)
    k_ref[...] = dot_nn(h_all_ref[...], w_k).astype(BF)
    v_ref[...] = (dot_nn(h_all_ref[...], w_v) + bias_ref[1:2]).astype(BF)
    mask = mask_ref[...]
    k_lane, q_lane = lane_ids((k_ref.shape[0], LANES)), lane_ids((q_ref.shape[0], LANES))
    units = [(pair, half) for pair in range(part // LANES) for half in range(2)]
    scores, probs, done = {}, {}, {}

    def cols(pair):
        return slice(pair * LANES, (pair + 1) * LANES)

    def score(unit):
        pair, half = unit
        spare = HD * (1 - half)
        low_q = (q_ref[:, cols(pair)].astype(F32) * HD**-0.5).astype(BF)
        q_one = jnp.where(q_lane == spare, 1.0, 0.0).astype(BF)
        k_bias = jnp.where(k_lane == spare, mask, 0.0).astype(BF)
        q_own = jnp.where((q_lane // HD) == half, low_q, q_one)
        k_own = jnp.where((k_lane // HD) == half, k_ref[:, cols(pair)], k_bias)
        scores[unit] = dot_nt(q_own, k_own)

    def soften(unit):
        rows = scores.pop(unit)
        top = jnp.max(rows, axis=1, keepdims=True)
        probs[unit] = (jnp.exp(rows - top).astype(BF), top)

    def mix(unit):
        pair, half = unit
        spare = HD * (1 - half)
        prob, top = probs.pop(unit)
        v_one = jnp.where(k_lane == spare, 1.0, 0.0).astype(BF)
        v_own = jnp.where((k_lane // HD) == half, v_ref[:, cols(pair)], v_one)
        out = dot_nn(prob, v_own)
        total = out[:, spare : spare + 1]
        done[unit] = (out * (1.0 / total), top + jnp.log(total))
        if half == 1:
            first, second = done.pop((pair, 0)), done.pop(unit)
            o_ref[:, cols(pair)] = jnp.where(q_lane < HD, first[0], second[0]).astype(BF)
            lse_ref[:, cols(pair)] = jnp.where(q_lane < HD, first[1], second[1])

    staged(units, score, soften, mix)


def attend(h_one, h_all, weights, base, qv_rows, mask):
    slots, width = h_one.shape
    keys = h_all.shape[0]
    part = weights.shape[3]
    own, every = by_cols(slots, part), by_cols(keys, part)
    row = jax.ShapeDtypeStruct((slots, width), BF)
    col = jax.ShapeDtypeStruct((keys, width), BF)
    return call(
        attend_kernel,
        weights.shape[1],
        [
            (h_one, fixed(h_one.shape)),
            (h_all, fixed(h_all.shape)),
            (weights, by_shard(weights, part, base)),
            (weights, by_shard(weights, part, base + 1)),
            (weights, by_shard(weights, part, base + 2)),
            (qv_rows, by_cols(2, part)),
            (mask, fixed(mask.shape)),
        ],
        [(row, own), (col, every), (col, every), (row, own), (jax.ShapeDtypeStruct(row.shape, F32), own)],
        [],
        width * (2 * width * (slots + 2 * keys) + 16 * slots * keys),
        "attend",
        far=(1, 2),
    )


def split_three(value):
    first = value.astype(BF)
    rest = value - first.astype(F32)
    second = rest.astype(BF)
    return first, second, (rest - second.astype(F32)).astype(BF)


def attend_back_kernel(
    d_attn_ref, w_proj_ref, w_q_ref, w_k_ref, w_v_ref, q_ref, k_ref, v_ref, ctx_ref, lse_ref, mask_ref,
    dq_ref, dk_ref, dv_ref, sums_ref, own_ref, near_ref, mate_ref,
    do_ref, acc_q, acc_k,
):
    slots, part = q_ref.shape
    do_ref[...] = dot_nt(d_attn_ref[...], join_cols(w_proj_ref[:, 0])).astype(BF)
    mask = mask_ref[...]
    q_lane, k_lane = lane_ids((slots, LANES)), lane_ids((k_ref.shape[0], LANES))
    units = [(pair, half) for pair in range(part // LANES) for half in range(2)]
    first_part, done = {}, {}

    def cols(pair):
        return slice(pair * LANES, (pair + 1) * LANES)

    def low_queries(pair):
        return (q_ref[:, cols(pair)].astype(F32) * HD**-0.5).astype(BF)

    def score(unit):
        pair, half = unit
        at = cols(pair)
        spare = HD * (1 - half)
        d_out, lse = do_ref[:, at], lse_ref[:, at]
        q_own, k_own = (q_lane // HD) == half, (k_lane // HD) == half
        zero_q, one_q = jnp.zeros(q_lane.shape, BF), jnp.ones(q_lane.shape, BF)
        l_one, l_two, l_three = split_three(-lse[:, HD * half : HD * half + 1])
        product = d_out.astype(F32) * ctx_ref[:, at].astype(F32)
        inner = jnp.sum(jnp.where(q_own, product, 0.0), axis=1, keepdims=True)
        i_one, i_two, _ = split_three(-inner)
        q_more = jnp.where(q_lane == spare + 2, l_two, jnp.where(q_lane == spare + 3, l_three, zero_q))
        q_more = jnp.where(q_lane == spare, one_q, jnp.where(q_lane == spare + 1, l_one, q_more))
        k_more = jnp.where((k_lane > spare) & (k_lane < spare + 4), 1.0, 0.0).astype(BF)
        k_more = jnp.where(k_lane == spare, mask, k_more)
        o_more = jnp.where(q_lane == spare, i_one, jnp.where(q_lane == spare + 1, i_two, zero_q))
        v_more = jnp.where((k_lane >= spare) & (k_lane < spare + 2), 1.0, 0.0).astype(BF)
        score = dot_nt(jnp.where(q_own, low_queries(pair), q_more), jnp.where(k_own, k_ref[:, at], k_more))
        d_prob = dot_nt(jnp.where(q_own, d_out, o_more), jnp.where(k_own, v_ref[:, at], v_more))
        prob = jnp.exp(score)
        first_part[unit] = (prob.astype(BF), (prob * d_prob).astype(BF))

    def mix(unit):
        pair, half = unit
        at = cols(pair)
        prob, d_score = first_part.pop(unit)
        done[unit] = (
            dot_nn(d_score, k_ref[:, at]) * HD**-0.5,
            dot_tn(d_score, low_queries(pair)),
            dot_tn(prob, do_ref[:, at]),
        )
        if half == 1:
            one, two = done.pop((pair, 0)), done.pop(unit)
            d_q = jnp.where(q_lane < HD, one[0], two[0]).astype(BF)
            d_k = jnp.where(k_lane < HD, one[1], two[1]).astype(BF)
            d_v = jnp.where(k_lane < HD, one[2], two[2]).astype(BF)
            dq_ref[:, at], dk_ref[:, at], dv_ref[:, at] = d_q, d_k, d_v
            sums_ref[0:1, at] = jnp.sum(d_q.astype(F32), axis=0, keepdims=True)
            sums_ref[1:2, at] = jnp.sum(d_v.astype(F32), axis=0, keepdims=True)

    staged(units, score, mix)
    w_q, w_k, w_v = (stack_rows(w[:, 0]) for w in (w_q_ref, w_k_ref, w_v_ref))
    from_q = dot_nt(dq_ref[...], w_q)
    from_k = dot_nt(
        jnp.concatenate([dk_ref[...], dv_ref[...]], axis=1), jnp.concatenate([w_k, w_v], axis=1)
    )

    @pl.when(pl.program_id(0) == 0)
    def _():
        acc_q[...] = from_q
        acc_k[...] = from_k

    @pl.when(pl.program_id(0) > 0)
    def _():
        acc_q[...] += from_q
        acc_k[...] += from_k

    @pl.when(pl.program_id(0) == pl.num_programs(0) - 1)
    def _():
        near = near_ref.shape[0]
        own_ref[...] = acc_q[...] + acc_k[0:slots]
        near_ref[...] = acc_k[slots : slots + near].astype(BF)
        mate_ref[...] = acc_k[slots + near :].astype(BF)


def attend_back(d_attn, weights, base, queries, key_rows, values, context, lse, mask):
    slots, width = queries.shape
    keys = key_rows.shape[0]
    part = weights.shape[3]
    own, every = by_cols(slots, part), by_cols(keys, part)
    row = jax.ShapeDtypeStruct((slots, width), BF)
    col = jax.ShapeDtypeStruct((keys, width), BF)
    near = jax.ShapeDtypeStruct((keys // 2 - slots, width), BF)
    mate = jax.ShapeDtypeStruct((keys // 2, width), BF)
    return call(
        attend_back_kernel,
        weights.shape[1],
        [
            (d_attn, fixed(d_attn.shape)),
            (weights, by_shard(weights, part, base + 3)),
            (weights, by_shard(weights, part, base)),
            (weights, by_shard(weights, part, base + 1)),
            (weights, by_shard(weights, part, base + 2)),
            (queries, own),
            (key_rows, every),
            (values, every),
            (context, own),
            (lse, own),
            (mask, fixed(mask.shape)),
        ],
        [
            (row, own),
            (col, every),
            (col, every),
            (jax.ShapeDtypeStruct((2, width), F32), by_cols(2, part)),
            (jax.ShapeDtypeStruct((slots, width), F32), fixed((slots, width))),
            (near, fixed(near.shape)),
            (mate, fixed(mate.shape)),
        ],
        [pltpu.VMEM((slots, part), BF), pltpu.VMEM((slots, width), F32), pltpu.VMEM((keys, width), F32)],
        width * (2 * width * (2 * slots + 2 * keys) + 40 * slots * keys),
        "attend_back",
        far=(0, 1, 2),
    )


def mlp_kernel(
    ctx_ref, rows_ref, w_proj_ref, vec_ref, live_ref, bias_ref, w_up_ref, w_down_ref,
    attn_ref, mid_ref, h_ref, act_ref, slope_ref, out_ref, low_ref,
):
    dp, _, part, _ = w_up_ref.shape
    step = pl.program_id(0)

    @pl.when(step == 0)
    def _():
        context = ctx_ref[...]
        sides = [dot_nn(context, stack_rows(w_proj_ref[i])) for i in range(dp)]
        attn_out = jnp.concatenate(sides, axis=1) + vec_ref[5:6]
        attn_ref[...] = attn_out
        mid = rows_ref[...].astype(F32) + vec_ref[1:2] * attn_out
        mid_ref[...] = mid
        h_ref[...] = layer_norm(mid, vec_ref[2:3], vec_ref[6:7]).astype(BF)
        out_ref[...] = jnp.zeros_like(out_ref)

    h = h_ref[...]
    piece = w_up_ref.shape[3]
    pre, act = {}, {}

    def rise(unit):
        at = slice(unit * piece, (unit + 1) * piece)
        pre[unit] = dot_nn(h, stack_rows(w_up_ref[:, 0, at])) + bias_ref[:, at]

    def bend(unit):
        at = slice(unit * piece, (unit + 1) * piece)
        value, slope = gelu_and_slope(pre.pop(unit))
        act[unit] = value.astype(BF)
        act_ref[:, at] = act[unit]
        slope_ref[:, at] = slope.astype(BF)

    def fall(unit):
        at = slice((unit - 1) * piece, (unit + 1) * piece)
        both = jnp.concatenate([act.pop(unit - 1), act.pop(unit)], axis=1)
        out_ref[...] += dot_nn(both, join_cols(w_down_ref[:, 0, at]))

    in_pairs(part // piece, rise, bend, fall)

    @pl.when(step == pl.num_programs(0) - 1)
    def _():
        mlp_out = out_ref[...] + vec_ref[7:8]
        out_ref[...] = mlp_out
        low_ref[...] = (live_ref[:, 0:1] * (mid_ref[...] + vec_ref[3:4] * mlp_out)).astype(BF)


def mlp(context, rows, weights, base, vectors, live, up_bias):
    slots, width = rows.shape
    dp, shards, _, lanes = weights.shape
    part = base * lanes // 2
    hidden = part * shards
    full = fixed((slots, width))
    wide = jax.ShapeDtypeStruct((slots, width), F32)
    low = jax.ShapeDtypeStruct((slots, width), BF)
    tall = jax.ShapeDtypeStruct((slots, hidden), BF)
    return call(
        mlp_kernel,
        shards,
        [
            (context, full),
            (rows, full),
            (weights, pl.BlockSpec((dp, shards, lanes, lanes), lambda i: (0, 0, base + 3, 0))),
            (vectors, fixed(vectors.shape)),
            (live, fixed(live.shape)),
            (up_bias, by_cols(1, part)),
            (weights, by_shard(weights, part)),
            (weights, by_shard(weights, part, 1)),
        ],
        [
            (wide, full),
            (wide, full),
            (low, full),
            (tall, by_cols(slots, part)),
            (tall, by_cols(slots, part)),
            (wide, full),
            (low, full),
        ],
        [],
        2 * slots * width * (width + 2 * hidden),
        "mlp",
        far=(2, 3),
    )


def mlp_back_kernel(
    cot_ref, live_ref, vec_ref, out_ref, mid_ref, attn_ref, slope_ref, w_up_ref, w_down_ref,
    d_mlp_ref, d_pre_ref, d_mid_ref, d_attn_ref, sums_ref, up_sum_ref,
    acc,
):
    part = slope_ref.shape[1]
    step = pl.program_id(0)

    @pl.when(step == 0)
    def _():
        d_res = live_ref[:, 0:1] * cot_ref[...].astype(F32)
        d_mlp = vec_ref[3:4] * d_res
        sums_ref[3:4] = jnp.sum(d_res * out_ref[...], axis=0, keepdims=True)
        sums_ref[7:8] = jnp.sum(d_mlp, axis=0, keepdims=True)
        d_mlp_ref[...] = d_mlp.astype(BF)
        acc[...] = jnp.zeros_like(acc)

    d_mlp = d_mlp_ref[...]
    piece = w_up_ref.shape[3]
    d_act, d_pre = {}, {}

    def rise(unit):
        at = slice(unit * piece, (unit + 1) * piece)
        d_act[unit] = dot_nt(d_mlp, join_cols(w_down_ref[:, 0, at]))

    def bend(unit):
        at = slice(unit * piece, (unit + 1) * piece)
        d_pre[unit] = (d_act.pop(unit) * slope_ref[:, at].astype(F32)).astype(BF)
        d_pre_ref[:, at] = d_pre[unit]
        up_sum_ref[:, at] = jnp.sum(d_pre[unit].astype(F32), axis=0, keepdims=True)

    def fall(unit):
        both = jnp.concatenate([d_pre.pop(unit - 1), d_pre.pop(unit)], axis=1)
        w_up = [stack_rows(w_up_ref[:, 0, u * piece : (u + 1) * piece]) for u in (unit - 1, unit)]
        acc[...] += dot_nt(both, jnp.concatenate(w_up, axis=1))

    in_pairs(part // piece, rise, bend, fall)

    @pl.when(step == pl.num_programs(0) - 1)
    def _():
        d_mid_ln, d_gain, d_shift = layer_norm_back(mid_ref[...], vec_ref[2:3], acc[...])
        d_mid = live_ref[:, 0:1] * cot_ref[...].astype(F32) + d_mid_ln
        d_attn = vec_ref[1:2] * d_mid
        d_mid_ref[...] = d_mid
        d_attn_ref[...] = d_attn.astype(BF)
        sums_ref[2:3] = d_gain
        sums_ref[6:7] = d_shift
        sums_ref[1:2] = jnp.sum(d_mid * attn_ref[...], axis=0, keepdims=True)
        sums_ref[5:6] = jnp.sum(d_attn, axis=0, keepdims=True)
        sums_ref[0:1] = jnp.zeros_like(d_gain)
        sums_ref[4:5] = jnp.zeros_like(d_gain)


def mlp_back(cotangent, live, vectors, mlp_out, mid_rows, attn_out, slope, weights, base):
    slots, width = cotangent.shape
    part, shards = base * weights.shape[3] // 2, weights.shape[1]
    hidden = part * shards
    full = fixed((slots, width))
    low = jax.ShapeDtypeStruct((slots, width), BF)
    return call(
        mlp_back_kernel,
        shards,
        [
            (cotangent, full),
            (live, fixed(live.shape)),
            (vectors, fixed(vectors.shape)),
            (mlp_out, full),
            (mid_rows, full),
            (attn_out, full),
            (slope, by_cols(slots, part)),
            (weights, by_shard(weights, part)),
            (weights, by_shard(weights, part, 1)),
        ],
        [
            (low, full),
            (jax.ShapeDtypeStruct((slots, hidden), BF), by_cols(slots, part)),
            (jax.ShapeDtypeStruct((slots, width), F32), full),
            (low, full),
            (jax.ShapeDtypeStruct((8, width), F32), fixed((8, width))),
            (jax.ShapeDtypeStruct((1, hidden), F32), by_cols(1, part)),
        ],
        [pltpu.VMEM((slots, width), F32)],
        4 * slots * width * hidden,
        "mlp_back",
        far=(0, 1),
    )


def summed(refs, steps, stride, left, rights, base):
    def right(step):
        return jnp.concatenate([refs[stride * step + n][...] for n in rights], axis=1)

    if base:
        late = lax.axis_index("section") == 0
        return dot_tn(refs[left][...], jnp.where(late, right(1), right(0)))
    return sum(dot_tn(refs[stride * step + left][...], right(step)) for step in range(steps))


def put(out_ref, base, i, at, value):
    if base:
        value = value + base[0][i, 0, at].astype(F32)
    out_ref[i, 0, at] = value.astype(out_ref.dtype)


def down_grad_kernel(steps, *refs):
    base, out_ref = refs[2 * steps : -1], refs[-1]
    total = summed(refs, steps, 2, 0, (1,), base)
    cols = out_ref.shape[3]
    for i in range(out_ref.shape[0]):
        put(out_ref, base, i, slice(None), total[:, i * cols : (i + 1) * cols])


def up_grad_kernel(steps, *refs):
    base, out_ref = refs[2 * steps : -1], refs[-1]
    total = summed(refs, steps, 2, 0, (1,), base)
    rows = out_ref.shape[2]
    for i in range(out_ref.shape[0]):
        put(out_ref, base, i, slice(None), total[i * rows : (i + 1) * rows])


def attn_grad_kernel(steps, *refs):
    base, out_ref = refs[7 * steps : -1], refs[-1]
    dp, _, _, lanes = out_ref.shape
    for n, left, rights in ((0, 0, (2,)), (1, 1, (3, 4))):
        total = summed(refs, steps, 7, left, rights, base)
        for k in range(len(rights)):
            for i in range(dp):
                value = total[i * lanes : (i + 1) * lanes, k * lanes : (k + 1) * lanes]
                put(out_ref, base, i, slice((n + k) * lanes, (n + k + 1) * lanes), value)
    total = summed(refs, steps, 7, 5, (6,), base)
    for i in range(dp):
        put(out_ref, base, i, slice(3 * lanes, 4 * lanes), total[:, i * lanes : (i + 1) * lanes])


def grad_call(kernel, steps, shards, ins, shape, base, flops, name):
    out = jax.ShapeDtypeStruct(shape, BF)
    if base is not None:
        ins = ins + [(base, by_shard(base))]
    return call(partial(kernel, steps), shards, ins, [(out, by_shard(out))], [], flops, name, 60)[0]


def attn_grad(steps, dp, shards, base):
    ins, flops = [], 0
    lanes = steps[0][0].shape[1] // shards
    for h_one, h_all, d_q, d_k, d_v, context, d_attn in steps:
        ins += [(h_one, fixed(h_one.shape)), (h_all, fixed(h_all.shape))]
        ins += [(d, by_cols(d.shape[0], lanes)) for d in (d_q, d_k, d_v, context)]
        ins += [(d_attn, fixed(d_attn.shape))]
        flops += 4 * (h_one.size + h_all.size) * h_one.shape[1]
    shape = (dp, shards, 4 * lanes, lanes)
    return grad_call(attn_grad_kernel, len(steps), shards, ins, shape, base, flops, "attn_grad")


def down_grad(pairs, dp, shards, base):
    ins = []
    for left, right in pairs:
        ins += [(left, by_cols(left.shape[0], left.shape[1] // shards)), (right, fixed(right.shape))]
    shape = (dp, shards, pairs[0][0].shape[1] // shards, pairs[0][1].shape[1] // dp)
    flops = sum(2 * left.size * right.shape[1] for left, right in pairs)
    return grad_call(down_grad_kernel, len(pairs), shards, ins, shape, base, flops, "down_grad")


def up_grad(pairs, dp, shards, base):
    ins = []
    for left, right in pairs:
        ins += [(left, fixed(left.shape)), (right, by_cols(right.shape[0], right.shape[1] // shards))]
    shape = (dp, shards, pairs[0][0].shape[1] // dp, pairs[0][1].shape[1] // shards)
    flops = sum(2 * left.size * right.shape[1] for left, right in pairs)
    return grad_call(up_grad_kernel, len(pairs), shards, ins, shape, base, flops, "up_grad")


def shed_order(count, place):
    return sorted(range(count), key=lambda t: (-abs(t - place), -t))


def scatter_kernel(dp, shards, kinds, *refs):
    parts, outs = refs[:kinds], refs[kinds : 2 * kinds]
    own, got, side, line = (refs[(2 + n) * kinds : (3 + n) * kinds] for n in range(4))
    load_sem, core_sem, side_sem, line_sem = refs[6 * kinds :]
    groups = dp // 2
    section, dp_idx, place = lax.axis_index("section"), lax.axis_index("dp"), lax.axis_index("tensor")
    group, odd = dp_idx // 2, dp_idx % 2
    mate = (section, group * 2 + 1 - odd, place)
    others = [(section, lax.rem(group + r, groups) * 2 + odd, place) for r in range(1, groups)]
    before, after = (section, dp_idx, place - 1), (section, dp_idx, place + 1)
    mesh_id = pl.DeviceIdType.MESH
    tables = [shed_order(shards, z) for z in range(shards)]

    def owner(step):
        return sum(jnp.where(place == z, tables[z][step], 0) for z in range(shards))

    barrier = pltpu.get_barrier_semaphore()
    for device in [mate] + others:
        pl.semaphore_signal(barrier, inc=1, device_id=device, device_id_type=mesh_id)

    @pl.when(place > 0)
    def _():
        pl.semaphore_signal(barrier, inc=1, device_id=before, device_id_type=mesh_id)

    @pl.when(place < shards - 1)
    def _():
        pl.semaphore_signal(barrier, inc=1, device_id=after, device_id_type=mesh_id)

    ends = jnp.where(place == 0, 1, 0) + jnp.where(place == shards - 1, 1, 0)
    pl.semaphore_wait(barrier, groups + 2 - ends)

    def core_copy(step, kind):
        return pltpu.make_async_remote_copy(
            src_ref=parts[kind].at[:, 1 - odd, owner(step)],
            dst_ref=got[kind].at[step],
            send_sem=core_sem.at[0, step, kind],
            recv_sem=core_sem.at[1, step, kind],
            device_id=mate,
            device_id_type=mesh_id,
        )

    def load(step, kind):
        return pltpu.make_async_copy(
            parts[kind].at[:, odd, owner(step)], own[kind].at[step], load_sem.at[step, kind]
        )

    def side_copy(step, kind, r):
        return pltpu.make_async_remote_copy(
            src_ref=own[kind].at[step, lax.rem(group + r, groups)],
            dst_ref=side[kind].at[step, r - 1],
            send_sem=side_sem.at[0, step, kind, r - 1],
            recv_sem=side_sem.at[1, step, kind, r - 1],
            device_id=others[r - 1],
            device_id_type=mesh_id,
        )

    def line_copy(step, kind, ahead):
        target = owner(step)
        slot = target + 1 if ahead else target
        return pltpu.make_async_remote_copy(
            src_ref=own[kind].at[step, group],
            dst_ref=line[kind].at[slot],
            send_sem=line_sem.at[0, slot, kind],
            recv_sem=line_sem.at[1, slot, kind],
            device_id=after if ahead else before,
            device_id_type=mesh_id,
        )

    def add(one, two):
        return (one.astype(F32) + two.astype(F32)).astype(one.dtype)

    units = [(step, kind) for step in range(shards) for kind in range(kinds)]
    for step, kind in units:
        core_copy(step, kind).start()
        load(step, kind).start()

    def meet(unit):
        step, kind = unit
        load(step, kind).wait()
        core_copy(step, kind).wait_recv()
        for r in range(1, groups):
            at = lax.rem(group + r, groups)
            own[kind][step, at] = add(own[kind][step, at], got[kind][step, at])
            side_copy(step, kind, r).start()
        own[kind][step, group] = add(own[kind][step, group], got[kind][step, group])

    def pass_on(unit):
        step, kind = unit
        mine = own[kind][step, group].astype(F32)
        for r in range(1, groups):
            side_copy(step, kind, r).wait_recv()
            mine = mine + side[kind][step, r - 1].astype(F32)
        own[kind][step, group] = mine.astype(own[kind].dtype)
        target = owner(step)

        @pl.when((target >= place) & (place > 0))
        def _():
            line_copy(step, kind, True).wait_recv()
            slot = target + 1
            own[kind][step, group] = add(own[kind][step, group], line[kind][slot])

        @pl.when((target <= place) & (place < shards - 1))
        def _():
            line_copy(step, kind, False).wait_recv()
            own[kind][step, group] = add(own[kind][step, group], line[kind][target])

        @pl.when(target > place)
        def _():
            line_copy(step, kind, True).start()

        @pl.when(target < place)
        def _():
            line_copy(step, kind, False).start()

        if step == shards - 1:
            outs[kind][...] = own[kind][step, group].astype(F32)

    lag = kinds
    for at in range(len(units) + lag):
        if at < len(units):
            meet(units[at])
        if at >= lag:
            pass_on(units[at - lag])

    for step, kind in units:
        core_copy(step, kind).wait_send()
        for r in range(1, groups):
            side_copy(step, kind, r).wait_send()
        if step < shards - 1:
            target = owner(step)

            @pl.when(target > place)
            def _():
                line_copy(step, kind, True).wait_send()

            @pl.when(target < place)
            def _():
                line_copy(step, kind, False).wait_send()


def scatter_sums(parts, dp, shards):
    kinds, groups = len(parts), dp // 2
    split = [p.reshape((groups, 2) + p.shape[1:]) for p in parts]
    blocks = [p.shape[2:] for p in parts]
    scratch = []
    for lead in ((shards, groups), (shards, groups), (shards, max(groups - 1, 1)), (shards + 1,)):
        scratch += [pltpu.VMEM(lead + b, p.dtype) for p, b in zip(parts, blocks)]
    scratch += [
        pltpu.SemaphoreType.DMA((shards, kinds)),
        pltpu.SemaphoreType.DMA((2, shards, kinds)),
        pltpu.SemaphoreType.DMA((2, shards, kinds, max(groups - 1, 1))),
        pltpu.SemaphoreType.DMA((2, shards + 1, kinds)),
    ]
    return pl.pallas_call(
        partial(scatter_kernel, dp, shards, kinds),
        in_specs=[pl.BlockSpec(memory_space=pl.ANY)] * kinds,
        out_specs=[pl.BlockSpec(memory_space=pltpu.VMEM)] * kinds,
        out_shape=[jax.ShapeDtypeStruct(b, F32) for b in blocks],
        scratch_shapes=scratch,
        compiler_params=pltpu.CompilerParams(
            vmem_limit_bytes=60 * MIB, collective_id=1, has_side_effects=True
        ),
        cost_estimate=pl.CostEstimate(
            flops=0, bytes_accessed=sum(4 * p.size * p.dtype.itemsize for p in parts), transcendentals=0
        ),
        name="scatter_sums",
    )(*split)


def local(
    block_input,
    out_cotangent,
    lengths,
    qkv_weight,
    qv_bias,
    proj_weight,
    fc1_weight,
    fc1_bias,
    fc2_weight,
    gains,
    biases,
):
    section_idx = lax.axis_index("section")
    dp_count, shard_count = lax.axis_size("dp"), lax.axis_size("tensor")
    dp_idx, shard_idx = lax.axis_index("dp"), lax.axis_index("tensor")
    micro_count, _, slots, width = block_input.shape
    hidden = fc1_weight.shape[2] * shard_count
    first_section = section_idx == 0

    span = shard_count // 2
    odd, own_u = dp_idx % 2, shard_idx % span

    swap_pairs = [
        ((2 * j + a) * shard_count + b * span + u, (2 * j + b) * shard_count + a * span + u)
        for j in range(dp_count // 2)
        for a in range(2)
        for b in range(2)
        for u in range(span)
    ]
    mate_pairs = [(d, d + 1 - 2 * (d % 2)) for d in range(dp_count)]

    def turned(steps):
        return [
            (half * span + (u + steps) % span, half * span + u) for half in range(2) for u in range(span)
        ]

    def swapped(rows):
        return lax.ppermute(rows, BOTH, swap_pairs)

    def near_group(rows):
        pieces = [rows] + [lax.ppermute(rows, "tensor", turned(r)) for r in range(1, span)]
        return jnp.concatenate(pieces, axis=0)

    def with_mate(near):
        return jnp.concatenate([near, lax.ppermute(near, "dp", mate_pairs)], axis=0)

    def reduce_near(own_rows, near_rows, mate_rows):
        got = lax.ppermute(mate_rows, "dp", mate_pairs).astype(F32)
        parts = [own_rows + got[:slots]]
        for r in range(1, span):
            piece = near_rows[(r - 1) * slots : r * slots].astype(F32) + got[r * slots : (r + 1) * slots]
            parts.append(lax.ppermute(piece.astype(BF), "tensor", turned(-r)))
        return parts

    shard_of = jnp.stack([((odd + a) % 2) * span + (own_u + r) % span for a in range(2) for r in range(span)])
    slot_ids = jnp.arange(slots, dtype=jnp.int32)
    live = slot_ids[None, :] < jnp.take(lengths, shard_of)[:, None]
    own_live = live[0].astype(F32)[:, None]
    live_cols = jnp.broadcast_to(own_live, (slots, LANES))
    mask = jnp.broadcast_to(jnp.where(live.reshape(-1, 1), 0.0, NEG).astype(BF), (live.size, LANES))

    small = jnp.concatenate(
        [gains[0].reshape(-1), biases[0].reshape(-1), qv_bias[0].reshape(-1), fc1_bias[0].reshape(-1)]
    )
    rows_dp, rows_shard = width // dp_count, width // shard_count

    def whole(part):
        return lax.all_gather(part, BOTH, axis=0, tiled=False).reshape(
            (dp_count, shard_count) + part.shape
        )

    up_rows = fc1_weight[0].reshape(rows_dp, -1, rows_dp).transpose(1, 0, 2).reshape(-1, rows_dp)
    qkv_rows = qkv_weight[0].transpose(1, 0, 2).reshape(-1, rows_dp)
    shard = jnp.concatenate(
        [up_rows, fc2_weight[0], qkv_rows, proj_weight[0], small.reshape(-1, rows_dp)], axis=0
    )
    weights = whole(jnp.pad(shard, ((0, -shard.shape[0] % 16), (0, 0))))
    base = 2 * fc2_weight.shape[1] // rows_dp
    small = weights[:, :, (base + 4) * rows_dp :].reshape(dp_count * shard_count, -1)[:, : small.size]
    own = width // (dp_count * shard_count)
    vectors = small[:, : 8 * own].reshape(-1, 8, own).transpose(1, 0, 2).reshape(8, width).astype(F32)
    shared = small[:shard_count, 8 * own :]
    cut = 2 * rows_shard
    qv_rows = shared[:, :cut].reshape(shard_count, 2, -1).transpose(1, 0, 2).reshape(2, width).astype(F32)
    up_bias = shared[:, cut:].reshape(1, hidden).astype(F32)

    def tied(*values):
        return lax.optimization_barrier(values)

    def forward_attend(rows, rows_all):
        h_one = layer_norm(rows.astype(F32), vectors[0], vectors[4]).astype(BF)
        h_all = layer_norm(rows_all.astype(F32), vectors[0], vectors[4]).astype(BF)
        return (h_one, h_all) + tuple(attend(h_one, h_all, weights, base, qv_rows, mask))

    def forward_mlp(rows, attended):
        return mlp(attended[5], rows, weights, base, vectors, live_cols, up_bias)

    def backward(cotangent, attended, risen):
        h_one, h_all, queries, key_rows, values, context, lse = attended
        attn_out, mid_rows, h_two, act, slope, mlp_out, _ = risen
        d_mlp, d_pre, d_mid, d_attn, row_sums, d_up_bias = mlp_back(
            cotangent, live_cols, vectors, mlp_out, mid_rows, attn_out, slope, weights, base
        )
        d_q, d_k, d_v, d_qv, own_part, near, mate = attend_back(
            d_attn, weights, base, queries, key_rows, values, context, lse, mask
        )
        operands = ((act, d_mlp), (h_two, d_pre), (h_one, h_all, d_q, d_k, d_v, context, d_attn))
        return (d_mid, own_part, near, mate), (row_sums, d_qv, d_up_bias), operands

    def finish(rows, d_mid, parts, sums):
        d_h_one = sum(p.astype(F32) for p in parts)
        d_rows_ln, d_gain, d_shift = layer_norm_back(rows.astype(F32), vectors[0], d_h_one)
        row_sums, d_qv, d_up_bias = sums
        none = jnp.zeros((3, width), F32)
        row_sums = row_sums + jnp.concatenate([d_gain, none, d_shift, none], axis=0)
        return (d_mid + d_rows_ln).astype(BF), (row_sums, d_qv, d_up_bias)

    tokens = [swapped(block_input[0, 0])]
    tokens_all = [with_mate(near_group(tokens[0]))]
    weights, early_rows = tied(weights, block_input)
    for m in range(1, micro_count - 1):
        tokens.append(swapped(early_rows[m, 0]))
    start_attended, start_risen = [None] * micro_count, [None] * micro_count
    attended = forward_attend(tokens[0], tokens_all[0])
    if micro_count > 2:
        tokens[1], context = tied(tokens[1], attended[5])
        attended = attended[:5] + (context,) + attended[6:]
    start_attended[0] = attended
    for m in range(1, micro_count - 1):
        tokens_all.append(near_group(tokens[m]))
    start_risen[0] = forward_mlp(tokens[0], attended)
    for m in range(1, micro_count - 1):
        tokens_all[m], low = tied(tokens_all[m], start_risen[0][6])
        start_risen[0] = tuple(start_risen[0][:6]) + (low,)
        tokens_all[m] = with_mate(tokens_all[m])
    last = micro_count - 1
    late_rows, low = tied(block_input[last, 0], start_risen[0][6])
    received = [lax.ppermute(low, "section", [(0, 1)])]
    tokens.append(swapped(late_rows))
    start_low = [low]
    for m in range(1, last):
        attended = forward_attend(tokens[m], tokens_all[m])
        if m == 1:
            received[0], context = tied(received[0], attended[5])
            attended = attended[:5] + (context,) + attended[6:]
            rows = jnp.where(first_section, tokens[last], received[0])
            near_rows = near_group(rows)
        start_risen[m] = forward_mlp(tokens[m], attended)
        low = start_risen[m][6]
        if m == 1:
            near_rows, low = tied(near_rows, low)
        start_low.append(low)
        received.append(lax.ppermute(low, "section", [(0, 1)]))

    zero_rows = jnp.zeros_like(tokens[0])
    section_out, input_grad, back_rows, sums, operands = [], [], [], [], []
    d_received, pending, kept = zero_rows, None, None
    for m in range(micro_count):
        near_rows, cotangent = tied(near_rows, out_cotangent[m, 0])
        cotangent = swapped(cotangent)
        attended = forward_attend(rows, with_mate(near_rows))
        if pending is not None:
            old_rows, d_mid, parts, part_sums = pending
            parts, context = tied(parts, attended[5])
            attended = attended[:5] + (context,) + attended[6:]
            d_low, part_sums = finish(old_rows, d_mid, parts, part_sums)
            back_rows.append(d_low)
            sums.append(part_sums)
            d_received = lax.ppermute(d_low, "section", [(1, 0)])
        if m < last:
            received[m + 1], context = tied(received[m + 1], attended[5])
            attended = attended[:5] + (context,) + attended[6:]
            next_rows = jnp.where(first_section, tokens[m], received[m + 1])
            near_rows = near_group(next_rows)
        risen = forward_mlp(rows, attended)
        near_rows, d_received, cotangent, slope = tied(near_rows, d_received, cotangent, risen[4])
        risen = risen[:4] + (slope,) + risen[5:]
        if m == 0:
            received.append(lax.ppermute(risen[6], "section", [(0, 1)]))
            kept = (rows, attended, risen)
        section_out.append(swapped(jnp.where(first_section, (start_low + [kept[2][6]])[m], risen[6])))
        cotangent = jnp.where(first_section, d_received, cotangent)
        (d_mid, own_part, near, mate), part_sums, pieces = backward(cotangent, attended, risen)
        operands.append(pieces)
        section_out[m], mate = tied(section_out[m], mate)
        if m >= 2:
            done_rows = swapped(jnp.where(first_section, back_rows[m - 1], back_rows[m - 2]))
            done_rows, mate = tied(done_rows, mate)
            input_grad.append(done_rows)
        pending = (rows, d_mid, reduce_near(own_part, near, mate), part_sums)
        rows = next_rows
    full_steps = operands[1:]
    early_attn = attn_grad([step[2] for step in full_steps], dp_count, shard_count, None)
    old_rows, d_mid, parts, part_sums = pending
    parts, early_attn = tied(parts, early_attn)
    d_low, part_sums = finish(old_rows, d_mid, parts, part_sums)
    back_rows.append(d_low)
    sums.append(part_sums)
    held, d_low = tied([step[:2] for step in full_steps], d_low)
    d_received = lax.ppermute(d_low, "section", [(1, 0)])
    early_down = down_grad([step[0] for step in held], dp_count, shard_count, None)
    early_up = up_grad([step[1] for step in held], dp_count, shard_count, None)
    d_received, early_down, early_up = tied(d_received, early_down, early_up)
    if micro_count >= 2:
        input_grad.append(swapped(jnp.where(first_section, back_rows[-1], back_rows[-2])))
    rows, attended, risen = kept
    (d_mid, own_part, near, mate), part_sums, pieces = backward(
        jnp.where(first_section, d_received, zero_rows), attended, risen
    )
    last_steps = [operands[0], pieces]
    if micro_count >= 2:
        input_grad[-1], mate = tied(input_grad[-1], mate)
    parts = reduce_near(own_part, near, mate)
    late_attn = attn_grad([step[2] for step in last_steps], dp_count, shard_count, early_attn)
    parts, late_attn = tied(parts, late_attn)
    d_low, part_sums = finish(rows, d_mid, parts, part_sums)
    sums.append(part_sums)
    d_low, held = tied(d_low, [step[:2] for step in last_steps])
    input_grad.append(swapped(jnp.where(first_section, d_low, back_rows[-1])))

    grads = [
        down_grad([step[0] for step in held], dp_count, shard_count, early_down),
        up_grad([step[1] for step in held], dp_count, shard_count, early_up),
        late_attn,
    ]
    grads, input_grad[-1] = lax.optimization_barrier((grads, input_grad[-1]))
    row_sums, d_qv, d_up_bias = (sum(step[n] for step in sums) for n in range(3))
    whole_grid = (dp_count, shard_count)
    small_sums = jnp.concatenate(
        [
            row_sums.reshape((8,) + whole_grid + (own,)).transpose(1, 2, 0, 3).reshape(whole_grid + (-1,)),
            jnp.broadcast_to(
                d_qv.reshape(2, shard_count, rows_dp).transpose(1, 0, 2).reshape(1, shard_count, -1),
                whole_grid + (2 * rows_dp,),
            ),
            jnp.broadcast_to(d_up_bias.reshape(1, shard_count, -1), whole_grid + (hidden // shard_count,)),
        ],
        axis=2,
    ).reshape(whole_grid + (-1, rows_dp))
    d_down, d_up, d_attn, small_total = scatter_sums(list(grads) + [small_sums], dp_count, shard_count)
    d_qkv = d_attn[: 3 * rows_dp].reshape(3, rows_dp, rows_dp).transpose(1, 0, 2)
    d_proj = d_attn[3 * rows_dp :]
    small_total = small_total.reshape(-1)
    gain_grad = small_total[: 4 * own].reshape(4, own)
    bias_grad = small_total[4 * own : 8 * own].reshape(4, own)
    qv_grad = small_total[8 * own : 8 * own + 2 * rows_dp].reshape(2, rows_dp)
    up_bias_grad = small_total[8 * own + 2 * rows_dp :]

    section_out, input_grad = jnp.stack(section_out), jnp.stack(input_grad)
    return (
        section_out[None, :, None],
        input_grad[None, :, None],
        d_qkv[None],
        qv_grad[None],
        d_proj[None],
        d_up[None],
        up_bias_grad[None],
        d_down[None],
        gain_grad[None],
        bias_grad[None],
    )


def solution(mesh):
    in_specs = (
        P(None, "dp", "tensor", None),
        P(None, "dp", "tensor", None),
        P(),
        P("section", "dp", None, "tensor"),
        P("section", None, "tensor"),
        P("section", "tensor", "dp"),
        P("section", "dp", "tensor"),
        P("section", "tensor"),
        P("section", "tensor", "dp"),
        P("section", None, ("dp", "tensor")),
        P("section", None, ("dp", "tensor")),
    )
    out_specs = (
        P("section", None, "dp", "tensor", None),
        P("section", None, "dp", "tensor", None),
        P("section", "dp", None, "tensor"),
        P("section", None, "tensor"),
        P("section", "tensor", "dp"),
        P("section", "dp", "tensor"),
        P("section", "tensor"),
        P("section", "tensor", "dp"),
        P("section", None, ("dp", "tensor")),
        P("section", None, ("dp", "tensor")),
    )
    return jax.shard_map(local, mesh=mesh, in_specs=in_specs, out_specs=out_specs, check_vma=False)
```

```python
from functools import partial

import jax
import jax.numpy as jnp
from jax import lax
from jax.experimental import pallas as pl
from jax.experimental.pallas import tpu as pltpu
from jax.sharding import PartitionSpec as P

HD = 64
LANES = 128
EPS = 1e-06
NEG = -1000000000.0
F32 = jnp.float32
BF = jnp.bfloat16
BOTH = ("dp", "tensor")
MIB = 2**20


def dot_nt(a, b):
    return lax.dot_general(a, b, (((1,), (1,)), ((), ())), preferred_element_type=F32)


def dot_nn(a, b):
    return lax.dot_general(a, b, (((1,), (0,)), ((), ())), preferred_element_type=F32)


def dot_tn(a, b):
    return lax.dot_general(a, b, (((0,), (0,)), ((), ())), preferred_element_type=F32)


def normalize(rows):
    mean = jnp.mean(rows, axis=-1, keepdims=True)
    centred = rows - mean
    spread = jnp.mean(centred * centred, axis=-1, keepdims=True)
    inverse = lax.rsqrt(spread + EPS)
    return centred * inverse, inverse


def layer_norm(rows, gain, shift):
    return normalize(rows)[0] * gain + shift


def layer_norm_back(rows, gain, d_out):
    normed, inverse = normalize(rows)
    scaled = gain * d_out
    mean = jnp.mean(scaled, axis=-1, keepdims=True)
    along = jnp.mean(scaled * normed, axis=-1, keepdims=True)
    d_rows = inverse * (scaled - mean - normed * along)
    d_gain = jnp.sum(d_out * normed, axis=0, keepdims=True)
    return d_rows, d_gain, jnp.sum(d_out, axis=0, keepdims=True)


def gelu_and_slope(x):
    size = jnp.abs(x)
    t = 1.0 / (1.0 + (0.3275911 * 0.7071067811865476) * size)
    bell = jnp.exp(-0.5 * x * x)
    poly = 0.5 * 1.061405429
    for factor in (-1.453152027, 1.421413741, -0.284496736, 0.254829592):
        poly = poly * t + 0.5 * factor
    tail = poly * t * bell
    below = jnp.where(x < 0.0, tail, 1.0 - tail)
    return x * below, below + x * bell * 0.3989422804014327


def lane_ids(shape):
    return lax.broadcasted_iota(jnp.int32, shape, 1)


def staged(units, *stages):
    for at in range(len(units) + len(stages) - 1):
        for late, stage in enumerate(stages):
            if 0 <= at - late < len(units):
                stage(units[at - late])


def in_pairs(count, rise, bend, fall):
    waiting = []
    rise(0)
    for unit in range(count):
        if unit + 1 < count:
            rise(unit + 1)
        bend(unit)
        if unit % 2:
            waiting.append(unit)
        if waiting and (unit % 2 == 0 or unit + 1 == count):
            for ready in waiting:
                fall(ready)
            waiting = []


def stack_rows(blocks):
    return blocks.reshape(blocks.shape[0] * blocks.shape[1], blocks.shape[2])


def join_cols(blocks):
    return jnp.concatenate([blocks[i] for i in range(blocks.shape[0])], axis=1)


def call(kernel, grid, ins, outs, scratch, flops, name, grant=32, far=()):
    arrays, in_specs = zip(*ins)
    shapes, out_specs = zip(*outs)
    shapes = [pltpu.HBM(o.shape, o.dtype) if n in far else o for n, o in enumerate(shapes)]
    moved = sum(a.size * a.dtype.itemsize for a in arrays) + sum(s.size * s.dtype.itemsize for s, _ in outs)
    return pl.pallas_call(
        kernel,
        grid=(grid,),
        in_specs=list(in_specs),
        out_specs=list(out_specs),
        out_shape=list(shapes),
        scratch_shapes=scratch,
        compiler_params=pltpu.CompilerParams(vmem_limit_bytes=grant * MIB),
        cost_estimate=pl.CostEstimate(flops=flops, bytes_accessed=moved, transcendentals=0),
        name=name,
    )(*arrays)


def fixed(shape):
    return pl.BlockSpec(shape, lambda i: (0,) * len(shape))


def by_cols(rows, cols):
    return pl.BlockSpec((rows, cols), lambda i: (0, i))


def by_shard(blocks, rows=None, at=0):
    dp, _, own_rows, cols = blocks.shape
    return pl.BlockSpec((dp, 1, rows or own_rows, cols), lambda i: (0, i, at, 0))


def attend_kernel(
    h_ref, h_all_ref, w_q_ref, w_k_ref, w_v_ref, bias_ref, mask_ref, q_ref, k_ref, v_ref, o_ref, lse_ref
):
    part = q_ref.shape[1]
    w_q, w_k, w_v = (stack_rows(w[:, 0]) for w in (w_q_ref, w_k_ref, w_v_ref))
    q_ref[...] = (dot_nn(h_ref[...], w_q) + bias_ref[0:1]).astype(BF)
    k_ref[...] = dot_nn(h_all_ref[...], w_k).astype(BF)
    v_ref[...] = (dot_nn(h_all_ref[...], w_v) + bias_ref[1:2]).astype(BF)
    mask = mask_ref[...]
    k_lane, q_lane = lane_ids((k_ref.shape[0], LANES)), lane_ids((q_ref.shape[0], LANES))
    units = [(pair, half) for pair in range(part // LANES) for half in range(2)]
    scores, probs, done = {}, {}, {}

    def cols(pair):
        return slice(pair * LANES, (pair + 1) * LANES)

    def score(unit):
        pair, half = unit
        spare = HD * (1 - half)
        low_q = (q_ref[:, cols(pair)].astype(F32) * HD**-0.5).astype(BF)
        q_one = jnp.where(q_lane == spare, 1.0, 0.0).astype(BF)
        k_bias = jnp.where(k_lane == spare, mask, 0.0).astype(BF)
        q_own = jnp.where((q_lane // HD) == half, low_q, q_one)
        k_own = jnp.where((k_lane // HD) == half, k_ref[:, cols(pair)], k_bias)
        scores[unit] = dot_nt(q_own, k_own)

    def soften(unit):
        rows = scores.pop(unit)
        top = jnp.max(rows, axis=1, keepdims=True)
        probs[unit] = (jnp.exp(rows - top).astype(BF), top)

    def mix(unit):
        pair, half = unit
        spare = HD * (1 - half)
        prob, top = probs.pop(unit)
        v_one = jnp.where(k_lane == spare, 1.0, 0.0).astype(BF)
        v_own = jnp.where((k_lane // HD) == half, v_ref[:, cols(pair)], v_one)
        out = dot_nn(prob, v_own)
        total = out[:, spare : spare + 1]
        done[unit] = (out * (1.0 / total), top + jnp.log(total))
        if half == 1:
            first, second = done.pop((pair, 0)), done.pop(unit)
            o_ref[:, cols(pair)] = jnp.where(q_lane < HD, first[0], second[0]).astype(BF)
            lse_ref[:, cols(pair)] = jnp.where(q_lane < HD, first[1], second[1])

    staged(units, score, soften, mix)


def attend(h_one, h_all, weights, base, qv_rows, mask):
    slots, width = h_one.shape
    keys = h_all.shape[0]
    part = weights.shape[3]
    own, every = by_cols(slots, part), by_cols(keys, part)
    row = jax.ShapeDtypeStruct((slots, width), BF)
    col = jax.ShapeDtypeStruct((keys, width), BF)
    return call(
        attend_kernel,
        weights.shape[1],
        [
            (h_one, fixed(h_one.shape)),
            (h_all, fixed(h_all.shape)),
            (weights, by_shard(weights, part, base)),
            (weights, by_shard(weights, part, base + 1)),
            (weights, by_shard(weights, part, base + 2)),
            (qv_rows, by_cols(2, part)),
            (mask, fixed(mask.shape)),
        ],
        [(row, own), (col, every), (col, every), (row, own), (jax.ShapeDtypeStruct(row.shape, F32), own)],
        [],
        width * (2 * width * (slots + 2 * keys) + 16 * slots * keys),
        "attend",
        far=(1, 2),
    )


def split_three(value):
    first = value.astype(BF)
    rest = value - first.astype(F32)
    second = rest.astype(BF)
    return first, second, (rest - second.astype(F32)).astype(BF)


def attend_back_kernel(
    d_attn_ref, w_proj_ref, w_q_ref, w_k_ref, w_v_ref, q_ref, k_ref, v_ref, ctx_ref, lse_ref, mask_ref,
    dq_ref, dk_ref, dv_ref, sums_ref, own_ref, near_ref, mate_ref,
    do_ref, acc_q, acc_k,
):
    slots, part = q_ref.shape
    do_ref[...] = dot_nt(d_attn_ref[...], join_cols(w_proj_ref[:, 0])).astype(BF)
    mask = mask_ref[...]
    q_lane, k_lane = lane_ids((slots, LANES)), lane_ids((k_ref.shape[0], LANES))
    units = [(pair, half) for pair in range(part // LANES) for half in range(2)]
    first_part, done = {}, {}

    def cols(pair):
        return slice(pair * LANES, (pair + 1) * LANES)

    def low_queries(pair):
        return (q_ref[:, cols(pair)].astype(F32) * HD**-0.5).astype(BF)

    def score(unit):
        pair, half = unit
        at = cols(pair)
        spare = HD * (1 - half)
        d_out, lse = do_ref[:, at], lse_ref[:, at]
        q_own, k_own = (q_lane // HD) == half, (k_lane // HD) == half
        zero_q, one_q = jnp.zeros(q_lane.shape, BF), jnp.ones(q_lane.shape, BF)
        l_one, l_two, l_three = split_three(-lse[:, HD * half : HD * half + 1])
        product = d_out.astype(F32) * ctx_ref[:, at].astype(F32)
        inner = jnp.sum(jnp.where(q_own, product, 0.0), axis=1, keepdims=True)
        i_one, i_two, _ = split_three(-inner)
        q_more = jnp.where(q_lane == spare + 2, l_two, jnp.where(q_lane == spare + 3, l_three, zero_q))
        q_more = jnp.where(q_lane == spare, one_q, jnp.where(q_lane == spare + 1, l_one, q_more))
        k_more = jnp.where((k_lane > spare) & (k_lane < spare + 4), 1.0, 0.0).astype(BF)
        k_more = jnp.where(k_lane == spare, mask, k_more)
        o_more = jnp.where(q_lane == spare, i_one, jnp.where(q_lane == spare + 1, i_two, zero_q))
        v_more = jnp.where((k_lane >= spare) & (k_lane < spare + 2), 1.0, 0.0).astype(BF)
        score = dot_nt(jnp.where(q_own, low_queries(pair), q_more), jnp.where(k_own, k_ref[:, at], k_more))
        d_prob = dot_nt(jnp.where(q_own, d_out, o_more), jnp.where(k_own, v_ref[:, at], v_more))
        prob = jnp.exp(score)
        first_part[unit] = (prob.astype(BF), (prob * d_prob).astype(BF))

    def mix(unit):
        pair, half = unit
        at = cols(pair)
        prob, d_score = first_part.pop(unit)
        done[unit] = (
            dot_nn(d_score, k_ref[:, at]) * HD**-0.5,
            dot_tn(d_score, low_queries(pair)),
            dot_tn(prob, do_ref[:, at]),
        )
        if half == 1:
            one, two = done.pop((pair, 0)), done.pop(unit)
            d_q = jnp.where(q_lane < HD, one[0], two[0]).astype(BF)
            d_k = jnp.where(k_lane < HD, one[1], two[1]).astype(BF)
            d_v = jnp.where(k_lane < HD, one[2], two[2]).astype(BF)
            dq_ref[:, at], dk_ref[:, at], dv_ref[:, at] = d_q, d_k, d_v
            sums_ref[0:1, at] = jnp.sum(d_q.astype(F32), axis=0, keepdims=True)
            sums_ref[1:2, at] = jnp.sum(d_v.astype(F32), axis=0, keepdims=True)

    staged(units, score, mix)
    w_q, w_k, w_v = (stack_rows(w[:, 0]) for w in (w_q_ref, w_k_ref, w_v_ref))
    from_q = dot_nt(dq_ref[...], w_q)
    from_k = dot_nt(
        jnp.concatenate([dk_ref[...], dv_ref[...]], axis=1), jnp.concatenate([w_k, w_v], axis=1)
    )

    @pl.when(pl.program_id(0) == 0)
    def _():
        acc_q[...] = from_q
        acc_k[...] = from_k

    @pl.when(pl.program_id(0) > 0)
    def _():
        acc_q[...] += from_q
        acc_k[...] += from_k

    @pl.when(pl.program_id(0) == pl.num_programs(0) - 1)
    def _():
        near = near_ref.shape[0]
        own_ref[...] = acc_q[...] + acc_k[0:slots]
        near_ref[...] = acc_k[slots : slots + near].astype(BF)
        mate_ref[...] = acc_k[slots + near :].astype(BF)


def attend_back(d_attn, weights, base, queries, key_rows, values, context, lse, mask):
    slots, width = queries.shape
    keys = key_rows.shape[0]
    part = weights.shape[3]
    own, every = by_cols(slots, part), by_cols(keys, part)
    row = jax.ShapeDtypeStruct((slots, width), BF)
    col = jax.ShapeDtypeStruct((keys, width), BF)
    near = jax.ShapeDtypeStruct((keys // 2 - slots, width), BF)
    mate = jax.ShapeDtypeStruct((keys // 2, width), BF)
    return call(
        attend_back_kernel,
        weights.shape[1],
        [
            (d_attn, fixed(d_attn.shape)),
            (weights, by_shard(weights, part, base + 3)),
            (weights, by_shard(weights, part, base)),
            (weights, by_shard(weights, part, base + 1)),
            (weights, by_shard(weights, part, base + 2)),
            (queries, own),
            (key_rows, every),
            (values, every),
            (context, own),
            (lse, own),
            (mask, fixed(mask.shape)),
        ],
        [
            (row, own),
            (col, every),
            (col, every),
            (jax.ShapeDtypeStruct((2, width), F32), by_cols(2, part)),
            (jax.ShapeDtypeStruct((slots, width), F32), fixed((slots, width))),
            (near, fixed(near.shape)),
            (mate, fixed(mate.shape)),
        ],
        [pltpu.VMEM((slots, part), BF), pltpu.VMEM((slots, width), F32), pltpu.VMEM((keys, width), F32)],
        width * (2 * width * (2 * slots + 2 * keys) + 40 * slots * keys),
        "attend_back",
        far=(0, 1, 2),
    )


def mlp_kernel(
    ctx_ref, rows_ref, w_proj_ref, vec_ref, live_ref, bias_ref, w_up_ref, w_down_ref,
    attn_ref, mid_ref, h_ref, act_ref, slope_ref, out_ref, low_ref,
    acc,
):
    dp, _, part, _ = w_up_ref.shape
    step = pl.program_id(0)

    @pl.when(step == 0)
    def _():
        context = ctx_ref[...]
        sides = [dot_nn(context, stack_rows(w_proj_ref[i])) for i in range(dp)]
        attn_out = jnp.concatenate(sides, axis=1) + vec_ref[5:6]
        attn_ref[...] = attn_out.astype(BF)
        mid = rows_ref[...].astype(F32) + vec_ref[1:2] * attn_out
        mid_ref[...] = mid
        h_ref[...] = layer_norm(mid, vec_ref[2:3], vec_ref[6:7]).astype(BF)
        acc[...] = jnp.zeros_like(acc)

    h = h_ref[...]
    piece = w_up_ref.shape[3]
    pre, act = {}, {}

    def rise(unit):
        at = slice(unit * piece, (unit + 1) * piece)
        pre[unit] = dot_nn(h, stack_rows(w_up_ref[:, 0, at])) + bias_ref[:, at]

    def bend(unit):
        at = slice(unit * piece, (unit + 1) * piece)
        value, slope = gelu_and_slope(pre.pop(unit))
        act[unit] = value.astype(BF)
        act_ref[:, at] = act[unit]
        slope_ref[:, at] = slope.astype(BF)

    def fall(unit):
        at = slice((unit - 1) * piece, (unit + 1) * piece)
        both = jnp.concatenate([act.pop(unit - 1), act.pop(unit)], axis=1)
        acc[...] += dot_nn(both, join_cols(w_down_ref[:, 0, at]))

    in_pairs(part // piece, rise, bend, fall)

    @pl.when(step == pl.num_programs(0) - 1)
    def _():
        mlp_out = acc[...] + vec_ref[7:8]
        out_ref[...] = mlp_out.astype(BF)
        low_ref[...] = (live_ref[:, 0:1] * (mid_ref[...] + vec_ref[3:4] * mlp_out)).astype(BF)


def mlp(context, rows, weights, base, vectors, live, up_bias):
    slots, width = rows.shape
    dp, shards, _, lanes = weights.shape
    part = base * lanes // 2
    hidden = part * shards
    full = fixed((slots, width))
    wide = jax.ShapeDtypeStruct((slots, width), F32)
    low = jax.ShapeDtypeStruct((slots, width), BF)
    tall = jax.ShapeDtypeStruct((slots, hidden), BF)
    return call(
        mlp_kernel,
        shards,
        [
            (context, full),
            (rows, full),
            (weights, pl.BlockSpec((dp, shards, lanes, lanes), lambda i: (0, 0, base + 3, 0))),
            (vectors, fixed(vectors.shape)),
            (live, fixed(live.shape)),
            (up_bias, by_cols(1, part)),
            (weights, by_shard(weights, part)),
            (weights, by_shard(weights, part, 1)),
        ],
        [
            (low, full),
            (wide, full),
            (low, full),
            (tall, by_cols(slots, part)),
            (tall, by_cols(slots, part)),
            (low, full),
            (low, full),
        ],
        [pltpu.VMEM((slots, width), F32)],
        2 * slots * width * (width + 2 * hidden),
        "mlp",
        far=(2, 3),
    )


def mlp_back_kernel(
    cot_ref, live_ref, vec_ref, out_ref, mid_ref, attn_ref, slope_ref, w_up_ref, w_down_ref,
    d_mlp_ref, d_pre_ref, d_mid_ref, d_attn_ref, sums_ref, up_sum_ref,
    acc,
):
    part = slope_ref.shape[1]
    step = pl.program_id(0)

    @pl.when(step == 0)
    def _():
        d_res = live_ref[:, 0:1] * cot_ref[...].astype(F32)
        d_mlp = vec_ref[3:4] * d_res
        sums_ref[3:4] = jnp.sum(d_res * out_ref[...].astype(F32), axis=0, keepdims=True)
        sums_ref[7:8] = jnp.sum(d_mlp, axis=0, keepdims=True)
        d_mlp_ref[...] = d_mlp.astype(BF)
        acc[...] = jnp.zeros_like(acc)

    d_mlp = d_mlp_ref[...]
    piece = w_up_ref.shape[3]
    d_act, d_pre = {}, {}

    def rise(unit):
        at = slice(unit * piece, (unit + 1) * piece)
        d_act[unit] = dot_nt(d_mlp, join_cols(w_down_ref[:, 0, at]))

    def bend(unit):
        at = slice(unit * piece, (unit + 1) * piece)
        d_pre[unit] = (d_act.pop(unit) * slope_ref[:, at].astype(F32)).astype(BF)
        d_pre_ref[:, at] = d_pre[unit]
        up_sum_ref[:, at] = jnp.sum(d_pre[unit].astype(F32), axis=0, keepdims=True)

    def fall(unit):
        both = jnp.concatenate([d_pre.pop(unit - 1), d_pre.pop(unit)], axis=1)
        w_up = [stack_rows(w_up_ref[:, 0, u * piece : (u + 1) * piece]) for u in (unit - 1, unit)]
        acc[...] += dot_nt(both, jnp.concatenate(w_up, axis=1))

    in_pairs(part // piece, rise, bend, fall)

    @pl.when(step == pl.num_programs(0) - 1)
    def _():
        d_mid_ln, d_gain, d_shift = layer_norm_back(mid_ref[...], vec_ref[2:3], acc[...])
        d_mid = live_ref[:, 0:1] * cot_ref[...].astype(F32) + d_mid_ln
        d_attn = vec_ref[1:2] * d_mid
        d_mid_ref[...] = d_mid
        d_attn_ref[...] = d_attn.astype(BF)
        sums_ref[2:3] = d_gain
        sums_ref[6:7] = d_shift
        sums_ref[1:2] = jnp.sum(d_mid * attn_ref[...].astype(F32), axis=0, keepdims=True)
        sums_ref[5:6] = jnp.sum(d_attn, axis=0, keepdims=True)
        sums_ref[0:1] = jnp.zeros_like(d_gain)
        sums_ref[4:5] = jnp.zeros_like(d_gain)


def mlp_back(cotangent, live, vectors, mlp_out, mid_rows, attn_out, slope, weights, base):
    slots, width = cotangent.shape
    part, shards = base * weights.shape[3] // 2, weights.shape[1]
    hidden = part * shards
    full = fixed((slots, width))
    low = jax.ShapeDtypeStruct((slots, width), BF)
    return call(
        mlp_back_kernel,
        shards,
        [
            (cotangent, full),
            (live, fixed(live.shape)),
            (vectors, fixed(vectors.shape)),
            (mlp_out, full),
            (mid_rows, full),
            (attn_out, full),
            (slope, by_cols(slots, part)),
            (weights, by_shard(weights, part)),
            (weights, by_shard(weights, part, 1)),
        ],
        [
            (low, full),
            (jax.ShapeDtypeStruct((slots, hidden), BF), by_cols(slots, part)),
            (jax.ShapeDtypeStruct((slots, width), F32), full),
            (low, full),
            (jax.ShapeDtypeStruct((8, width), F32), fixed((8, width))),
            (jax.ShapeDtypeStruct((1, hidden), F32), by_cols(1, part)),
        ],
        [pltpu.VMEM((slots, width), F32)],
        4 * slots * width * hidden,
        "mlp_back",
        far=(0, 1),
    )


def summed(refs, steps, stride, left, rights, base):
    def right(step):
        return jnp.concatenate([refs[stride * step + n][...] for n in rights], axis=1)

    if base:
        late = lax.axis_index("section") == 0
        return dot_tn(refs[left][...], jnp.where(late, right(1), right(0)))
    return sum(dot_tn(refs[stride * step + left][...], right(step)) for step in range(steps))


def put(out_ref, base, i, at, value):
    if base:
        value = value + base[0][i, 0, at].astype(F32)
    out_ref[i, 0, at] = value.astype(out_ref.dtype)


def down_grad_kernel(steps, *refs):
    base, out_ref = refs[2 * steps : -1], refs[-1]
    total = summed(refs, steps, 2, 0, (1,), base)
    cols = out_ref.shape[3]
    for i in range(out_ref.shape[0]):
        put(out_ref, base, i, slice(None), total[:, i * cols : (i + 1) * cols])


def up_grad_kernel(steps, *refs):
    base, out_ref = refs[2 * steps : -1], refs[-1]
    total = summed(refs, steps, 2, 0, (1,), base)
    rows = out_ref.shape[2]
    for i in range(out_ref.shape[0]):
        put(out_ref, base, i, slice(None), total[i * rows : (i + 1) * rows])


def attn_grad_kernel(steps, *refs):
    base, out_ref = refs[7 * steps : -1], refs[-1]
    dp, _, _, lanes = out_ref.shape
    for n, left, rights in ((0, 0, (2,)), (1, 1, (3, 4))):
        total = summed(refs, steps, 7, left, rights, base)
        for k in range(len(rights)):
            for i in range(dp):
                value = total[i * lanes : (i + 1) * lanes, k * lanes : (k + 1) * lanes]
                put(out_ref, base, i, slice((n + k) * lanes, (n + k + 1) * lanes), value)
    total = summed(refs, steps, 7, 5, (6,), base)
    for i in range(dp):
        put(out_ref, base, i, slice(3 * lanes, 4 * lanes), total[:, i * lanes : (i + 1) * lanes])


def grad_call(kernel, steps, shards, ins, shape, base, flops, name):
    out = jax.ShapeDtypeStruct(shape, BF)
    if base is not None:
        ins = ins + [(base, by_shard(base))]
    return call(partial(kernel, steps), shards, ins, [(out, by_shard(out))], [], flops, name, 60)[0]


def attn_grad(steps, dp, shards, base):
    ins, flops = [], 0
    lanes = steps[0][0].shape[1] // shards
    for h_one, h_all, d_q, d_k, d_v, context, d_attn in steps:
        ins += [(h_one, fixed(h_one.shape)), (h_all, fixed(h_all.shape))]
        ins += [(d, by_cols(d.shape[0], lanes)) for d in (d_q, d_k, d_v, context)]
        ins += [(d_attn, fixed(d_attn.shape))]
        flops += 4 * (h_one.size + h_all.size) * h_one.shape[1]
    shape = (dp, shards, 4 * lanes, lanes)
    return grad_call(attn_grad_kernel, len(steps), shards, ins, shape, base, flops, "attn_grad")


def down_grad(pairs, dp, shards, base):
    ins = []
    for left, right in pairs:
        ins += [(left, by_cols(left.shape[0], left.shape[1] // shards)), (right, fixed(right.shape))]
    shape = (dp, shards, pairs[0][0].shape[1] // shards, pairs[0][1].shape[1] // dp)
    flops = sum(2 * left.size * right.shape[1] for left, right in pairs)
    return grad_call(down_grad_kernel, len(pairs), shards, ins, shape, base, flops, "down_grad")


def up_grad(pairs, dp, shards, base):
    ins = []
    for left, right in pairs:
        ins += [(left, fixed(left.shape)), (right, by_cols(right.shape[0], right.shape[1] // shards))]
    shape = (dp, shards, pairs[0][0].shape[1] // dp, pairs[0][1].shape[1] // shards)
    flops = sum(2 * left.size * right.shape[1] for left, right in pairs)
    return grad_call(up_grad_kernel, len(pairs), shards, ins, shape, base, flops, "up_grad")


def shed_order(count, place):
    return sorted(range(count), key=lambda t: (-abs(t - place), -t))


def scatter_kernel(dp, shards, kinds, *refs):
    parts, outs = refs[:kinds], refs[kinds : 2 * kinds]
    own, got, side, line = (refs[(2 + n) * kinds : (3 + n) * kinds] for n in range(4))
    load_sem, core_sem, side_sem, line_sem = refs[6 * kinds :]
    groups = dp // 2
    section, dp_idx, place = lax.axis_index("section"), lax.axis_index("dp"), lax.axis_index("tensor")
    group, odd = dp_idx // 2, dp_idx % 2
    mate = (section, group * 2 + 1 - odd, place)
    others = [(section, lax.rem(group + r, groups) * 2 + odd, place) for r in range(1, groups)]
    before, after = (section, dp_idx, place - 1), (section, dp_idx, place + 1)
    mesh_id = pl.DeviceIdType.MESH
    tables = [shed_order(shards, z) for z in range(shards)]

    def owner(step):
        return sum(jnp.where(place == z, tables[z][step], 0) for z in range(shards))

    barrier = pltpu.get_barrier_semaphore()
    for device in [mate] + others:
        pl.semaphore_signal(barrier, inc=1, device_id=device, device_id_type=mesh_id)

    @pl.when(place > 0)
    def _():
        pl.semaphore_signal(barrier, inc=1, device_id=before, device_id_type=mesh_id)

    @pl.when(place < shards - 1)
    def _():
        pl.semaphore_signal(barrier, inc=1, device_id=after, device_id_type=mesh_id)

    ends = jnp.where(place == 0, 1, 0) + jnp.where(place == shards - 1, 1, 0)
    pl.semaphore_wait(barrier, groups + 2 - ends)

    def core_copy(step, kind):
        return pltpu.make_async_remote_copy(
            src_ref=parts[kind].at[:, 1 - odd, owner(step)],
            dst_ref=got[kind].at[step],
            send_sem=core_sem.at[0, step, kind],
            recv_sem=core_sem.at[1, step, kind],
            device_id=mate,
            device_id_type=mesh_id,
        )

    def load(step, kind):
        return pltpu.make_async_copy(
            parts[kind].at[:, odd, owner(step)], own[kind].at[step], load_sem.at[step, kind]
        )

    def side_copy(step, kind, r):
        return pltpu.make_async_remote_copy(
            src_ref=own[kind].at[step, lax.rem(group + r, groups)],
            dst_ref=side[kind].at[step, r - 1],
            send_sem=side_sem.at[0, step, kind, r - 1],
            recv_sem=side_sem.at[1, step, kind, r - 1],
            device_id=others[r - 1],
            device_id_type=mesh_id,
        )

    def line_copy(step, kind, ahead):
        target = owner(step)
        slot = target + 1 if ahead else target
        return pltpu.make_async_remote_copy(
            src_ref=own[kind].at[step, group],
            dst_ref=line[kind].at[slot],
            send_sem=line_sem.at[0, slot, kind],
            recv_sem=line_sem.at[1, slot, kind],
            device_id=after if ahead else before,
            device_id_type=mesh_id,
        )

    def add(one, two):
        return (one.astype(F32) + two.astype(F32)).astype(one.dtype)

    units = [(step, kind) for step in range(shards) for kind in range(kinds)]
    for step, kind in units:
        core_copy(step, kind).start()
        load(step, kind).start()

    def meet(unit):
        step, kind = unit
        load(step, kind).wait()
        core_copy(step, kind).wait_recv()
        for r in range(1, groups):
            at = lax.rem(group + r, groups)
            own[kind][step, at] = add(own[kind][step, at], got[kind][step, at])
            side_copy(step, kind, r).start()
        own[kind][step, group] = add(own[kind][step, group], got[kind][step, group])

    def pass_on(unit):
        step, kind = unit
        mine = own[kind][step, group].astype(F32)
        for r in range(1, groups):
            side_copy(step, kind, r).wait_recv()
            mine = mine + side[kind][step, r - 1].astype(F32)
        own[kind][step, group] = mine.astype(own[kind].dtype)
        target = owner(step)

        @pl.when((target >= place) & (place > 0))
        def _():
            line_copy(step, kind, True).wait_recv()
            slot = target + 1
            own[kind][step, group] = add(own[kind][step, group], line[kind][slot])

        @pl.when((target <= place) & (place < shards - 1))
        def _():
            line_copy(step, kind, False).wait_recv()
            own[kind][step, group] = add(own[kind][step, group], line[kind][target])

        @pl.when(target > place)
        def _():
            line_copy(step, kind, True).start()

        @pl.when(target < place)
        def _():
            line_copy(step, kind, False).start()

        if step == shards - 1:
            outs[kind][...] = own[kind][step, group].astype(F32)

    lag = kinds
    for at in range(len(units) + lag):
        if at < len(units):
            meet(units[at])
        if at >= lag:
            pass_on(units[at - lag])

    for step, kind in units:
        core_copy(step, kind).wait_send()
        for r in range(1, groups):
            side_copy(step, kind, r).wait_send()
        if step < shards - 1:
            target = owner(step)

            @pl.when(target > place)
            def _():
                line_copy(step, kind, True).wait_send()

            @pl.when(target < place)
            def _():
                line_copy(step, kind, False).wait_send()


def scatter_sums(parts, dp, shards):
    kinds, groups = len(parts), dp // 2
    split = [p.reshape((groups, 2) + p.shape[1:]) for p in parts]
    blocks = [p.shape[2:] for p in parts]
    scratch = []
    for lead in ((shards, groups), (shards, groups), (shards, max(groups - 1, 1)), (shards + 1,)):
        scratch += [pltpu.VMEM(lead + b, p.dtype) for p, b in zip(parts, blocks)]
    scratch += [
        pltpu.SemaphoreType.DMA((shards, kinds)),
        pltpu.SemaphoreType.DMA((2, shards, kinds)),
        pltpu.SemaphoreType.DMA((2, shards, kinds, max(groups - 1, 1))),
        pltpu.SemaphoreType.DMA((2, shards + 1, kinds)),
    ]
    return pl.pallas_call(
        partial(scatter_kernel, dp, shards, kinds),
        in_specs=[pl.BlockSpec(memory_space=pl.ANY)] * kinds,
        out_specs=[pl.BlockSpec(memory_space=pltpu.VMEM)] * kinds,
        out_shape=[jax.ShapeDtypeStruct(b, F32) for b in blocks],
        scratch_shapes=scratch,
        compiler_params=pltpu.CompilerParams(
            vmem_limit_bytes=60 * MIB, collective_id=1, has_side_effects=True
        ),
        cost_estimate=pl.CostEstimate(
            flops=0, bytes_accessed=sum(4 * p.size * p.dtype.itemsize for p in parts), transcendentals=0
        ),
        name="scatter_sums",
    )(*split)


def local(
    block_input,
    out_cotangent,
    lengths,
    qkv_weight,
    qv_bias,
    proj_weight,
    fc1_weight,
    fc1_bias,
    fc2_weight,
    gains,
    biases,
):
    section_idx = lax.axis_index("section")
    dp_count, shard_count = lax.axis_size("dp"), lax.axis_size("tensor")
    dp_idx, shard_idx = lax.axis_index("dp"), lax.axis_index("tensor")
    micro_count, _, slots, width = block_input.shape
    hidden = fc1_weight.shape[2] * shard_count
    first_section = section_idx == 0

    span = shard_count // 2
    odd, own_u = dp_idx % 2, shard_idx % span

    swap_pairs = [
        ((2 * j + a) * shard_count + b * span + u, (2 * j + b) * shard_count + a * span + u)
        for j in range(dp_count // 2)
        for a in range(2)
        for b in range(2)
        for u in range(span)
    ]
    mate_pairs = [(d, d + 1 - 2 * (d % 2)) for d in range(dp_count)]

    def turned(steps):
        return [
            (half * span + (u + steps) % span, half * span + u) for half in range(2) for u in range(span)
        ]

    def swapped(rows):
        return lax.ppermute(rows, BOTH, swap_pairs)

    def near_group(rows):
        pieces = [rows] + [lax.ppermute(rows, "tensor", turned(r)) for r in range(1, span)]
        return jnp.concatenate(pieces, axis=0)

    def with_mate(near):
        return jnp.concatenate([near, lax.ppermute(near, "dp", mate_pairs)], axis=0)

    def reduce_near(own_rows, near_rows, mate_rows):
        got = lax.ppermute(mate_rows, "dp", mate_pairs).astype(F32)
        parts = [own_rows + got[:slots]]
        for r in range(1, span):
            piece = near_rows[(r - 1) * slots : r * slots].astype(F32) + got[r * slots : (r + 1) * slots]
            parts.append(lax.ppermute(piece.astype(BF), "tensor", turned(-r)))
        return parts

    shard_of = jnp.stack([((odd + a) % 2) * span + (own_u + r) % span for a in range(2) for r in range(span)])
    slot_ids = jnp.arange(slots, dtype=jnp.int32)
    live = slot_ids[None, :] < jnp.take(lengths, shard_of)[:, None]
    own_live = live[0].astype(F32)[:, None]
    live_cols = jnp.broadcast_to(own_live, (slots, LANES))
    mask = jnp.broadcast_to(jnp.where(live.reshape(-1, 1), 0.0, NEG).astype(BF), (live.size, LANES))

    small = jnp.concatenate(
        [gains[0].reshape(-1), biases[0].reshape(-1), qv_bias[0].reshape(-1), fc1_bias[0].reshape(-1)]
    )
    rows_dp, rows_shard = width // dp_count, width // shard_count

    def whole(part):
        return lax.all_gather(part, BOTH, axis=0, tiled=False).reshape(
            (dp_count, shard_count) + part.shape
        )

    up_rows = fc1_weight[0].reshape(rows_dp, -1, rows_dp).transpose(1, 0, 2).reshape(-1, rows_dp)
    qkv_rows = qkv_weight[0].transpose(1, 0, 2).reshape(-1, rows_dp)
    shard = jnp.concatenate(
        [up_rows, fc2_weight[0], qkv_rows, proj_weight[0], small.reshape(-1, rows_dp)], axis=0
    )
    weights = whole(jnp.pad(shard, ((0, -shard.shape[0] % 16), (0, 0))))
    base = 2 * fc2_weight.shape[1] // rows_dp
    small = weights[:, :, (base + 4) * rows_dp :].reshape(dp_count * shard_count, -1)[:, : small.size]
    own = width // (dp_count * shard_count)
    vectors = small[:, : 8 * own].reshape(-1, 8, own).transpose(1, 0, 2).reshape(8, width).astype(F32)
    shared = small[:shard_count, 8 * own :]
    cut = 2 * rows_shard
    qv_rows = shared[:, :cut].reshape(shard_count, 2, -1).transpose(1, 0, 2).reshape(2, width).astype(F32)
    up_bias = shared[:, cut:].reshape(1, hidden).astype(F32)

    def tied(*values):
        return lax.optimization_barrier(values)

    def forward_attend(rows, rows_all):
        h_one = layer_norm(rows.astype(F32), vectors[0], vectors[4]).astype(BF)
        h_all = layer_norm(rows_all.astype(F32), vectors[0], vectors[4]).astype(BF)
        return (h_one, h_all) + tuple(attend(h_one, h_all, weights, base, qv_rows, mask))

    def forward_mlp(rows, attended):
        return mlp(attended[5], rows, weights, base, vectors, live_cols, up_bias)

    def backward(cotangent, attended, risen):
        h_one, h_all, queries, key_rows, values, context, lse = attended
        attn_out, mid_rows, h_two, act, slope, mlp_out, _ = risen
        d_mlp, d_pre, d_mid, d_attn, row_sums, d_up_bias = mlp_back(
            cotangent, live_cols, vectors, mlp_out, mid_rows, attn_out, slope, weights, base
        )
        d_q, d_k, d_v, d_qv, own_part, near, mate = attend_back(
            d_attn, weights, base, queries, key_rows, values, context, lse, mask
        )
        operands = ((act, d_mlp), (h_two, d_pre), (h_one, h_all, d_q, d_k, d_v, context, d_attn))
        return (d_mid, own_part, near, mate), (row_sums, d_qv, d_up_bias), operands

    def finish(rows, d_mid, parts, sums):
        d_h_one = sum(p.astype(F32) for p in parts)
        d_rows_ln, d_gain, d_shift = layer_norm_back(rows.astype(F32), vectors[0], d_h_one)
        row_sums, d_qv, d_up_bias = sums
        none = jnp.zeros((3, width), F32)
        row_sums = row_sums + jnp.concatenate([d_gain, none, d_shift, none], axis=0)
        return (d_mid + d_rows_ln).astype(BF), (row_sums, d_qv, d_up_bias)

    tokens = [swapped(block_input[0, 0])]
    tokens_all = [with_mate(near_group(tokens[0]))]
    weights, early_rows = tied(weights, block_input)
    for m in range(1, micro_count - 1):
        tokens.append(swapped(early_rows[m, 0]))
    start_attended, start_risen = [None] * micro_count, [None] * micro_count
    attended = forward_attend(tokens[0], tokens_all[0])
    if micro_count > 2:
        tokens[1], context = tied(tokens[1], attended[5])
        attended = attended[:5] + (context,) + attended[6:]
    start_attended[0] = attended
    for m in range(1, micro_count - 1):
        tokens_all.append(near_group(tokens[m]))
    start_risen[0] = forward_mlp(tokens[0], attended)
    for m in range(1, micro_count - 1):
        tokens_all[m], low = tied(tokens_all[m], start_risen[0][6])
        start_risen[0] = tuple(start_risen[0][:6]) + (low,)
        tokens_all[m] = with_mate(tokens_all[m])
    last = micro_count - 1
    late_rows, low = tied(block_input[last, 0], start_risen[0][6])
    received = [lax.ppermute(low, "section", [(0, 1)])]
    tokens.append(swapped(late_rows))
    start_low = [low]
    for m in range(1, last):
        attended = forward_attend(tokens[m], tokens_all[m])
        if m == 1:
            received[0], context = tied(received[0], attended[5])
            attended = attended[:5] + (context,) + attended[6:]
            rows = jnp.where(first_section, tokens[last], received[0])
            near_rows = near_group(rows)
        start_risen[m] = forward_mlp(tokens[m], attended)
        low = start_risen[m][6]
        if m == 1:
            near_rows, low = tied(near_rows, low)
        start_low.append(low)
        received.append(lax.ppermute(low, "section", [(0, 1)]))

    zero_rows = jnp.zeros_like(tokens[0])
    section_out, input_grad, back_rows, sums, operands = [], [], [], [], []
    d_received, pending, kept = zero_rows, None, None
    for m in range(micro_count):
        near_rows, cotangent = tied(near_rows, out_cotangent[m, 0])
        cotangent = swapped(cotangent)
        attended = forward_attend(rows, with_mate(near_rows))
        if pending is not None:
            old_rows, d_mid, parts, part_sums = pending
            parts, context = tied(parts, attended[5])
            attended = attended[:5] + (context,) + attended[6:]
            d_low, part_sums = finish(old_rows, d_mid, parts, part_sums)
            back_rows.append(d_low)
            sums.append(part_sums)
            d_received = lax.ppermute(d_low, "section", [(1, 0)])
        if m < last:
            received[m + 1], context = tied(received[m + 1], attended[5])
            attended = attended[:5] + (context,) + attended[6:]
            next_rows = jnp.where(first_section, tokens[m], received[m + 1])
            near_rows = near_group(next_rows)
        risen = forward_mlp(rows, attended)
        near_rows, d_received, cotangent, slope = tied(near_rows, d_received, cotangent, risen[4])
        risen = risen[:4] + (slope,) + risen[5:]
        if m == 0:
            received.append(lax.ppermute(risen[6], "section", [(0, 1)]))
            kept = (rows, attended, risen)
        section_out.append(swapped(jnp.where(first_section, (start_low + [kept[2][6]])[m], risen[6])))
        cotangent = jnp.where(first_section, d_received, cotangent)
        (d_mid, own_part, near, mate), part_sums, pieces = backward(cotangent, attended, risen)
        operands.append(pieces)
        section_out[m], mate = tied(section_out[m], mate)
        if m >= 2:
            done_rows = swapped(jnp.where(first_section, back_rows[m - 1], back_rows[m - 2]))
            done_rows, mate = tied(done_rows, mate)
            input_grad.append(done_rows)
        pending = (rows, d_mid, reduce_near(own_part, near, mate), part_sums)
        rows = next_rows
    full_steps = operands[1:]
    early_attn = attn_grad([step[2] for step in full_steps], dp_count, shard_count, None)
    old_rows, d_mid, parts, part_sums = pending
    parts, early_attn = tied(parts, early_attn)
    d_low, part_sums = finish(old_rows, d_mid, parts, part_sums)
    back_rows.append(d_low)
    sums.append(part_sums)
    held, d_low = tied([step[:2] for step in full_steps], d_low)
    d_received = lax.ppermute(d_low, "section", [(1, 0)])
    early_down = down_grad([step[0] for step in held], dp_count, shard_count, None)
    early_up = up_grad([step[1] for step in held], dp_count, shard_count, None)
    d_received, early_down, early_up = tied(d_received, early_down, early_up)
    if micro_count >= 2:
        input_grad.append(swapped(jnp.where(first_section, back_rows[-1], back_rows[-2])))
    rows, attended, risen = kept
    (d_mid, own_part, near, mate), part_sums, pieces = backward(
        jnp.where(first_section, d_received, zero_rows), attended, risen
    )
    last_steps = [operands[0], pieces]
    if micro_count >= 2:
        input_grad[-1], mate = tied(input_grad[-1], mate)
    parts = reduce_near(own_part, near, mate)
    late_attn = attn_grad([step[2] for step in last_steps], dp_count, shard_count, early_attn)
    parts, late_attn = tied(parts, late_attn)
    d_low, part_sums = finish(rows, d_mid, parts, part_sums)
    sums.append(part_sums)
    d_low, held = tied(d_low, [step[:2] for step in last_steps])
    input_grad.append(swapped(jnp.where(first_section, d_low, back_rows[-1])))

    grads = [
        down_grad([step[0] for step in held], dp_count, shard_count, early_down),
        up_grad([step[1] for step in held], dp_count, shard_count, early_up),
        late_attn,
    ]
    grads, input_grad[-1] = lax.optimization_barrier((grads, input_grad[-1]))
    row_sums, d_qv, d_up_bias = (sum(step[n] for step in sums) for n in range(3))
    whole_grid = (dp_count, shard_count)
    small_sums = jnp.concatenate(
        [
            row_sums.reshape((8,) + whole_grid + (own,)).transpose(1, 2, 0, 3).reshape(whole_grid + (-1,)),
            jnp.broadcast_to(
                d_qv.reshape(2, shard_count, rows_dp).transpose(1, 0, 2).reshape(1, shard_count, -1),
                whole_grid + (2 * rows_dp,),
            ),
            jnp.broadcast_to(d_up_bias.reshape(1, shard_count, -1), whole_grid + (hidden // shard_count,)),
        ],
        axis=2,
    ).reshape(whole_grid + (-1, rows_dp))
    d_down, d_up, d_attn, small_total = scatter_sums(list(grads) + [small_sums], dp_count, shard_count)
    d_qkv = d_attn[: 3 * rows_dp].reshape(3, rows_dp, rows_dp).transpose(1, 0, 2)
    d_proj = d_attn[3 * rows_dp :]
    small_total = small_total.reshape(-1)
    gain_grad = small_total[: 4 * own].reshape(4, own)
    bias_grad = small_total[4 * own : 8 * own].reshape(4, own)
    qv_grad = small_total[8 * own : 8 * own + 2 * rows_dp].reshape(2, rows_dp)
    up_bias_grad = small_total[8 * own + 2 * rows_dp :]

    section_out, input_grad = jnp.stack(section_out), jnp.stack(input_grad)
    return (
        section_out[None, :, None],
        input_grad[None, :, None],
        d_qkv[None],
        qv_grad[None],
        d_proj[None],
        d_up[None],
        up_bias_grad[None],
        d_down[None],
        gain_grad[None],
        bias_grad[None],
    )


def solution(mesh):
    in_specs = (
        P(None, "dp", "tensor", None),
        P(None, "dp", "tensor", None),
        P(),
        P("section", "dp", None, "tensor"),
        P("section", None, "tensor"),
        P("section", "tensor", "dp"),
        P("section", "dp", "tensor"),
        P("section", "tensor"),
        P("section", "tensor", "dp"),
        P("section", None, ("dp", "tensor")),
        P("section", None, ("dp", "tensor")),
    )
    out_specs = (
        P("section", None, "dp", "tensor", None),
        P("section", None, "dp", "tensor", None),
        P("section", "dp", None, "tensor"),
        P("section", None, "tensor"),
        P("section", "tensor", "dp"),
        P("section", "dp", "tensor"),
        P("section", "tensor"),
        P("section", "tensor", "dp"),
        P("section", None, ("dp", "tensor")),
        P("section", None, ("dp", "tensor")),
    )
    return jax.shard_map(local, mesh=mesh, in_specs=in_specs, out_specs=out_specs, check_vma=False)
```
